32 devices in a mesh: dp: 8 (over y, x, core), seq: 4 (over z).
Axes of the slice: x: 2, y: 2, z: 4, core: 2. Of those that a mesh axis runs over, the one named last changes fastest.
Arguments:
- tokens: bfloat16 [2, 8, 1024, 1600], P(None, 'dp', 'seq'), may hold values from -6 to 6
- doc_ids: int32 [2, 8, 1024], P(None, 'dp', 'seq'), may hold values from 0 to 15, never falling along the last dimension, each value on 1 to 256 neighbouring positions
- cotangent: bfloat16 [2, 8, 1024, 1600], P(None, 'dp', 'seq'), may hold values from -6 to 6
- enc_in: bfloat16 [1280000], P(('dp', 'seq')), may hold values from -0.15625 to 0.15625
- enc_conv: bfloat16 [3200000], P(('dp', 'seq')), may hold values from -0.09375 to 0.09375
- enc_out: bfloat16 [1280000], P(('dp', 'seq')), may hold values from -0.21875 to 0.21875
- enc_gain: float32 [3200], replicated, may hold values from 0.25 to 1.75
- enc_shift: float32 [3200], replicated, may hold values from -3 to 3
- enc_bias: float32 [1600], replicated, may hold values from -3 to 3
- dec_in: bfloat16 [1280000], P(('dp', 'seq')), may hold values from -0.15625 to 0.15625
- dec_conv: bfloat16 [1920000], P(('dp', 'seq')), may hold values from -0.125 to 0.125
- dec_out: bfloat16 [1280000], P(('dp', 'seq')), may hold values from -0.21875 to 0.21875
- dec_gain: float32 [3200], replicated, may hold values from 0.25 to 1.75
- dec_shift: float32 [3200], replicated, may hold values from -3 to 3
- dec_bias: float32 [1600], replicated, may hold values from -3 to 3
Outputs:
- output: bfloat16 [2, 8, 1024, 1600], P(None, 'dp', 'seq')
- token_grad: float32 [2, 8, 1024, 1600], P(None, 'dp', 'seq')
- enc_in_grad: float32 [1280000], P(('dp', 'seq'))
- enc_conv_grad: float32 [3200000], P(('dp', 'seq'))
- enc_out_grad: float32 [1280000], P(('dp', 'seq'))
- enc_gain_grad: float32 [3200], replicated
- enc_shift_grad: float32 [3200], replicated
- enc_bias_grad: float32 [1600], replicated
- dec_in_grad: float32 [1280000], P(('dp', 'seq'))
- dec_conv_grad: float32 [1920000], P(('dp', 'seq'))
- dec_out_grad: float32 [1280000], P(('dp', 'seq'))
- dec_gain_grad: float32 [3200], replicated
- dec_shift_grad: float32 [3200], replicated
- dec_bias_grad: float32 [1600], replicated
The draws below stay inside these ranges and needn't reach their ends.
Inputs may be any that keep to these rules, and one draw needn't show every extreme that they name: `doc_ids`: along each sequence the document numbers never fall; each document has 1 to 256 characters.
All inputs are finite; a program needn't handle non-finite values.
Results may differ from the reference program's by a relative error of at most 0.012.
Values may be sent and summed in bfloat16 or wider, within the bound.
A program may use at most 192 MiB of HBM per device.

```python
import math
import jax
import jax.numpy as jnp
import numpy as np
from jax import lax

D2 = 1600
D = 800
ENCODER_TAPS = 5
ENCODER_SPACING = 4
DECODER_TAPS = 3
DECODER_SPACING = 8
LEN = 1024
MICRO = 2
DOCS = 16
MOST_DOC = 256
SEQS = 8


def block_levels(rng, shape, shards, smallest, top_value):
    def one(position, shards_of):
        heights = jax.random.uniform(jax.random.fold_in(jax.random.fold_in(rng, 6), position), (shards_of,), jnp.float32, smallest / len(shards), top_value / len(shards))
        return jnp.repeat(jnp.exp(heights), shape[position] // shards_of).reshape((-1,) + (1,) * (len(shape) - position - 1))

    loudness = one(*shards[0])
    for cut in shards[1:]:
        loudness = loudness * one(*cut)
    return loudness


def profile(number_of, total, limit, slope):
    portions = [(1 << 20) // math.isqrt(rank ** slope) + 1 for rank in range(2, number_of + 1)]
    spare, counts = total - limit - (number_of - 1), [1] * (number_of - 1)
    while spare > 0:
        free = [i for i in range(number_of - 1) if counts[i] < limit]
        pool, budget = sum([portions[i] for i in free]), spare
        for i in free:
            extra = min(limit - counts[i], max(1, budget * portions[i] // pool), spare)
            counts[i] = counts[i] + extra
            spare = spare - extra
    return np.array([limit] + counts)


def ragged(stream_key, number_of, total, limit, lean):
    if number_of == 2:
        one = jax.random.randint(stream_key, (), max(1, total - limit), min(limit, total - 1) + 1)
        return jnp.stack([one, total - one])
    tallies = jnp.asarray(profile(number_of, total, limit, lean), jnp.int32)
    pairs = (number_of - 1) // 2
    source_of, sink = tallies[1:1 + 2 * pairs:2], tallies[2:2 + 2 * pairs:2]
    margin = jnp.minimum(source_of - 1, limit - sink)
    moved = jax.random.randint(jax.random.fold_in(stream_key, 1), (pairs,), 0, 1 << 20) % (margin + 1)
    tallies = tallies.at[1:1 + 2 * pairs:2].set(source_of - moved).at[2:2 + 2 * pairs:2].set(sink + moved)
    return tallies[jax.random.permutation(jax.random.fold_in(stream_key, 2), number_of)]


def scatter_about(stream_key, shape, deviation, most, shards=(), held_as=jnp.bfloat16):
    entries = jax.random.normal(stream_key, shape, jnp.float32) * deviation
    if len(shards) > 0:
        entries = block_levels(stream_key, shape, shards, -0.22, 0.18) * entries
    return jnp.clip(entries, min=-most, max=most).astype(held_as)


def setup_inputs(seed: int = 0) -> dict:
    key_list = jax.random.split(jax.random.key(seed), 16)
    tokens = scatter_about(key_list[0], (MICRO, SEQS, LEN, D2), 1.0, 6.0, ((1, 8), (2, 4)))
    doc_ids = jax.vmap(lambda own: jnp.searchsorted(jnp.cumsum(ragged(own, DOCS, LEN, MOST_DOC, 2)), jnp.arange(LEN), side="right"))(jax.random.split(key_list[1], MICRO * SEQS)).reshape((MICRO, SEQS, LEN)).astype(jnp.int32)
    cotangent = scatter_about(key_list[2], (MICRO, SEQS, LEN, D2), 1.0, 6.0, ((1, 8), (2, 4)))
    enc_in = scatter_about(key_list[3], (D2 * D,), D2 ** -0.5, 0.15625, ((0, 32),))
    enc_conv = scatter_about(key_list[4], (ENCODER_TAPS * D * D,), (ENCODER_TAPS * D) ** -0.5, 0.09375, ((0, 32),))
    enc_out = scatter_about(key_list[5], (D * D2,), D ** -0.5, 0.21875, ((0, 32),))
    enc_gain = jnp.clip(1.0 + 0.15 * jax.random.normal(key_list[6], (D2 + 2 * D,), jnp.float32), 0.25, 1.75)
    enc_shift = scatter_about(key_list[7], (D2 + 2 * D,), 0.5, 3.0, (), jnp.float32)
    enc_bias = scatter_about(key_list[8], (D2,), 0.5, 3.0, (), jnp.float32)
    dec_in = scatter_about(key_list[9], (D2 * D,), D2 ** -0.5, 0.15625, ((0, 32),))
    dec_conv = scatter_about(key_list[10], (DECODER_TAPS * D * D,), (DECODER_TAPS * D) ** -0.5, 0.125, ((0, 32),))
    dec_out = scatter_about(key_list[11], (D * D2,), D ** -0.5, 0.21875, ((0, 32),))
    dec_gain = jnp.clip(1.0 + 0.15 * jax.random.normal(key_list[12], (D2 + 2 * D,), jnp.float32), 0.25, 1.75)
    dec_shift = scatter_about(key_list[13], (D2 + 2 * D,), 0.5, 3.0, (), jnp.float32)
    dec_bias = scatter_about(key_list[14], (D2,), 0.5, 3.0, (), jnp.float32)
    return {"tokens": tokens, "doc_ids": doc_ids, "cotangent": cotangent, "enc_in": enc_in, "enc_conv": enc_conv, "enc_out": enc_out, "enc_gain": enc_gain, "enc_shift": enc_shift, "enc_bias": enc_bias, "dec_in": dec_in, "dec_conv": dec_conv, "dec_out": dec_out, "dec_gain": dec_gain, "dec_shift": dec_shift, "dec_bias": dec_bias}


@jax.custom_vjp
def low(v):
    return lax.optimization_barrier(v.astype(jnp.bfloat16)).astype(jnp.float32)

@jax.custom_vjp
def low_back(v):
    return v

def low_keep(v):
    return (low(v), None)

def low_pass(kept, grad):
    return (grad,)

def back_keep(v):
    return (v, None)

def back_low(kept, grad):
    return (low(grad),)
low.defvjp(low_keep, low_pass)
low_back.defvjp(back_keep, back_low)
epsilon = 1e-05
FULL_ACCURACY = lax.Precision.HIGHEST

def normalize(values):
    centred = values - lax.optimization_barrier(jnp.mean(values, axis=-1, keepdims=True))
    return centred * lax.rsqrt(lax.optimization_barrier(jnp.mean(centred * centred, axis=-1, keepdims=True)) + epsilon)

def stacked_taps(activity, document_row, shift_offsets):
    reach_rows = max([abs(offset) for offset in shift_offsets])
    length = activity.shape[1]
    padded = jnp.pad(activity, ((0, 0), (reach_rows, reach_rows), (0, 0)))
    ids_pad = jnp.pad(document_row, ((0, 0), (reach_rows, reach_rows)), constant_values=-1)
    pieces = []
    for offset in shift_offsets:
        shifted = padded[:, reach_rows + offset:reach_rows + offset + length]
        same_doc = ids_pad[:, reach_rows + offset:reach_rows + offset + length] == document_row
        pieces.append(shifted * same_doc[:, :, None].astype(jnp.float32))
    return jnp.concatenate(pieces, axis=-1)

def block(inputs, document_row, weights, norm_gain, norm_shift, output_bias, shift_offsets):
    input_weight, convolution_weight, output_weight = weights
    wide_dim = input_weight.shape[0]
    narrow = input_weight.shape[1]
    hidden_one = normalize(inputs) * norm_gain[:wide_dim] + norm_shift[:wide_dim]
    act_first = low(jax.nn.silu(hidden_one))
    narrowed_rows = low_back(jnp.einsum('vhx,xq->vhq', act_first, input_weight, precision=FULL_ACCURACY))
    hidden_two = normalize(narrowed_rows) * norm_gain[wide_dim:wide_dim + narrow] + norm_shift[wide_dim:wide_dim + narrow]
    act_second = low(jax.nn.silu(hidden_two))
    convolved_output = low_back(jnp.einsum('vhx,xq->vhq', stacked_taps(act_second, document_row, shift_offsets), convolution_weight, precision=FULL_ACCURACY))
    hidden_three = normalize(convolved_output) * norm_gain[wide_dim + narrow:] + norm_shift[wide_dim + narrow:]
    act_third = low(jax.nn.silu(hidden_three))
    residual_branch = low_back(jnp.einsum('vhx,xq->vhq', act_third, output_weight, precision=FULL_ACCURACY) + output_bias)
    return inputs + residual_branch

def reference(tokens, doc_ids, cotangent, enc_in, enc_conv, enc_out, enc_gain, enc_shift, enc_bias, dec_in, dec_conv, dec_out, dec_gain, dec_shift, dec_bias):
    encoder_tap_offsets = [ENCODER_SPACING * (tap_position - (ENCODER_TAPS - 1) // 2) for tap_position in range(ENCODER_TAPS)]
    decoder_tap_offsets = [DECODER_SPACING * (tap_position - DECODER_TAPS + 1) for tap_position in range(DECODER_TAPS)]
    params = (enc_in.astype(jnp.float32).reshape(D2, D), enc_conv.astype(jnp.float32).reshape(ENCODER_TAPS * D, D), enc_out.astype(jnp.float32).reshape(D, D2), enc_gain, enc_shift, enc_bias, dec_in.astype(jnp.float32).reshape(D2, D), dec_conv.astype(jnp.float32).reshape(DECODER_TAPS * D, D), dec_out.astype(jnp.float32).reshape(D, D2), dec_gain, dec_shift, dec_bias)
    seq_total = MICRO * SEQS
    group_size = math.gcd(seq_total, max(1, 4096 // LEN))
    rounds = seq_total // group_size
    all_tokens = tokens.reshape(rounds, group_size, LEN, D2)
    all_ids = doc_ids.reshape(rounds, group_size, LEN)
    all_cot = cotangent.reshape(rounds, group_size, LEN, D2)

    def network(inputs, document_row, weights):
        middle = block(inputs, document_row, weights[0:3], weights[3], weights[4], weights[5], encoder_tap_offsets)
        return block(middle, document_row, weights[6:9], weights[9], weights[10], weights[11], decoder_tap_offsets)

    def one_round(running, pieces):
        inputs, document_row, grad_top = pieces
        final_rows, pullback = jax.vjp(lambda values, weights: network(values, document_row, weights), inputs.astype(jnp.float32), params)
        grad_inputs, grad_weights = pullback(grad_top.astype(jnp.float32))
        running = jax.tree.map(jnp.add, running, grad_weights)
        return (running, (final_rows.astype(jnp.bfloat16), grad_inputs))
    zero_grads = jax.tree.map(jnp.zeros_like, params)
    grad_sums, (finals, grad_rows) = lax.scan(one_round, zero_grads, (all_tokens, all_ids, all_cot))
    return (finals.reshape(MICRO, SEQS, LEN, D2), grad_rows.reshape(MICRO, SEQS, LEN, D2), grad_sums[0].reshape(-1), grad_sums[1].reshape(-1), grad_sums[2].reshape(-1), grad_sums[3], grad_sums[4], grad_sums[5], grad_sums[6].reshape(-1), grad_sums[7].reshape(-1), grad_sums[8].reshape(-1), grad_sums[9], grad_sums[10], grad_sums[11])
```

```python
import functools

import jax
import jax.numpy as jnp
from jax import lax
from jax.experimental import pallas as pl
from jax.experimental.pallas import tpu as pltpu
from jax.sharding import PartitionSpec as P

MESH = pl.DeviceIdType.MESH
D2 = 1600
D = 800
ENCODER_TAPS = 5
ENCODER_SPACING = 4
DECODER_TAPS = 3
DECODER_SPACING = 8


epsilon = 1e-05


def from_behind(value, axis, by):
    length = lax.axis_size(axis)
    pairs = [(i, i + by) for i in range(length) if 0 <= i + by < length]
    return lax.ppermute(value, axis, pairs)


def extended(value, sides, width):
    for axis, dim in sides:
        size, length = (lax.axis_size(axis), value.shape[dim])
        up = [(i, (i + 1) % size) for i in range(size - 1)]
        down = [(j, i) for i, j in up]
        last = lax.slice_in_dim(value, length - width, length, axis=dim)
        initial = lax.slice_in_dim(value, 0, width, axis=dim)
        before = lax.ppermute(last, axis, up)
        after = lax.ppermute(initial, axis, down)
        value = jnp.concatenate([before, value, after], axis=dim)
    return value


def normalize(values):
    centred = values - jnp.mean(values, axis=-1, keepdims=True)
    factor = lax.rsqrt(jnp.mean(centred * centred, axis=-1, keepdims=True) + epsilon)
    return (centred * factor, factor)


def silu_slope(hidden):
    sigma = jax.nn.sigmoid(hidden)
    return sigma * (1.0 + hidden * (1.0 - sigma))


def norm_back(grad_h, scale_row, normed, factor):
    scaled = grad_h * scale_row
    mean_one = jnp.mean(scaled, axis=-1, keepdims=True)
    mean_two = jnp.mean(scaled * normed, axis=-1, keepdims=True)
    grad_in = factor * (scaled - mean_one - normed * mean_two)
    return (grad_in, jnp.sum(grad_h * normed, axis=0), jnp.sum(grad_h, axis=0))


def tap_offsets(causal):
    if causal:
        return [
            DECODER_SPACING * (tap_position - DECODER_TAPS + 1)
            for tap_position in range(DECODER_TAPS)
        ]
    return [
        ENCODER_SPACING * (tap_position - (ENCODER_TAPS - 1) // 2)
        for tap_position in range(ENCODER_TAPS)
    ]


def stacked_taps(padded, lead_rows, seg_pad, segment_leading, shift_offsets, length):
    own_ids = seg_pad[:, segment_leading : segment_leading + length]
    pieces = []
    for offset in shift_offsets:
        shifted = padded[:, lead_rows + offset : lead_rows + offset + length]
        same_doc = (
            seg_pad[:, segment_leading + offset : segment_leading + offset + length] == own_ids
        )
        pieces.append(jnp.where(same_doc[:, :, None], shifted, jnp.zeros_like(shifted)))
    return jnp.concatenate(pieces, axis=-1)


def block_forward(
    inputs, seg_pad, segment_leading, weights, norm_gain, norm_shift, output_bias, causal
):
    input_weight, convolution_weight, output_weight = weights
    seqs_here, length, wide_dim = inputs.shape
    narrow = input_weight.shape[1]
    flat_rows = inputs.reshape(-1, wide_dim)
    normed_one, factor_one = normalize(flat_rows)
    hidden_one = normed_one * norm_gain[:wide_dim] + norm_shift[:wide_dim]
    act_first = jax.nn.silu(hidden_one).astype(jnp.bfloat16)
    narrowed_rows = jnp.dot(act_first, input_weight, preferred_element_type=jnp.float32)
    normed_two, factor_two = normalize(narrowed_rows)
    hidden_two = (
        normed_two * norm_gain[wide_dim : wide_dim + narrow]
        + norm_shift[wide_dim : wide_dim + narrow]
    )
    act_second = jax.nn.silu(hidden_two).astype(jnp.bfloat16).reshape(seqs_here, length, narrow)
    shift_offsets = tap_offsets(causal)
    reach_rows = max([abs(offset) for offset in shift_offsets])
    if causal:
        tail_rows = from_behind(act_second[:, length - reach_rows :], "seq", 1)
        padded = jnp.concatenate([tail_rows, act_second], axis=1)
    else:
        padded = extended(act_second, (("seq", 1),), reach_rows)
    stacked = stacked_taps(
        padded, reach_rows, seg_pad, segment_leading, shift_offsets, length
    ).reshape(flat_rows.shape[0], -1)
    convolved_output = jnp.dot(stacked, convolution_weight, preferred_element_type=jnp.float32)
    normed_three, factor_three = normalize(convolved_output)
    hidden_three = normed_three * norm_gain[wide_dim + narrow :] + norm_shift[wide_dim + narrow :]
    act_third = jax.nn.silu(hidden_three).astype(jnp.bfloat16)
    residual_branch = (
        jnp.dot(act_third, output_weight, preferred_element_type=jnp.float32) + output_bias
    )
    result = (flat_rows + residual_branch).reshape(inputs.shape)
    kept_state = (
        normed_one,
        factor_one,
        hidden_one,
        act_first,
        normed_two,
        factor_two,
        hidden_two,
        stacked,
        normed_three,
        factor_three,
        hidden_three,
        act_third,
    )
    return (result, kept_state)


def block_backward(
    grad_out, kept_state, seg_pad, segment_leading, weights, norm_gain, causal, seqs_here, length
):
    input_weight, convolution_weight, output_weight = weights
    (
        normed_one,
        factor_one,
        hidden_one,
        act_first,
        normed_two,
        factor_two,
        hidden_two,
        stacked,
        normed_three,
        factor_three,
        hidden_three,
        act_third,
    ) = kept_state
    wide_dim = input_weight.shape[0]
    narrow = input_weight.shape[1]
    grad_low = grad_out.astype(jnp.bfloat16)
    grad_bias = jnp.sum(grad_low.astype(jnp.float32), axis=0)
    grad_w_out = jnp.einsum("nc,nd->cd", act_third, grad_low, preferred_element_type=jnp.float32)
    grad_act = jnp.einsum("nd,cd->nc", grad_low, output_weight, preferred_element_type=jnp.float32)
    grad_act = grad_act * silu_slope(hidden_three)
    grad_conv_out, gain_three, shift_three = norm_back(
        grad_act, norm_gain[wide_dim + narrow :], normed_three, factor_three
    )
    grad_conv_low = grad_conv_out.astype(jnp.bfloat16)
    grad_w_conv = jnp.einsum(
        "nc,nd->cd", stacked, grad_conv_low, preferred_element_type=jnp.float32
    )
    shift_offsets = tap_offsets(causal)
    reach_rows = max([abs(offset) for offset in shift_offsets])
    grad_grid = grad_conv_low.reshape(seqs_here, length, narrow)
    if causal:
        head_rows = from_behind(grad_grid[:, :reach_rows], "seq", -1)
        padded = jnp.concatenate([grad_grid, head_rows], axis=1)
        lead_rows = 0
    else:
        padded = extended(grad_grid, (("seq", 1),), reach_rows)
        lead_rows = reach_rows
    back_stack = stacked_taps(
        padded, lead_rows, seg_pad, segment_leading, [-offset for offset in shift_offsets], length
    ).reshape(seqs_here * length, -1)
    grad_act = sum(
        lax.dot_general(
            back_stack[:, k * narrow : (k + 1) * narrow],
            convolution_weight[k * narrow : (k + 1) * narrow],
            (((1,), (1,)), ((), ())),
            preferred_element_type=jnp.float32,
        )
        for k in range(len(shift_offsets))
    )
    grad_act = grad_act * silu_slope(hidden_two)
    grad_narrow, gain_two, shift_two = norm_back(
        grad_act, norm_gain[wide_dim : wide_dim + narrow], normed_two, factor_two
    )
    grad_narrow_low = grad_narrow.astype(jnp.bfloat16)
    grad_w_in = jnp.einsum(
        "nc,nd->cd", act_first, grad_narrow_low, preferred_element_type=jnp.float32
    )
    grad_act = jnp.einsum(
        "nd,cd->nc", grad_narrow_low, input_weight, preferred_element_type=jnp.float32
    )
    grad_act = grad_act * silu_slope(hidden_one)
    grad_flat, gain_one, shift_one = norm_back(
        grad_act, norm_gain[:wide_dim], normed_one, factor_one
    )
    grad_input = grad_out + grad_flat
    grad_gain = jnp.concatenate([gain_one, gain_two, gain_three])
    grad_shift = jnp.concatenate([shift_one, shift_two, shift_three])
    return (
        grad_input,
        (grad_w_in, grad_w_conv, grad_w_out),
        (grad_gain, grad_shift, grad_bias),
    )


F32, BF = jnp.float32, jnp.bfloat16
T16 = 16
MATS = ((50, 800, False), (125, 800, True), (25, 1600, False), (50, 800, False), (75, 800, True), (25, 1600, False))

def tile_at(n, s): return (n * s + T16 - 1) // T16

def places():
    dp = lax.axis_index("dp"); z = lax.axis_index("seq")
    return dp // 4, (dp // 2) % 2, dp % 2, z

def dev(y, x, c, z): return ((y * 2 + x) * 2 + c, z)
def shard(y, x, c, z): return ((y * 2 + x) * 2 + c) * 4 + z

def when(cond, f):
    if cond is None: f()
    else: pl.when(cond)(f)

def both(a, b):
    if a is None: return b
    if b is None: return a
    return jnp.logical_and(a, b)

def greet(y, x, c, z):
    barrier = pltpu.get_barrier_semaphore()
    dp = (y * 2 + x) * 2 + c
    far_next = jnp.logical_and(z == 3, dp < 7)
    far_prev = jnp.logical_and(z == 0, dp > 0)
    peers = [(dev(y, 1 - x, c, z), None), (dev(1 - y, x, c, z), None), (dev(y, x, 1 - c, z), None)]
    peers += [((dp, (z + i) % 4), None) for i in (1, 2, 3)]
    peers += [((jnp.minimum(dp + 1, 7), 0), far_next), ((jnp.maximum(dp - 1, 0), 3), far_prev)]
    for d, cond in peers:
        when(cond, lambda d=d: pl.semaphore_signal(barrier, inc=1, device_id=d, device_id_type=MESH))
    pl.semaphore_wait(barrier, 6 + jnp.where(far_next, 1, 0) + jnp.where(far_prev, 1, 0))

class Sender:
    def __init__(self, sem): self.sem, self.sent = sem, []
    def __call__(self, src, dst, rsem, target, cond=None):
        d = pltpu.make_async_remote_copy(src_ref=src, dst_ref=dst, send_sem=self.sem.at[self.k], recv_sem=rsem,
                                         device_id=target, device_id_type=MESH)
        self.sent.append((d, cond))
        when(cond, d.start)
    def next(self): self.k = getattr(self, "k", -1) + 1
    def finish(self):
        for d, cond in self.sent: when(cond, d.wait_send)

def arrive(dst, rsem, ssem, me):
    pltpu.make_async_remote_copy(src_ref=dst, dst_ref=dst, send_sem=ssem, recv_sem=rsem, device_id=me, device_id_type=MESH).wait_recv()

def sizes(n, s, units):
    f, exact = (n * units) // T16, (n * units) % T16 == 0
    if exact: return [(f, None)]
    cnt = tile_at(n, s + units) - tile_at(n, s)
    return [(f, cnt == f), (f + 1, cnt == f + 1)]

def rows_at(n, s, tiles): return pl.ds(pl.multiple_of(tile_at(n, s) * T16, T16), tiles * T16)

def gather_kernel(order, *refs):
    nm = len(MATS)
    inp, out = refs[:nm], refs[nm:2 * nm]
    own, nxt = refs[2 * nm:3 * nm], refs[3 * nm:4 * nm]
    ext, exw, send_sem, recv_sem, n_sem, local_sem = refs[4 * nm:]
    y, x, c, z = places()
    X, Y, C = 1 - x, 1 - y, 1 - c
    dp = (y * 2 + x) * 2 + c
    me = shard(y, x, c, z)
    greet(y, x, c, z)
    here = dev(y, x, C, z)
    snd = Sender(send_sem)
    has_up, has_down = z < 3, z > 0
    tX, tY, tC = dev(y, X, c, z), dev(Y, x, c, z), dev(y, x, C, z)
    tU, tD = dev(y, x, c, jnp.minimum(z + 1, 3)), dev(y, x, c, jnp.maximum(z - 1, 0))
    has_prev, has_next = me > 0, me < 31
    prev = jnp.maximum(me - 1, 0)
    tP = (prev // 4, prev % 4)
    for m, (n, L, _) in enumerate(MATS):
        snd.next()
        snd(inp[m].at[pl.ds(0, T16)], nxt[m], n_sem.at[m], tP, has_prev)
    def build(m):
        n, L, _ = MATS[m]
        e = exw if L == 1600 else ext
        tiles = n // T16 + 1
        pl.when(has_next)(lambda: arrive(nxt[m], n_sem.at[m], send_sem.at[0], here))
        e[0:n, :] = inp[m][...].astype(F32)
        e[n:n + T16, :] = nxt[m][...].astype(F32)
        o = tile_at(n, me) * T16 - n * me
        size = -(-max(n + T16, 15 + tiles * T16) // 8) * 8
        v = pltpu.roll(e[0:size, :], lax.rem(size - o, size), axis=0)
        own[m][...] = v[0:tiles * T16].astype(BF)
    locals_ = []
    def send(m, s, target, cond=None, mine=False):
        n = MATS[m][0]
        snd.next()
        for tiles, c2 in sizes(n, s, 1):
            r = rows_at(n, s, tiles)
            src = own[m].at[pl.ds(0, tiles * T16)] if mine else out[m].at[r]
            snd(src, out[m].at[r], recv_sem.at[s, m], target, both(cond, c2))
    def wait(m, s, cond=None):
        n = MATS[m][0]
        for tiles, c2 in sizes(n, s, 1):
            when(both(cond, c2), lambda: arrive(out[m].at[rows_at(n, s, tiles)], recv_sem.at[s, m], send_sem.at[0], here))
    def first(m): return tX if MATS[m][2] else tY
    def second(m): return tY if MATS[m][2] else tX
    def st_own(m):
        build(m)
        send(m, me, first(m), None, True)
        send(m, me, tU, has_up, True)
        send(m, me, tD, has_down, True)
        send(m, me, second(m), None, True)
        send(m, me, tC, None, True)
        for tiles, c2 in sizes(MATS[m][0], me, 1):
            l = pltpu.make_async_copy(own[m].at[pl.ds(0, tiles * T16)], out[m].at[rows_at(MATS[m][0], me, tiles)], local_sem.at[m])
            locals_.append((l, c2)); when(c2, l.start)
    def st_z(m, d):
        for o, has, t, has_t in ((z - d, z - d >= 0, tU, has_up), (z + d, z + d <= 3, tD, has_down)):
            s = shard(y, x, c, jnp.clip(o, 0, 3))
            wait(m, s, has)
            send(m, s, first(m), has)
            if d < 3: send(m, s, t, jnp.logical_and(has, has_t))
            send(m, s, second(m), has)
            send(m, s, tC, has)
    def zorder(j):
        if j == 0: return [(z, None)]
        return [(jnp.clip(z - j, 0, 3), z - j >= 0), (jnp.clip(z + j, 0, 3), z + j <= 3)]
    def st_f(m, j):
        yy, xx = (y, X) if MATS[m][2] else (Y, x)
        for o, cond in zorder(j):
            s = shard(yy, xx, c, o)
            wait(m, s, cond)
            send(m, s, second(m), cond)
            send(m, s, tC, cond)
    def st_s(m, j):
        yy, xx = (Y, x) if MATS[m][2] else (y, X)
        for o, cond in zorder(j):
            s = shard(yy, xx, c, o)
            wait(m, s, cond)
            send(m, s, tC, cond)
    def st_d(m, j):
        for o, cond in zorder(j):
            s = shard(Y, X, c, o)
            wait(m, s, cond)
            send(m, s, tC, cond)
    ev = []
    for m in range(nm):
        def add(t, f, *a): ev.append((order(m, t), m, functools.partial(f, m, *a)))
        add(0, st_own)
        for d in (1, 2, 3): add(d, st_z, d)
        for j in range(4):
            add(1.1 + j, st_f, j)
            add(1.2 + j, st_s, j)
            add(2.3 + j, st_d, j)
    for _, _, f in sorted(ev, key=lambda e: (e[0], e[1])): f()
    for m in range(nm):
        for q in range(16): wait(m, shard(q // 8, (q // 4) % 2, C, q % 4))
    snd.finish()
    for l, c2 in locals_: when(c2, l.wait)

def gather(shards, order, cid=0):
    nm = len(MATS)
    any_ = pl.BlockSpec(memory_space=pl.ANY)
    vm = pl.BlockSpec(memory_space=pltpu.VMEM)
    V = pltpu.VMEM
    D_ = pltpu.SemaphoreType.DMA
    return pl.pallas_call(
        functools.partial(gather_kernel, order),
        out_shape=[jax.ShapeDtypeStruct((n * 32, L), BF) for n, L, _ in MATS],
        in_specs=[vm] * nm, out_specs=[any_] * nm,
        scratch_shapes=[V(((n // T16 + 1) * T16, L), BF) for n, L, _ in MATS] + [V((T16, L), BF) for n, L, _ in MATS]
        + [V((144, 800), F32), V((48, 1600), F32), D_((nm * 64,)), D_((32, nm)), D_((nm,)), D_((nm,))],
        compiler_params=pltpu.CompilerParams(collective_id=cid, has_side_effects=True, vmem_limit_bytes=24 * 2**20),
    )(*shards)

def scatter_kernel(order, *refs):
    nm = len(MATS)
    small_in, g = refs[0], refs[1:1 + nm]
    small_out, out = refs[1 + nm], refs[2 + nm:2 + 2 * nm]
    p = 2 + 2 * nm
    own, rbc, rb1, rb2, rbz = (refs[p + i * nm:p + (i + 1) * nm] for i in range(5))
    p += 5 * nm
    tail, res = refs[p:p + nm], refs[p + nm:p + 2 * nm]
    p += 2 * nm
    (sm_a, sm_r, sm_z, send_sem, c_sem, s1_sem, s2_sem, z_sem, t_sem, local_sem, sm_sem) = refs[p:]
    y, x, c, z = places()
    X, Y, C = 1 - x, 1 - y, 1 - c
    dp = (y * 2 + x) * 2 + c
    me = shard(y, x, c, z)
    greet(y, x, c, z)
    snd = Sender(send_sem)
    has_up, has_down = z < 3, z > 0
    tX, tY, tC = dev(y, X, c, z), dev(Y, x, c, z), dev(y, x, C, z)
    tU, tD = dev(y, x, c, jnp.minimum(z + 1, 3)), dev(y, x, c, jnp.maximum(z - 1, 0))
    edge = jnp.logical_or(z == 0, z == 3)
    mid = jnp.logical_not(edge)
    def wait(dst, rsem): arrive(dst, rsem, send_sem.at[0], tC)
    def groups(m):
        if MATS[m][2]: return [(Y, X), (y, X), (Y, x), (y, x)]
        return [(Y, X), (Y, x), (y, X), (y, x)]
    def first_shard(yy, xx, cc): return ((yy * 2 + xx) * 2 + cc) * 4
    def add(refs_, dst, r0, tiles):
        def body(i, _):
            r = pl.ds(pl.multiple_of(r0 + i * T16, T16), T16)
            t = refs_[0][r, :].astype(F32)
            for q in refs_[1:]: t = t + q[r, :].astype(F32)
            dst(i, r, t)
            return 0
        lax.fori_loop(0, tiles, body, 0)
    def st_start(m):
        n = MATS[m][0]
        for i, (yy, xx) in enumerate(groups(m)):
            q = yy * 2 + xx
            snd.next()
            s = first_shard(yy, xx, C)
            for tiles, c2 in sizes(n, s, 4):
                snd(g[m].at[rows_at(n, s, tiles)], rbc[m].at[q, pl.ds(0, tiles * T16)], c_sem.at[i, m], tC, c2)
            s = first_shard(yy, xx, c)
            for tiles, c2 in sizes(n, s, 4):
                when(c2, pltpu.make_async_copy(g[m].at[rows_at(n, s, tiles)], own[m].at[q, pl.ds(0, tiles * T16)], local_sem.at[i, m]).start)
    def got(m, i):
        n = MATS[m][0]
        yy, xx = groups(m)[i]
        q = yy * 2 + xx
        s = first_shard(yy, xx, c)
        for tiles, c2 in sizes(n, s, 4):
            r = pl.ds(0, tiles * T16)
            def f():
                wait(rbc[m].at[q, r], c_sem.at[i, m])
                pltpu.make_async_copy(rbc[m].at[q, r], own[m].at[q, r], local_sem.at[i, m]).wait()
            when(c2, f)
        return q, s, tile_at(n, s + 4) - tile_at(n, s)
    def st_1(m, i):
        n, _, xf = MATS[m]
        q, s, tiles = got(m, i)
        rest = (Y, y)[i] if xf else (X, x)[i]
        ow = own[m].at[q]
        def put(i, r, t): ow[r, :] = t.astype(BF)
        add([ow, rbc[m].at[q]], put, 0, tiles)
        snd.next()
        for t, c2 in sizes(n, s, 4):
            snd(own[m].at[q, pl.ds(0, t * T16)], rb1[m].at[rest, pl.ds(0, t * T16)], s1_sem.at[i, m], tX if xf else tY, c2)
    def wait1(m, s, slot, i):
        for t, c2 in sizes(MATS[m][0], s, 4):
            when(c2, lambda: wait(rb1[m].at[slot, pl.ds(0, t * T16)], s1_sem.at[i, m]))
    def st_2(m):
        n, _, xf = MATS[m]
        q, s, tiles = got(m, 2)
        rest = Y if xf else X
        wait1(m, s, rest, 0)
        ow = own[m].at[q]
        def put(i, r, t): ow[r, :] = t.astype(BF)
        add([ow, rbc[m].at[q], rb1[m].at[rest]], put, 0, tiles)
        snd.next()
        for t, c2 in sizes(n, s, 4):
            snd(own[m].at[q, pl.ds(0, t * T16)], rb2[m].at[pl.ds(0, t * T16)], s2_sem.at[m], tY if xf else tX, c2)
    def st_3(m):
        n, _, xf = MATS[m]
        q, s, tiles = got(m, 3)
        wait1(m, s, y if xf else x, 1)
        for t, c2 in sizes(n, s, 4):
            when(c2, lambda: wait(rb2[m].at[pl.ds(0, t * T16)], s2_sem.at[m]))
    def column(m, zz):
        n, _, xf = MATS[m]
        q = y * 2 + x
        s0 = first_shard(y, x, c)
        r0 = (tile_at(n, s0 + zz) - tile_at(n, s0)) * T16
        return [own[m].at[q], rbc[m].at[q], rb1[m].at[y if xf else x], rb2[m]], r0, tile_at(n, s0 + zz + 1) - tile_at(n, s0 + zz), s0 + zz
    def zwait(m, d, s, r0):
        for t, c2 in sizes(MATS[m][0], s, 1):
            when(c2, lambda: wait(rbz[m].at[d, pl.ds(pl.multiple_of(r0, T16), t * T16)], z_sem.at[d, s % 4, m]))
    def zsend(m, zz, d, comes, cond):
        refs_, r0, tiles, s = column(m, zz)
        ow = refs_[0]
        def put(i, r, t): ow[r, :] = t.astype(BF)
        @pl.when(cond)
        def _():
            more = []
            if comes:
                zwait(m, d, s, r0)
                more = [rbz[m].at[d]]
            add(refs_ + more, put, r0, tiles)
        t = tuple(jnp.where(d == 0, a, b) for a, b in zip(tU, tD))
        snd.next()
        for k, c2 in sizes(MATS[m][0], s, 1):
            r = pl.ds(pl.multiple_of(r0, T16), k * T16)
            snd(ow.at[r], rbz[m].at[d, r], z_sem.at[d, zz, m], t, both(cond, c2))
    def st_z1(m):
        d = jnp.where(z == 0, 0, 1)
        for i in range(3): zsend(m, jnp.where(z == 0, 3 - i, i), d, False, edge)
    def st_z2(m):
        d = jnp.where(z == 1, 0, 1)
        for i in range(2): zsend(m, jnp.where(z == 1, 3 - i, i), d, True, mid)
    def st_z3(m):
        d = jnp.where(z == 1, 1, 0)
        zsend(m, jnp.where(z == 1, 0, 3), d, True, mid)
    nxt = jnp.minimum(me + 1, 31)
    tN = (nxt // 4, nxt % 4)
    def st_z4(m):
        n = MATS[m][0]
        refs_, r0, tiles, s = column(m, z)
        d = jnp.where(z == 0, 1, 0)
        zwait(m, d, s, r0)
        def put(i, r, t): res[m][pl.ds(pl.multiple_of((i + 1) * T16, T16), T16), :] = t
        @pl.when(edge)
        def _(): add(refs_ + [rbz[m].at[d]], put, r0, tiles)
        @pl.when(mid)
        def _():
            zwait(m, 1, s, r0)
            add(refs_ + [rbz[m].at[0], rbz[m].at[1]], put, r0, tiles)
        snd.next()
        snd(res[m].at[pl.ds(pl.multiple_of(tiles * T16, T16), T16)], tail[m], t_sem.at[m], tN, me < 31)
    def st_out(m):
        n, L, _ = MATS[m]
        o = tile_at(n, me) * T16 - n * me
        pl.when(me > 0)(lambda: wait(tail[m], t_sem.at[m]))
        size = res[m].shape[0]
        res[m][0:T16, :] = tail[m][...]
        v = pltpu.roll(res[m][...], lax.rem(size - (T16 - o), size), axis=0)
        out[m][...] = v[0:n]
    def sm_pair(i, src, target, dst):
        snd.next()
        snd(src, sm_r.at[i], sm_sem.at[i], target)
        wait(sm_r.at[i], sm_sem.at[i])
        dst[...] = src[...] + sm_r[i]
    def sm_0(): sm_pair(0, small_in, tC, sm_a.at[0])
    def sm_1(): sm_pair(1, sm_a.at[0], tX, sm_a.at[1])
    def sm_2():
        sm_pair(2, sm_a.at[1], tY, sm_a.at[2])
        for i in (1, 2, 3):
            snd.next()
            snd(sm_a.at[2], sm_z.at[z], sm_sem.at[3 + i - 1], (dp, (z + i) % 4))
    def sm_3():
        sm_z[z] = sm_a[2]
        for i in (1, 2, 3): wait(sm_z.at[(z - i) % 4], sm_sem.at[3 + i - 1])
        small_out[...] = ((sm_z[0] + sm_z[1]) + sm_z[2]) + sm_z[3]
    ev = []
    for k, m in enumerate((5, 4, 3, 2, 1, 0)):
        def a(t, f, *ar): ev.append((order(k, t), k, functools.partial(f, m, *ar)))
        a(0, st_start)
        a(1, st_1, 0); a(1.3, st_1, 1); a(2, st_2); a(3, st_3); a(3.1, st_z1); a(4, st_z2); a(5, st_z3); a(6, st_z4)
        ev.append((1000, k, functools.partial(st_out, m)))
    ev += [(order(0, 0) , 10, sm_0), (order(1, 1), 10, sm_1), (order(2, 1), 10, sm_2), (order(5, 3), 10, sm_3)]
    for _, _, f in sorted(ev, key=lambda e: (e[0], e[1])): f()
    snd.finish()

def scatter(small, grads, order, cid=1):
    nm = len(MATS)
    any_ = pl.BlockSpec(memory_space=pl.ANY)
    vm = pl.BlockSpec(memory_space=pltpu.VMEM)
    V = pltpu.VMEM
    D_ = pltpu.SemaphoreType.DMA
    gr = [(4 * n // T16 + 1) * T16 for n, _, _ in MATS]
    def bufs(*lead): return [V(lead + (r, L), BF) for r, (_, L, _) in zip(gr, MATS)]
    return pl.pallas_call(
        functools.partial(scatter_kernel, order),
        out_shape=[jax.ShapeDtypeStruct(small.shape, F32)] + [jax.ShapeDtypeStruct((n, L), F32) for n, L, _ in MATS],
        in_specs=[vm] + [any_] * nm, out_specs=[vm] * (nm + 1),
        scratch_shapes=bufs(4) + bufs(4) + bufs(2) + bufs() + bufs(2)
        + [V((T16, L), F32) for _, L, _ in MATS] + [V((T16 + (n // T16 + 1) * T16, L), F32) for n, L, _ in MATS]
        + [V((3,) + small.shape, F32), V((3,) + small.shape, F32), V((4,) + small.shape, F32),
           D_((nm * 16 + 8,)), D_((4, nm)), D_((2, nm)), D_((nm,)), D_((2, 4, nm)), D_((nm,)), D_((4, nm)), D_((6,))],
        compiler_params=pltpu.CompilerParams(collective_id=cid, has_side_effects=True, vmem_limit_bytes=56 * 2**20),
    )(small, *grads)


EPS = 1e-5
W, N_ = 1600, 800
ROWS, LEN_ = 512, 256

def lane_tiles(n): return [(i, min(128, n - i)) for i in range(0, n, 128)]

def norm_of(v):
    c = v - jnp.mean(v, axis=-1, keepdims=True)
    r = lax.rsqrt(jnp.mean(c * c, axis=-1, keepdims=True) + EPS)
    return c * r, r

def sigmoid(h): return 1.0 / (1.0 + jnp.exp(-h))

def slope(h):
    s = sigmoid(h)
    return s * (1.0 + h * (1.0 - s))

def row_loop(step, body):
    def it(i, _):
        body(pl.multiple_of(i * step, step))
        return 0
    lax.fori_loop(0, ROWS // step, it, 0)

def put_transposed(dst, r, val, step):
    for c0, cn in lane_tiles(val.shape[1]):
        dst[c0:c0 + cn, pl.ds(r, step)] = jnp.transpose(val[:, c0:c0 + cn]).astype(BF)

def chunks(n, step):
    return n // step, n % step

def mm(lhs, w, out, epilogue=None, step=256):
    n = w.shape[1]
    full, rest = chunks(n, step)
    def one(c0, cn):
        t = jnp.dot(lhs[...], w[:, pl.ds(c0, cn)], preferred_element_type=F32)
        if epilogue is None: out[:, pl.ds(c0, cn)] = t
        else: epilogue(t, c0, cn)
    def it(i, _):
        one(pl.multiple_of(i * step, step), step)
        return 0
    lax.fori_loop(0, full, it, 0)
    if rest: one(full * step, rest)

def mm_taps(lhs, w, out, taps, step=256):
    full, rest = chunks(N_, step)
    def one(c0, cn):
        t = None
        for k in range(taps):
            d = jnp.dot(lhs[k], w[k * N_:(k + 1) * N_, pl.ds(c0, cn)], preferred_element_type=F32)
            t = d if t is None else t + d
        out[:, pl.ds(c0, cn)] = t
    def it(i, _):
        one(pl.multiple_of(i * step, step), step)
        return 0
    lax.fori_loop(0, full, it, 0)
    if rest: one(full * step, rest)

TT = (((1,), (1,)), ((), ()))

def mm_t(lhs, w, out, step=256):
    full, rest = chunks(w.shape[0], step)
    def one(c0, cn):
        out[:, pl.ds(c0, cn)] = lax.dot_general(lhs[...], w[pl.ds(c0, cn), :], TT, preferred_element_type=F32)
    def it(i, _):
        one(pl.multiple_of(i * step, step), step)
        return 0
    lax.fori_loop(0, full, it, 0)
    if rest: one(full * step, rest)

def mm_taps_t(lhs, w, out, taps, step=256):
    full, rest = chunks(N_, step)
    def one(c0, cn):
        t = None
        for k in range(taps):
            start = k * N_ + c0
            if not isinstance(c0, int): start = pl.multiple_of(start, 16)
            d = lax.dot_general(lhs[k], w[pl.ds(start, cn), :], TT, preferred_element_type=F32)
            t = d if t is None else t + d
        out[:, pl.ds(c0, cn)] = t
    def it(i, _):
        one(pl.multiple_of(i * step, step), step)
        return 0
    lax.fori_loop(0, full, it, 0)
    if rest: one(full * step, rest)

def fold8(v):
    return jnp.sum(v.reshape(v.shape[0] // 8, 8, v.shape[1]), axis=0)

def comp_kernel(tok_h, cot_h, ids_ref, ge_ref, gd_ref,
                wie_h, wce_h, woe_h, wid_h, wcd_h, wod_h,
                out_h, tg_h, small_ref, gie_h, gce_h, goe_h, gid_h, gcd_h, god_h,
                wie, wce, woe, wid, wcd, wod, tok, mid, ue, ve, ud, vd, a1b, a3b, a1te, a1td, a2te, a2td, a3te, a3td,
                ape, apd, gpe, idp, lk, big, st8, st16, acc1, acc2, acc3, accb,
                in_sem, h_send, h_recv, g_sem, o_sem):
    dp = lax.axis_index("dp"); z = lax.axis_index("seq")
    has_up, has_down = z < 3, z > 0
    tU, tD = (dp, jnp.minimum(z + 1, 3)), (dp, jnp.maximum(z - 1, 0))
    gpd, gub, obuf, cot = ape, a3b, a1b, tok
    loads = [pltpu.make_async_copy(s, d, in_sem.at[i]) for i, (s, d) in enumerate(
        [(tok_h, tok), (wie_h, wie), (wce_h, wce), (woe_h, woe), (wid_h, wid), (wcd_h, wcd), (wod_h, wod)])]
    for l in loads: l.start()
    barrier = pltpu.get_barrier_semaphore()
    for d, cond in ((tU, has_up), (tD, has_down)):
        @pl.when(cond)
        def _(d=d): pl.semaphore_signal(barrier, inc=1, device_id=d, device_id_type=MESH)
    pl.semaphore_wait(barrier, jnp.where(has_up, 1, 0) + jnp.where(has_down, 1, 0))

    def halo(k, buf, lead, reach, up, fill):
        if up:
            src, dst, target, can, arrives = buf.at[:, pl.ds(lead + LEN_ - reach, reach)], buf.at[:, pl.ds(lead - reach, reach)], tU, has_up, has_down
        else:
            src, dst, target, can, arrives = buf.at[:, pl.ds(lead, reach)], buf.at[:, pl.ds(lead + LEN_, reach)], tD, has_down, has_up
        d = pltpu.make_async_remote_copy(src_ref=src, dst_ref=dst, send_sem=h_send.at[k], recv_sem=h_recv.at[k], device_id=target, device_id_type=MESH)
        pl.when(can)(d.start)
        @pl.when(jnp.logical_not(arrives))
        def _(): dst[...] = jnp.full(dst.shape, fill, buf.dtype)
        return d, can, arrives
    def halo_wait(h):
        d, can, arrives = h
        pl.when(arrives)(d.wait_recv)
        pl.when(can)(d.wait_send)

    idp[:, 16:16 + LEN_] = ids_ref[...]
    h0, h1 = halo(0, idp, 16, 16, True, -1), halo(1, idp, 16, 16, False, -1)

    OE = [4 * (k - 2) for k in range(5)]
    OD = [8 * (k - 2) for k in range(3)]

    def first_norm(x_of, par, a, at, load=None):
        g, s = par[0:1, :], par[1:2, :]
        def body(r):
            n, _ = norm_of(x_of(r, 128))
            h = n * g + s
            a[pl.ds(r, 128), :] = (h * sigmoid(h)).astype(BF)
        row_loop(128, body)
        row_loop(128, lambda r: put_transposed(at, r, a[pl.ds(r, 128), :].astype(F32), 128))
    def mid_norm(u, par, row, dst, at):
        g, s = par[row:row + 1, 0:N_], par[row + 1:row + 2, 0:N_]
        def body(r):
            n, _ = norm_of(u[pl.ds(r, 128), :])
            h = n * g + s
            dst(r, 128, (h * sigmoid(h)).astype(BF))
        row_loop(128, body)
    def into(buf, lead):
        def dst(r, n, v):
            m = r // LEN_
            buf[m, pl.ds(pl.multiple_of(r - m * LEN_ + lead, 8), n), :] = v.astype(buf.dtype)
        return dst
    def transpose_pad(buf, lead, at):
        def it(i, _):
            m, q = i // 2, i % 2
            v = buf[m, pl.ds(pl.multiple_of(lead + q * 128, 8), 128), :]
            put_transposed(at, pl.multiple_of(i * 128, 128), v, 128)
            return 0
        lax.fori_loop(0, 4, it, 0)
    def stack(buf, lead, offsets):
        def it(m, _):
            rows = pl.ds(pl.multiple_of(m * LEN_, LEN_), LEN_)
            own = idp[m, 16:16 + LEN_, :]
            for k, o in enumerate(offsets):
                same = idp[m, 16 + o:16 + o + LEN_, :] == own
                for c0, cn in lane_tiles(N_):
                    v = buf[m, lead + o:lead + o + LEN_, c0:c0 + cn]
                    lk[k, rows, c0:c0 + cn] = jnp.where(same[:, :cn], v, 0.0).astype(BF)
            return 0
        lax.fori_loop(0, 2, it, 0)

    def forward(x_of, par, a1t, a2t, a3t, wi, wc, wo, u, v, ap, lead, offsets, hal, base, finish):
        first_norm(x_of, par, a1b, a1t)
        loads[base].wait()
        mm(a1b, wi, u)
        mid_norm(u, par, 3, into(ap, lead), None)
        hs = hal()
        transpose_pad(ap, lead, a2t)
        loads[base + 1].wait()
        for h in hs: halo_wait(h)
        stack(ap, lead, offsets)
        mm_taps(lk, wc, v, len(offsets))
        def keep3(r, n, val): a3b[pl.ds(r, n), :] = val
        mid_norm(v, par, 5, keep3, None)
        row_loop(128, lambda r: put_transposed(a3t, r, a3b[pl.ds(r, 128), :].astype(F32), 128))
        loads[base + 2].wait()
        bias = par[2:3, :]
        mm(a3b, wo, None, epilogue=finish)

    loads[0].wait()
    tok_rows = lambda r, n: tok[pl.ds(r, n), :].astype(F32)
    mid_rows = lambda r, n: mid[pl.ds(r, n), :]
    def fin_e(t, c0, cn):
        c = pl.ds(c0, cn)
        mid[:, c] = tok[:, c].astype(F32) + (t + ge_ref[2:3, c])
    halo_wait(h0); halo_wait(h1)
    forward(tok_rows, ge_ref, a1te, a2te, a3te, wie, wce, woe, ue, ve, ape, 8, OE,
            lambda: [halo(2, ape, 8, 8, True, 0), halo(3, ape, 8, 8, False, 0)], 1, fin_e)
    cot_load = pltpu.make_async_copy(cot_h, cot, in_sem.at[7])
    cot_load.start()
    def fin_d(t, c0, cn):
        c = pl.ds(c0, cn)
        obuf[:, c] = (mid[:, c] + (t + gd_ref[2:3, c])).astype(BF)
    forward(mid_rows, gd_ref, a1td, a2td, a3td, wid, wcd, wod, ud, vd, apd, 16, OD,
            lambda: [halo(4, apd, 16, 16, True, 0)], 4, fin_d)
    ocopy = pltpu.make_async_copy(obuf, out_h, o_sem.at[0])
    ocopy.start()

    used = [0, 0]
    def wgrad(at, rhs, dst, row0, which, step):
        st = (st8, st16)[which]
        m = at.shape[0]
        for i in range(m // step):
            k = used[which]; slot = k % 2
            c = pltpu.make_async_copy(st.at[slot], dst.at[pl.ds(row0 + i * step, step)], g_sem.at[which, slot])
            if k >= 2: c.wait()
            st[slot] = jnp.dot(at[i * step:(i + 1) * step, :], rhs, preferred_element_type=F32).astype(BF)
            c.start()
            used[which] += 1

    def back_norm(src, grad, par, row, accum, width, emit, step=128):
        g, s = par[row:row + 1, 0:width], par[row + 1:row + 2, 0:width]
        accum[...] = jnp.zeros_like(accum)
        def body(r):
            n, f = norm_of(src(r, step))
            h = n * g + s
            gh = grad[pl.ds(r, step), 0:width] * slope(h)
            accum[0] += fold8(gh * n)
            accum[1] += fold8(gh)
            p = gh * g
            m1 = jnp.mean(p, axis=-1, keepdims=True)
            m2 = jnp.mean(p * n, axis=-1, keepdims=True)
            emit(r, step, f * (p - m1 - n * m2))
        row_loop(step, body)

    def small(row, acc, width):
        small_ref[row:row + 1, 0:width] = jnp.sum(acc[0], axis=0, keepdims=True)
        small_ref[row + 1:row + 2, 0:width] = jnp.sum(acc[1], axis=0, keepdims=True)

    def backward(gy, par, sb, x_of, a1t, a2t, a3t, wi, wc, wo, u, v, gp, lead, offsets, hal, gi, gc, go, finish, load_x=None):
        accb[...] = jnp.zeros_like(accb)
        def bsum(r): accb[...] += fold8(gy[pl.ds(r, 32), :].astype(F32))
        row_loop(32, bsum)
        small_ref[sb + 2:sb + 3, :] = jnp.sum(accb[...], axis=0, keepdims=True)
        mm_t(gy, wo, big)
        wgrad(a3t, gy[...], go, 0, 1, 160)
        def keep(r, n, val): into(gp, lead)(r, n, val.astype(BF))
        back_norm(lambda r, n: v[pl.ds(r, n), :], big, par, 5, acc3, N_, keep)
        hs = hal()
        small(sb + 5, acc3, N_)
        for h in hs: halo_wait(h)
        stack(gp, lead, [-o for o in offsets])
        for k in range(len(offsets)): wgrad(a2t, lk[k], gc, k * N_, 0, 400)
        mm_taps_t(lk, wc, big, len(offsets))
        def keep2(r, n, val): gub[pl.ds(r, n), :] = val.astype(BF)
        back_norm(lambda r, n: u[pl.ds(r, n), :], big, par, 3, acc2, N_, keep2)
        small(sb + 3, acc2, N_)
        wgrad(a1t, gub[...], gi, 0, 0, 400)
        mm_t(gub, wi, big)
        if load_x is not None: load_x.wait()
        back_norm(x_of, big, par, 0, acc1, W, finish)
        small(sb, acc1, W)

    cot_load.wait()
    ocopy.wait()
    def fin_mid(r, n, val):
        g = cot[pl.ds(r, n), :].astype(F32) + val
        mid[pl.ds(r, n), :] = g
        obuf[pl.ds(r, n), :] = g.astype(BF)
    small_ref[...] = jnp.zeros_like(small_ref)
    backward(cot, gd_ref, 8, mid_rows, a1td, a2td, a3td, wid, wcd, wod, ud, vd, gpd, 0, OD,
             lambda: [halo(5, gpd, 0, 16, False, 0)], gid_h, gcd_h, god_h, fin_mid)
    tok_load = pltpu.make_async_copy(tok_h, tok, in_sem.at[7])
    tok_load.start()
    def fin_tok(r, n, val):
        mid[pl.ds(r, n), :] = mid[pl.ds(r, n), :] + val
    backward(obuf, ge_ref, 0, tok_rows, a1te, a2te, a3te, wie, wce, woe, ue, ve, gpe, 8, OE,
             lambda: [halo(6, gpe, 8, 8, True, 0), halo(7, gpe, 8, 8, False, 0)], gie_h, gce_h, goe_h, fin_tok, tok_load)
    tcopy = pltpu.make_async_copy(mid, tg_h, o_sem.at[1])
    tcopy.start()
    for which, (st, dst) in enumerate(((st8, gie_h), (st16, goe_h))):
        for slot in range(2):
            pltpu.make_async_copy(st.at[slot], dst.at[pl.ds(0, st.shape[1])], g_sem.at[which, slot]).wait()
    tcopy.wait()

def compute(tok, cot, ids, ge, gd, weights, cid=2):
    V = pltpu.VMEM
    any_ = pl.BlockSpec(memory_space=pl.ANY)
    vm = pl.BlockSpec(memory_space=pltpu.VMEM)
    sd = jax.ShapeDtypeStruct
    wshape = [(W, N_), (5 * N_, N_), (N_, W), (W, N_), (3 * N_, N_), (N_, W)]
    big_shape = [V(s, BF) for s in wshape]
    tbuf_alias = None
    scratch = big_shape + [V((ROWS, W), BF), V((ROWS, W), F32)] + [V((ROWS, N_), F32)] * 4 + [
        V((ROWS, W), BF), V((ROWS, N_), BF), V((W, ROWS), BF), V((W, ROWS), BF)] + [V((N_, ROWS), BF)] * 4 + [
        V((2, 272, N_), F32), V((2, 272, N_), F32), V((2, 272, N_), F32), V((2, 288, 128), jnp.int32),
        V((5, ROWS, N_), BF), V((ROWS, W), F32), V((2, 400, N_), BF), V((2, 160, W), BF),
        V((2, 8, W), F32), V((2, 8, N_), F32), V((2, 8, N_), F32), V((8, W), F32),
        pltpu.SemaphoreType.DMA((8,)), pltpu.SemaphoreType.DMA((8,)), pltpu.SemaphoreType.DMA((8,)), pltpu.SemaphoreType.DMA((2, 2)), pltpu.SemaphoreType.DMA((2,))]
    return pl.pallas_call(
        comp_kernel,
        out_shape=[sd((ROWS, W), BF), sd((ROWS, W), F32), sd((16, W), F32)] + [sd(s, BF) for s in wshape],
        in_specs=[any_, any_, vm, vm, vm] + [any_] * 6,
        out_specs=[any_, any_, vm] + [any_] * 6,
        scratch_shapes=scratch,
        compiler_params=pltpu.CompilerParams(collective_id=cid, has_side_effects=True, vmem_limit_bytes=63 * 2**20),
    )(tok, cot, ids, ge, gd, *weights)


def per_device(
    tokens, doc_ids, cotangent, enc_in, enc_conv, enc_out, enc_gain, enc_shift, enc_bias,
    dec_in, dec_conv, dec_out, dec_gain, dec_shift, dec_bias,
):
    flat = [enc_in, enc_conv, enc_out, dec_in, dec_conv, dec_out]
    size = lax.axis_size("dp"), lax.axis_size("seq"), tokens.shape
    if size != (8, 4, (2, 1, LEN_, W)):
        return any_mesh(
            tokens, doc_ids, cotangent, flat, (enc_gain, enc_shift, enc_bias), (dec_gain, dec_shift, dec_bias)
        )
    order = lambda k, t: t + k * 0.01
    weights = gather([w.reshape(n, L) for w, (n, L, _) in zip(flat, MATS)], order)
    ids = jnp.broadcast_to(doc_ids.reshape(2, LEN_, 1), (2, LEN_, 128))
    res = compute(
        tokens.reshape(ROWS, W), cotangent.reshape(ROWS, W), ids,
        table(enc_gain, enc_shift, enc_bias), table(dec_gain, dec_shift, dec_bias), weights,
    )
    sums = scatter(res[2], res[3:], lambda k, t: t + k)
    s, w = sums[0], [g.reshape(-1) for g in sums[1:]]
    e, d = untable(s[0:8]), untable(s[8:16])
    return (
        res[0].reshape(tokens.shape), res[1].reshape(tokens.shape), w[0], w[1], w[2], *e, w[3], w[4], w[5], *d,
    )


def table(gain, shift, bias):
    def wide(v): return jnp.pad(v, (0, W - v.shape[0]))
    one, two, three = slice(0, W), slice(W, W + N_), slice(W + N_, W + 2 * N_)
    rows = [gain[one], shift[one], bias, wide(gain[two]), wide(shift[two]), wide(gain[three]), wide(shift[three]), jnp.zeros((W,), F32)]
    return jnp.stack(rows)


def untable(s):
    gain = jnp.concatenate([s[0], s[3, :N_], s[5, :N_]])
    shift = jnp.concatenate([s[1], s[4, :N_], s[6, :N_]])
    return gain, shift, s[2]


def any_mesh(tokens, doc_ids, cotangent, flat, enc_small, dec_small):
    micro_count, seqs_here, length, wide_dim = tokens.shape
    count = micro_count * seqs_here
    lead = max(ENCODER_SPACING * ((ENCODER_TAPS - 1) // 2), DECODER_SPACING * (DECODER_TAPS - 1))
    seg_pad = extended(doc_ids.reshape(count, length), (("seq", 1),), lead)
    whole = [lax.all_gather(w, ("dp", "seq"), axis=0, tiled=True) for w in flat]
    enc, dec = [
        (whole[i].reshape(D2, D), whole[i + 1].reshape(-1, D), whole[i + 2].reshape(D, D2)) for i in (0, 3)
    ]
    rows = tokens.astype(jnp.float32).reshape(count, length, wide_dim)
    middle, enc_kept = block_forward(rows, seg_pad, lead, enc, *enc_small, False)
    final_rows, dec_kept = block_forward(middle, seg_pad, lead, dec, *dec_small, True)
    output = final_rows.astype(jnp.bfloat16).reshape(tokens.shape)
    grad_final = cotangent.astype(jnp.float32).reshape(-1, wide_dim)
    grad_middle, dec_w, dec_s = block_backward(
        grad_final, dec_kept, seg_pad, lead, dec, dec_small[0], True, count, length
    )
    grad_start, enc_w, enc_s = block_backward(
        grad_middle, enc_kept, seg_pad, lead, enc, enc_small[0], False, count, length
    )
    w = [lax.psum_scatter(g.reshape(-1), ("dp", "seq"), scatter_dimension=0, tiled=True) for g in enc_w + dec_w]
    s = lax.psum(enc_s + dec_s, ("dp", "seq"))
    return (
        output, grad_start.reshape(tokens.shape), w[0], w[1], w[2], s[0], s[1], s[2],
        w[3], w[4], w[5], s[3], s[4], s[5],
    )


def solution(mesh):
    placed = (
        P(None, "dp", "seq", None),
        P(None, "dp", "seq"),
        P(None, "dp", "seq", None),
        P(("dp", "seq")),
        P(("dp", "seq")),
        P(("dp", "seq")),
        P(),
        P(),
        P(),
        P(("dp", "seq")),
        P(("dp", "seq")),
        P(("dp", "seq")),
        P(),
        P(),
        P(),
    )
    return jax.shard_map(
        per_device,
        mesh=mesh,
        in_specs=placed,
        out_specs=(
            P(None, "dp", "seq", None),
            P(None, "dp", "seq", None),
            P(("dp", "seq")),
            P(("dp", "seq")),
            P(("dp", "seq")),
            P(),
            P(),
            P(),
            P(("dp", "seq")),
            P(("dp", "seq")),
            P(("dp", "seq")),
            P(),
            P(),
            P(),
        ),
        check_vma=False,
    )
```

```python
import functools

import jax
import jax.numpy as jnp
from jax import lax
from jax.experimental import pallas as pl
from jax.experimental.pallas import tpu as pltpu
from jax.sharding import PartitionSpec as P

MESH = pl.DeviceIdType.MESH
D2 = 1600
D = 800
ENCODER_TAPS = 5
ENCODER_SPACING = 4
DECODER_TAPS = 3
DECODER_SPACING = 8


epsilon = 1e-05


def from_behind(value, axis, by):
    length = lax.axis_size(axis)
    pairs = [(i, i + by) for i in range(length) if 0 <= i + by < length]
    return lax.ppermute(value, axis, pairs)


def extended(value, sides, width):
    for axis, dim in sides:
        size, length = (lax.axis_size(axis), value.shape[dim])
        up = [(i, (i + 1) % size) for i in range(size - 1)]
        down = [(j, i) for i, j in up]
        last = lax.slice_in_dim(value, length - width, length, axis=dim)
        initial = lax.slice_in_dim(value, 0, width, axis=dim)
        before = lax.ppermute(last, axis, up)
        after = lax.ppermute(initial, axis, down)
        value = jnp.concatenate([before, value, after], axis=dim)
    return value


def normalize(values):
    centred = values - jnp.mean(values, axis=-1, keepdims=True)
    factor = lax.rsqrt(jnp.mean(centred * centred, axis=-1, keepdims=True) + epsilon)
    return (centred * factor, factor)


def silu_slope(hidden):
    sigma = jax.nn.sigmoid(hidden)
    return sigma * (1.0 + hidden * (1.0 - sigma))


def norm_back(grad_h, scale_row, normed, factor):
    scaled = grad_h * scale_row
    mean_one = jnp.mean(scaled, axis=-1, keepdims=True)
    mean_two = jnp.mean(scaled * normed, axis=-1, keepdims=True)
    grad_in = factor * (scaled - mean_one - normed * mean_two)
    return (grad_in, jnp.sum(grad_h * normed, axis=0), jnp.sum(grad_h, axis=0))


def tap_offsets(causal):
    if causal:
        return [
            DECODER_SPACING * (tap_position - DECODER_TAPS + 1)
            for tap_position in range(DECODER_TAPS)
        ]
    return [
        ENCODER_SPACING * (tap_position - (ENCODER_TAPS - 1) // 2)
        for tap_position in range(ENCODER_TAPS)
    ]


def stacked_taps(padded, lead_rows, seg_pad, segment_leading, shift_offsets, length):
    own_ids = seg_pad[:, segment_leading : segment_leading + length]
    pieces = []
    for offset in shift_offsets:
        shifted = padded[:, lead_rows + offset : lead_rows + offset + length]
        same_doc = (
            seg_pad[:, segment_leading + offset : segment_leading + offset + length] == own_ids
        )
        pieces.append(jnp.where(same_doc[:, :, None], shifted, jnp.zeros_like(shifted)))
    return jnp.concatenate(pieces, axis=-1)


def block_forward(
    inputs, seg_pad, segment_leading, weights, norm_gain, norm_shift, output_bias, causal
):
    input_weight, convolution_weight, output_weight = weights
    seqs_here, length, wide_dim = inputs.shape
    narrow = input_weight.shape[1]
    flat_rows = inputs.reshape(-1, wide_dim)
    normed_one, factor_one = normalize(flat_rows)
    hidden_one = normed_one * norm_gain[:wide_dim] + norm_shift[:wide_dim]
    act_first = jax.nn.silu(hidden_one).astype(jnp.bfloat16)
    narrowed_rows = jnp.dot(act_first, input_weight, preferred_element_type=jnp.float32)
    normed_two, factor_two = normalize(narrowed_rows)
    hidden_two = (
        normed_two * norm_gain[wide_dim : wide_dim + narrow]
        + norm_shift[wide_dim : wide_dim + narrow]
    )
    act_second = jax.nn.silu(hidden_two).astype(jnp.bfloat16).reshape(seqs_here, length, narrow)
    shift_offsets = tap_offsets(causal)
    reach_rows = max([abs(offset) for offset in shift_offsets])
    if causal:
        tail_rows = from_behind(act_second[:, length - reach_rows :], "seq", 1)
        padded = jnp.concatenate([tail_rows, act_second], axis=1)
    else:
        padded = extended(act_second, (("seq", 1),), reach_rows)
    stacked = stacked_taps(
        padded, reach_rows, seg_pad, segment_leading, shift_offsets, length
    ).reshape(flat_rows.shape[0], -1)
    convolved_output = jnp.dot(stacked, convolution_weight, preferred_element_type=jnp.float32)
    normed_three, factor_three = normalize(convolved_output)
    hidden_three = normed_three * norm_gain[wide_dim + narrow :] + norm_shift[wide_dim + narrow :]
    act_third = jax.nn.silu(hidden_three).astype(jnp.bfloat16)
    residual_branch = (
        jnp.dot(act_third, output_weight, preferred_element_type=jnp.float32) + output_bias
    )
    result = (flat_rows + residual_branch).reshape(inputs.shape)
    kept_state = (
        normed_one,
        factor_one,
        hidden_one,
        act_first,
        normed_two,
        factor_two,
        hidden_two,
        stacked,
        normed_three,
        factor_three,
        hidden_three,
        act_third,
    )
    return (result, kept_state)


def block_backward(
    grad_out, kept_state, seg_pad, segment_leading, weights, norm_gain, causal, seqs_here, length
):
    input_weight, convolution_weight, output_weight = weights
    (
        normed_one,
        factor_one,
        hidden_one,
        act_first,
        normed_two,
        factor_two,
        hidden_two,
        stacked,
        normed_three,
        factor_three,
        hidden_three,
        act_third,
    ) = kept_state
    wide_dim = input_weight.shape[0]
    narrow = input_weight.shape[1]
    grad_low = grad_out.astype(jnp.bfloat16)
    grad_bias = jnp.sum(grad_low.astype(jnp.float32), axis=0)
    grad_w_out = jnp.einsum("nc,nd->cd", act_third, grad_low, preferred_element_type=jnp.float32)
    grad_act = jnp.einsum("nd,cd->nc", grad_low, output_weight, preferred_element_type=jnp.float32)
    grad_act = grad_act * silu_slope(hidden_three)
    grad_conv_out, gain_three, shift_three = norm_back(
        grad_act, norm_gain[wide_dim + narrow :], normed_three, factor_three
    )
    grad_conv_low = grad_conv_out.astype(jnp.bfloat16)
    grad_w_conv = jnp.einsum(
        "nc,nd->cd", stacked, grad_conv_low, preferred_element_type=jnp.float32
    )
    shift_offsets = tap_offsets(causal)
    reach_rows = max([abs(offset) for offset in shift_offsets])
    grad_grid = grad_conv_low.reshape(seqs_here, length, narrow)
    if causal:
        head_rows = from_behind(grad_grid[:, :reach_rows], "seq", -1)
        padded = jnp.concatenate([grad_grid, head_rows], axis=1)
        lead_rows = 0
    else:
        padded = extended(grad_grid, (("seq", 1),), reach_rows)
        lead_rows = reach_rows
    back_stack = stacked_taps(
        padded, lead_rows, seg_pad, segment_leading, [-offset for offset in shift_offsets], length
    ).reshape(seqs_here * length, -1)
    grad_act = sum(
        lax.dot_general(
            back_stack[:, k * narrow : (k + 1) * narrow],
            convolution_weight[k * narrow : (k + 1) * narrow],
            (((1,), (1,)), ((), ())),
            preferred_element_type=jnp.float32,
        )
        for k in range(len(shift_offsets))
    )
    grad_act = grad_act * silu_slope(hidden_two)
    grad_narrow, gain_two, shift_two = norm_back(
        grad_act, norm_gain[wide_dim : wide_dim + narrow], normed_two, factor_two
    )
    grad_narrow_low = grad_narrow.astype(jnp.bfloat16)
    grad_w_in = jnp.einsum(
        "nc,nd->cd", act_first, grad_narrow_low, preferred_element_type=jnp.float32
    )
    grad_act = jnp.einsum(
        "nd,cd->nc", grad_narrow_low, input_weight, preferred_element_type=jnp.float32
    )
    grad_act = grad_act * silu_slope(hidden_one)
    grad_flat, gain_one, shift_one = norm_back(
        grad_act, norm_gain[:wide_dim], normed_one, factor_one
    )
    grad_input = grad_out + grad_flat
    grad_gain = jnp.concatenate([gain_one, gain_two, gain_three])
    grad_shift = jnp.concatenate([shift_one, shift_two, shift_three])
    return (
        grad_input,
        (grad_w_in, grad_w_conv, grad_w_out),
        (grad_gain, grad_shift, grad_bias),
    )


EPS = 1e-5
F32, BF = jnp.float32, jnp.bfloat16
W, N_ = 1600, 800
ROWS, LEN_ = 512, 256
T16 = 16
MATS = ((50, 800, False), (125, 800, True), (25, 1600, False), (50, 800, False), (75, 800, True), (25, 1600, False))
ENC_OFF = [ENCODER_SPACING * (k - 2) for k in range(ENCODER_TAPS)]
DEC_OFF = [DECODER_SPACING * (k - 2) for k in range(DECODER_TAPS)]
ROW_ROW = (((1,), (1,)), ((), ()))
COL_COL = (((0,), (0,)), ((), ()))


def tile_at(n, s):
    return (n * s + T16 - 1) // T16


def dev(y, x, c, z):
    return ((y * 2 + x) * 2 + c, z)


def shard(y, x, c, z):
    return ((y * 2 + x) * 2 + c) * 4 + z


def when(cond, f):
    if cond is None:
        f()
    else:
        pl.when(cond)(f)


def both(a, b):
    if a is None:
        return b
    return a if b is None else jnp.logical_and(a, b)


def sizes(n, s, units):
    f = (n * units) // T16
    if (n * units) % T16 == 0:
        return [(f, None)]
    cnt = tile_at(n, s + units) - tile_at(n, s)
    return [(f, cnt == f), (f + 1, cnt == f + 1)]


def most(n, units):
    return ((n * units) // T16 + 1) * T16


def from_tile(t, tiles):
    return pl.ds(pl.multiple_of(t * T16, T16), tiles * T16)


def lane_tiles(n):
    return [(i, min(128, n - i)) for i in range(0, n, 128)]


def steps(n, step):
    return [(i, min(step, n - i)) for i in range(0, n, step)]


def norm_of(v):
    c = v - jnp.mean(v, axis=-1, keepdims=True)
    r = lax.rsqrt(jnp.mean(c * c, axis=-1, keepdims=True) + EPS)
    return c * r, r


def sigmoid(h):
    return 1.0 / (1.0 + jnp.exp(-h))


def slope(h):
    s = sigmoid(h)
    return s * (1.0 + h * (1.0 - s))


def row_loop(step, body):
    def it(i, _):
        body(pl.multiple_of(i * step, step))
        return 0

    lax.fori_loop(0, ROWS // step, it, 0)


def fold8(v):
    return jnp.sum(v.reshape(v.shape[0] // 8, 8, v.shape[1]), axis=0)


class Net:
    def __init__(self, send_sem):
        dp, z = lax.axis_index("dp"), lax.axis_index("seq")
        y, x, c = dp // 4, (dp // 2) % 2, dp % 2
        self.dp, self.y, self.x, self.c, self.z = dp, y, x, c, z
        self.X, self.Y, self.C = 1 - x, 1 - y, 1 - c
        self.me = shard(y, x, c, z)
        self.has_up, self.has_down = z < 3, z > 0
        self.tX, self.tY, self.tC = dev(y, 1 - x, c, z), dev(1 - y, x, c, z), dev(y, x, 1 - c, z)
        self.tU, self.tD = (dp, jnp.minimum(z + 1, 3)), (dp, jnp.maximum(z - 1, 0))
        nxt, prv = jnp.minimum(self.me + 1, 31), jnp.maximum(self.me - 1, 0)
        self.tN, self.tP = (nxt // 4, nxt % 4), (prv // 4, prv % 4)
        self.send_sem, self.k, self.sent = send_sem, -1, []

    def greet(self):
        barrier = pltpu.get_barrier_semaphore()
        far_next = jnp.logical_and(self.z == 3, self.dp < 7)
        far_prev = jnp.logical_and(self.z == 0, self.dp > 0)
        peers = [(self.tX, None), (self.tY, None), (self.tC, None)]
        peers += [((self.dp, (self.z + i) % 4), None) for i in (1, 2, 3)]
        peers += [(self.tN, far_next), (self.tP, far_prev)]
        for d, cond in peers:
            when(cond, lambda d=d: pl.semaphore_signal(barrier, inc=1, device_id=d, device_id_type=MESH))
        pl.semaphore_wait(barrier, 6 + jnp.where(far_next, 1, 0) + jnp.where(far_prev, 1, 0))

    def slot(self):
        self.k += 1

    def send(self, src, dst, rsem, target, cond=None):
        d = pltpu.make_async_remote_copy(
            src_ref=src, dst_ref=dst, send_sem=self.send_sem.at[self.k], recv_sem=rsem,
            device_id=target, device_id_type=MESH,
        )
        self.sent.append((d, cond))
        when(cond, d.start)

    def arrived(self, dst, rsem):
        pltpu.make_async_remote_copy(
            src_ref=dst, dst_ref=dst, send_sem=self.send_sem.at[0], recv_sem=rsem,
            device_id=self.tC, device_id_type=MESH,
        ).wait_recv()

    def finish(self):
        for d, cond in self.sent:
            when(cond, d.wait_send)
        self.sent = []


def zorder(z, j):
    if j == 0:
        return [(z, None)]
    return [(jnp.clip(z - j, 0, 3), z - j >= 0), (jnp.clip(z + j, 0, 3), z + j <= 3)]


def gather_events(net, inp, out, own, nxt, ext, recv_sem, n_sem, local_sem, time):
    y, x, c, z, X, Y, C, me = net.y, net.x, net.c, net.z, net.X, net.Y, net.C, net.me
    pending = []

    def ask():
        for m in range(len(MATS)):
            net.slot()
            net.send(inp[m].at[pl.ds(0, T16)], nxt[m], n_sem.at[m], net.tP, me > 0)

    def build(m):
        n, L, _ = MATS[m]
        tiles = n // T16 + 1
        pl.when(me < 31)(lambda: net.arrived(nxt[m], n_sem.at[m]))
        ext[0:n, 0:L] = inp[m][...].astype(F32)
        ext[n : n + T16, 0:L] = nxt[m][...].astype(F32)
        o = tile_at(n, me) * T16 - n * me
        size = -(-max(n + T16, 15 + tiles * T16) // 8) * 8
        v = pltpu.roll(ext[0:size, 0:L], lax.rem(size - o, size), axis=0)
        own[m][...] = v[0 : tiles * T16].astype(BF)

    def send(m, s, target, cond=None, mine=False):
        n = MATS[m][0]
        net.slot()
        for tiles, c2 in sizes(n, s, 1):
            r = from_tile(tile_at(n, s), tiles)
            src = own[m].at[pl.ds(0, tiles * T16)] if mine else out[m].at[r]
            net.send(src, out[m].at[r], recv_sem.at[s, m], target, both(cond, c2))

    def wait(m, s, cond=None):
        n = MATS[m][0]
        for tiles, c2 in sizes(n, s, 1):
            when(both(cond, c2), lambda: net.arrived(out[m].at[from_tile(tile_at(n, s), tiles)], recv_sem.at[s, m]))

    def first(m):
        return net.tX if MATS[m][2] else net.tY

    def second(m):
        return net.tY if MATS[m][2] else net.tX

    def st_own(m):
        build(m)
        send(m, me, first(m), None, True)
        send(m, me, net.tU, net.has_up, True)
        send(m, me, net.tD, net.has_down, True)
        send(m, me, second(m), None, True)
        send(m, me, net.tC, None, True)
        for tiles, c2 in sizes(MATS[m][0], me, 1):
            l = pltpu.make_async_copy(
                own[m].at[pl.ds(0, tiles * T16)], out[m].at[from_tile(tile_at(MATS[m][0], me), tiles)], local_sem.at[m]
            )
            pending.append((m, l, c2))
            when(c2, l.start)

    def st_z(m, d):
        for o, has, t, has_t in (
            (z - d, z - d >= 0, net.tU, net.has_up), (z + d, z + d <= 3, net.tD, net.has_down)
        ):
            s = shard(y, x, c, jnp.clip(o, 0, 3))
            wait(m, s, has)
            send(m, s, first(m), has)
            if d < 3:
                send(m, s, t, jnp.logical_and(has, has_t))
            send(m, s, second(m), has)
            send(m, s, net.tC, has)

    def st_f(m, j):
        yy, xx = (y, X) if MATS[m][2] else (Y, x)
        for o, cond in zorder(z, j):
            s = shard(yy, xx, c, o)
            wait(m, s, cond)
            send(m, s, second(m), cond)
            send(m, s, net.tC, cond)

    def st_s(m, j):
        yy, xx = (Y, x) if MATS[m][2] else (y, X)
        for o, cond in zorder(z, j):
            s = shard(yy, xx, c, o)
            wait(m, s, cond)
            send(m, s, net.tC, cond)

    def st_d(m, j):
        for o, cond in zorder(z, j):
            s = shard(Y, X, c, o)
            wait(m, s, cond)
            send(m, s, net.tC, cond)

    def rest(m):
        for q in range(16):
            wait(m, shard(q // 8, (q // 4) % 2, C, q % 4))
        for k, l, c2 in pending:
            if k == m:
                when(c2, l.wait)

    ev = [(-1.0, 0, ask)]
    for m in range(len(MATS)):

        def add(t, f, *a):
            ev.append((time(m, t), m, functools.partial(f, m, *a)))

        add(0, st_own)
        for d in (1, 2, 3):
            add(d, st_z, d)
        for j in range(4):
            add(1.1 + j, st_f, j)
            add(1.2 + j, st_s, j)
            add(2.3 + j, st_d, j)
    return sorted(ev, key=lambda e: (e[0], e[1])), rest


def sum_events(net, mats, grads, b, time):
    y, x, c, z, X, Y, C, me = net.y, net.x, net.c, net.z, net.X, net.Y, net.C, net.me
    pieces = [(m, h) for m in mats for h in (0, 1)]

    def groups(p):
        return [(Y, X), (y, X), (Y, x), (y, x)] if p[1] == 0 else [(Y, X), (Y, x), (y, X), (y, x)]

    def span(p, yy, xx, cc):
        m, h = p
        n = MATS[m][0]
        s0 = ((yy * 2 + xx) * 2 + cc) * 4
        s = s0 + 2 * h
        return s, tile_at(n, s), tile_at(n, s) - tile_at(n, s0)

    def add(srcs, put, tiles):
        def body(i, _):
            t = None
            for ref, t0 in srcs:
                v = ref[from_tile(t0 + i, 1), :].astype(F32)
                t = v if t is None else t + v
            put(i, t)
            return 0

        lax.fori_loop(0, tiles, body, 0)

    units = []
    started = {}

    def load(j):
        if j >= len(units) or j in started:
            return
        p, i = units[j]
        m = p[0]
        n = MATS[m][0]
        s, t0, _ = span(p, *groups(p)[i], c)
        st = b.stage(m)
        started[j] = []
        for tiles, c2 in sizes(n, s, 2):
            l = pltpu.make_async_copy(
                grads[m].at[from_tile(t0, tiles)], st.at[j % 2, pl.ds(0, tiles * T16)], b.local_sem.at[j % 2]
            )
            started[j].append((l, c2))
            when(c2, l.start)

    def st_start(p):
        m = p[0]
        k = pieces.index(p)
        for i, (yy, xx) in enumerate(groups(p)):
            s, t0, o = span(p, yy, xx, C)
            net.slot()
            for tiles, c2 in sizes(MATS[m][0], s, 2):
                net.send(
                    grads[m].at[from_tile(t0, tiles)], b.rbc[m](yy * 2 + xx).at[from_tile(o, tiles)],
                    b.c_sem.at[i, k], net.tC, c2,
                )

    def unit(p, i):
        m, h = p
        k = pieces.index(p)
        n = MATS[m][0]
        yy, xx = groups(p)[i]
        q = yy * 2 + xx
        s, _, o = span(p, yy, xx, c)
        j = units.index((p, i))
        load(j)
        cnt = tile_at(n, s + 2) - tile_at(n, s)
        buf = b.rbc[m](q)
        srcs = [(b.stage(m).at[j % 2], 0), (buf, o)]
        o0 = h * (most(n, 2) // T16)
        for tiles, c2 in sizes(n, s, 2):

            def ready():
                r = from_tile(o, tiles)
                net.arrived(buf.at[r], b.c_sem.at[i, k])
                if i == 2:
                    net.arrived(b.rb1[m][0].at[from_tile(o0, tiles)], b.s1_sem.at[0, k])
                if i == 3:
                    net.arrived(b.rb1[m][1].at[r], b.s1_sem.at[1, k])
                    net.arrived(b.rb2[m].at[r], b.s2_sem.at[k])

            when(c2, ready)
        for l, c2 in started[j]:
            when(c2, l.wait)
        load(j + 1)
        if i == 2:
            srcs += [(b.rb1[m][0], o0)]
        if i == 3:
            srcs += [(b.rb1[m][1], o), (b.rb2[m], o)]

        def put(i_, t):
            buf[from_tile(o + i_, 1), :] = t.astype(BF)

        add(srcs, put, cnt)
        if i < 3:
            dst = b.rb1[m][i] if i < 2 else b.rb2[m]
            sem = b.s1_sem.at[i, k] if i < 2 else b.s2_sem.at[k]
            target = net.tX if (i < 2) == (h == 0) else net.tY
            b.before(target is net.tX, i)
            net.slot()
            for tiles, c2 in sizes(n, s, 2):
                net.send(buf.at[from_tile(o, tiles)], dst.at[from_tile(o0 if i == 0 else o, tiles)], sem, target, c2)

    def block(m, zz):
        n = MATS[m][0]
        s0 = ((y * 2 + x) * 2 + c) * 4
        return s0 + zz, tile_at(n, s0 + zz) - tile_at(n, s0), tile_at(n, s0 + zz + 1) - tile_at(n, s0 + zz)

    def z_place(m, zz, d, to, o):
        return (b.last[m], 0) if d == 1 and zz == to else (b.rbz[m], o)

    def from_z(m, s, zz, d, to, o):
        ref, t0 = z_place(m, zz, d, to, o)
        for tiles, c2 in sizes(MATS[m][0], s, 1):
            when(c2, lambda: net.arrived(ref.at[from_tile(t0, tiles)], b.z_sem.at[d, zz, m]))
        return ref, t0

    def hop(p, zz, d, at, comes):
        m = p[0]
        s, o, cnt = block(m, zz)
        buf = b.rbc[m](y * 2 + x)
        cond = z == at
        if comes:

            @pl.when(cond)
            def _():
                got = from_z(m, s, zz, d, at, o)

                def put(i, t):
                    buf[from_tile(o + i, 1), :] = t.astype(BF)

                add([(buf, o), got], put, cnt)

        b.before_z(d)
        net.slot()
        for tiles, c2 in sizes(MATS[m][0], s, 1):
            ref, t0 = z_place(m, zz, d, (at + 1, at - 1)[d], o)
            net.send(
                buf.at[from_tile(o, tiles)], ref.at[from_tile(t0, tiles)], b.z_sem.at[d, zz, m],
                (net.tU, net.tD)[d], both(cond, c2),
            )

    def st_hop(p, h):
        for zz in (2 * p[1], 2 * p[1] + 1):
            if zz > h:
                hop(p, zz, 0, h, h > 0)
            if zz < 3 - h:
                hop(p, zz, 1, 3 - h, h > 0)

    def st_last(p):
        m, h = p
        n = MATS[m][0]

        for zz in (2 * h, 2 * h + 1):
            s, o, cnt = block(m, zz)

            @pl.when(z == zz)
            def _():
                srcs = [(b.rbc[m](y * 2 + x), o)]
                for d in (0, 1):
                    if (zz > 0, zz < 3)[d]:
                        srcs.append(from_z(m, s, zz, d, zz, o))

                def put(i, t):
                    b.res[m][from_tile(i + 1, 1), :] = t

                add(srcs, put, cnt)
        if h == 1:
            cnt = tile_at(n, me + 1) - tile_at(n, me)
            net.slot()
            net.send(b.res[m].at[from_tile(cnt, 1)], b.tail[m], b.t_sem.at[m], net.tN, me < 31)

    ev = []
    for k, p in enumerate(pieces):

        def a(t, f, *ar):
            ev.append((time(k, t), k, f, (p,) + ar))

        a(0, st_start)
        a(1, unit, 0)
        a(1.3, unit, 1)
        a(2, unit, 2)
        a(3, unit, 3)
        for h in (0, 1, 2):
            a(3.1 + h, st_hop, h)
        a(6, st_last)
    ev.sort(key=lambda e: (e[0], e[1]))
    units.extend((e[3][0], e[3][1]) for e in ev if e[2] is unit)
    return [(e[0], e[1], functools.partial(e[2], *e[3])) for e in ev]


def finish_sum(net, m, b, out_h, sem):
    n, L, _ = MATS[m]
    o = tile_at(n, net.me) * T16 - n * net.me
    res = b.res[m]
    pl.when(net.me > 0)(lambda: net.arrived(b.tail[m], b.t_sem.at[m]))
    res[0:T16, :] = b.tail[m][...]
    size = T16 + most(n, 1)
    v = pltpu.roll(res[0:size, :], lax.rem(size - (T16 - o), size), axis=0)
    keep = -(-n // 8) * 8
    res[0:keep, :] = v[0:keep]
    l = pltpu.make_async_copy(res.at[pl.ds(0, keep)], out_h, sem)
    l.start()
    return l


class Buffers:
    pass


def interleave(gen, events, now=0.0):
    events = list(events)

    def pop(until):
        while events and until(events[0]):
            events.pop(0)[2]()

    pop(lambda e: e[0] <= now)
    for step in gen:
        if isinstance(step, tuple):
            m = step[1]
            while any(e[1] == m for e in events):
                now = max(now, events[0][0])
                events.pop(0)[2]()
            step[2](m)
        else:
            now += step
            pop(lambda e: e[0] <= now)
    pop(lambda e: True)


def step_kernel(*refs):
    r = refs
    (tok_h, cot_h, ids_ref, ge_ref, gd_ref), inp = r[0:5], r[5:11]
    out_h, tg_h, small_out = r[11:14]
    grad_h, fin_h = r[14:20], r[20:26]
    (wie, wce, woe, wid, wcd, wod, tbuf, gyd, mid, ue, ve, ud, vd, a1e, a1d, a2e, a2d, a3e, a3d, ape, apd, idp, lk, big,
     st8, st16, tgb, acc1, acc2, accb, small_ref, zdi, zdc, zdo, sgd, sgo, tl8, tl16, sm_r,
     send_sem, recv_sem, n_sem, l_sem, in_sem, h_sem, h_recv, g_sem, o_sem, hs_sem, rdy,
     c_sem, s1_sem, s2_sem, z_sem, t_sem, r_sem, sm_sem, f_sem) = r[26:]
    net = Net(send_sem)
    z, y, x = net.z, net.y, net.x
    weights = (wie, wce, woe, wid, wcd, wod)
    load_c = [pltpu.make_async_copy(cot_h.at[i], tbuf.at[:, pl.ds(i * LEN_, LEN_)], in_sem.at[i]) for i in (0, 1)]
    load_t = [pltpu.make_async_copy(tok_h.at[i], tbuf.at[:, pl.ds(i * LEN_, LEN_)], in_sem.at[i]) for i in (0, 1)]
    load_i = pltpu.make_async_copy(ids_ref, idp.at[:, pl.ds(16, LEN_)], in_sem.at[2])
    load_i.start()
    for l in load_c:
        l.start()
    net.greet()

    own = [st8.at[0, pl.ds(0, 64)], st8.at[0, pl.ds(64, 128)], st16.at[0, pl.ds(0, 32)],
           st8.at[0, pl.ds(192, 64)], st8.at[1, pl.ds(0, 80)], st16.at[0, pl.ds(32, 32)]]
    nxt = [st8.at[1, pl.ds(80, 16)], st8.at[1, pl.ds(96, 16)], st16.at[1, pl.ds(0, 16)],
           st8.at[1, pl.ds(112, 16)], st8.at[1, pl.ds(128, 16)], st16.at[1, pl.ds(16, 16)]]
    g_events, g_rest = gather_events(
        net, inp, weights, own, nxt, big, recv_sem, n_sem, l_sem, lambda m, t: GATHER_TIME(m, t)
    )

    def halo(k, buf, lead, reach, up, fill):
        if up:
            src, dst = buf.at[:, pl.ds(lead + LEN_ - reach, reach)], buf.at[:, pl.ds(lead - reach, reach)]
            target, can, arrives = net.tU, net.has_up, net.has_down
        else:
            src, dst = buf.at[:, pl.ds(lead, reach)], buf.at[:, pl.ds(lead + LEN_, reach)]
            target, can, arrives = net.tD, net.has_down, net.has_up
        d = pltpu.make_async_remote_copy(
            src_ref=src, dst_ref=dst, send_sem=h_sem.at[k], recv_sem=h_recv.at[k], device_id=target, device_id_type=MESH
        )
        pl.when(can)(d.start)

        @pl.when(jnp.logical_not(arrives))
        def _():
            dst[...] = jnp.full(dst.shape, fill, buf.dtype)

        return d, can, arrives

    def halo_wait(hs):
        for d, can, arrives in hs:
            pl.when(arrives)(d.wait_recv)
            pl.when(can)(d.wait_send)

    def first_norm(x_of, par, a):
        def body(r):
            n, _ = norm_of(x_of(r, 128))
            h = n * par[0:1, :] + par[1:2, :]
            a[pl.ds(r, 128), :] = (h * sigmoid(h)).astype(BF)

        row_loop(128, body)

    def mid_norm(u, par, row, put):
        def body(r):
            n, _ = norm_of(u[pl.ds(r, 128), :])
            h = n * par[row : row + 1, 0:N_] + par[row + 1 : row + 2, 0:N_]
            put(r, 128, (h * sigmoid(h)).astype(BF))

        row_loop(128, body)

    def into(buf, lead):
        def put(r, n, v):
            m = r // LEN_
            buf[m, pl.ds(pl.multiple_of(r - m * LEN_ + lead, 8), n), :] = v.astype(buf.dtype)

        return put

    def stack(buf, lead, offsets):
        def it(m, _):
            rows = pl.ds(pl.multiple_of(m * LEN_, LEN_), LEN_)
            mine = idp[m, 16 : 16 + LEN_, :]
            for k, o in enumerate(offsets):
                same = idp[m, 16 + o : 16 + o + LEN_, :] == mine
                for c0, cn in lane_tiles(N_):
                    v = buf[m, lead + o : lead + o + LEN_, c0 : c0 + cn]
                    lk[k, rows, c0 : c0 + cn] = jnp.where(same[:, :cn], v, 0.0).astype(BF)
            return 0

        lax.fori_loop(0, 2, it, 0)

    def tok_rows(r, n):
        return jnp.concatenate(
            [jnp.transpose(tbuf[c0 : c0 + cn, pl.ds(r, n)].astype(F32)) for c0, cn in lane_tiles(W)], axis=1
        )

    def mid_rows(r, n):
        return mid[pl.ds(r, n), :]

    def forward(x_of, par, a1, a2, a3, w, u, v, ap, lead, offsets, hal, base, put_out):
        wi, wc, wo = w
        first_norm(x_of, par, a1)
        yield 3.0
        yield ("need", base, g_rest)
        for c0, cn in steps(N_, 256):
            u[:, c0 : c0 + cn] = jnp.dot(a1[...], wi[:, c0 : c0 + cn], preferred_element_type=F32)
            yield 0.7

        def put2(r, n, val):
            a2[pl.ds(r, n), :] = val
            into(ap, lead)(r, n, val)

        mid_norm(u, par, 3, put2)
        hs = hal()
        yield 2.0
        halo_wait(hs)
        stack(ap, lead, offsets)
        yield 1.5
        yield ("need", base + 1, g_rest)
        for c0, cn in steps(N_, 256):
            t = None
            for k in range(len(offsets)):
                d = jnp.dot(lk[k], wc[k * N_ : (k + 1) * N_, c0 : c0 + cn], preferred_element_type=F32)
                t = d if t is None else t + d
            v[:, c0 : c0 + cn] = t
            yield 1.5

        def put3(r, n, val):
            a3[pl.ds(r, n), :] = val

        mid_norm(v, par, 5, put3)
        yield 1.5
        yield ("need", base + 2, g_rest)
        for c0, cn in steps(W, 256):
            put_out(jnp.dot(a3[...], wo[:, c0 : c0 + cn], preferred_element_type=F32) + par[2:3, c0 : c0 + cn], c0, cn)
            yield 0.5

    used = [[], []]

    def wgrad(a, rhs, dst, row0):
        which = 1 if rhs.shape[-1] == W else 0
        st = (st8, st16)[which]
        for c0, cn in steps(a.shape[1], st.shape[1]):
            log = used[which]
            slot = len(log) % 2
            if len(log) >= 2:
                log[-2].wait()
            c = pltpu.make_async_copy(
                st.at[slot, pl.ds(0, cn)], dst.at[pl.ds(row0 + c0, cn)], g_sem.at[which, slot]
            )
            st[slot, 0:cn, :] = lax.dot_general(
                a[:, c0 : c0 + cn], rhs, COL_COL, preferred_element_type=F32
            ).astype(BF)
            c.start()
            log.append(c)
            yield 0.4 if which == 0 else 0.3

    def drain():
        for log in used:
            for c in log[-2:]:
                c.wait()
            log.clear()

    def back_norm(src, par, row, accum, width, emit, step):
        accum[...] = jnp.zeros_like(accum)

        def body(r):
            n, f = norm_of(src(r, step))
            g = par[row : row + 1, 0:width]
            h = n * g + par[row + 1 : row + 2, 0:width]
            gh = big[pl.ds(r, step), 0:width] * slope(h)
            accum[0] += fold8(gh * n)
            accum[1] += fold8(gh)
            p = gh * g
            m1 = jnp.mean(p, axis=-1, keepdims=True)
            m2 = jnp.mean(p * n, axis=-1, keepdims=True)
            emit(r, step, f * (p - m1 - n * m2))

        row_loop(step, body)

    def small(row, acc, width):
        small_ref[row : row + 1, 0:width] = jnp.sum(acc[0], axis=0, keepdims=True)
        small_ref[row + 1 : row + 2, 0:width] = jnp.sum(acc[1], axis=0, keepdims=True)

    def backward(gy, par, sb, x_of, a1, a2, a3, w, u, v, gp, lead, offsets, hal, g, emit):
        wi, wc, wo = w
        gi, gc, go = g
        accb[...] = jnp.zeros_like(accb)

        def bsum(r):
            accb[...] += fold8(gy[pl.ds(r, 64), :].astype(F32))

        row_loop(64, bsum)
        small_ref[sb + 2 : sb + 3, :] = jnp.sum(accb[...], axis=0, keepdims=True)
        yield 0.5
        for c0, cn in steps(N_, 256):
            big[:, c0 : c0 + cn] = lax.dot_general(gy[...], wo[c0 : c0 + cn, :], ROW_ROW, preferred_element_type=F32)
            yield 0.7
        yield from wgrad(a3, gy[...], go, 0)
        put = into(gp, lead)
        back_norm(
            lambda r, n: v[pl.ds(r, n), :], par, 5, acc2, N_, lambda r, n, val: put(r, n, val.astype(BF)), 128
        )
        hs = hal()
        small(sb + 5, acc2, N_)
        yield 2.5
        halo_wait(hs)
        stack(gp, lead, [-o for o in offsets])
        yield 1.5
        for k in range(len(offsets)):
            yield from wgrad(a2, lk[k], gc, k * N_)
        for c0, cn in steps(N_, 256):
            t = None
            for k in range(len(offsets)):
                d = lax.dot_general(
                    lk[k], wc[k * N_ + c0 : k * N_ + c0 + cn, :], ROW_ROW, preferred_element_type=F32
                )
                t = d if t is None else t + d
            big[:, c0 : c0 + cn] = t
            yield 1.5
        gub = a3

        def put2(r, n, val):
            gub[pl.ds(r, n), :] = val.astype(BF)

        back_norm(lambda r, n: u[pl.ds(r, n), :], par, 3, acc2, N_, put2, 128)
        small(sb + 3, acc2, N_)
        yield 2.5
        yield from wgrad(a1, gub[...], gi, 0)
        for c0, cn in steps(W, 256):
            big[:, c0 : c0 + cn] = lax.dot_general(
                gub[...], wi[c0 : c0 + cn, :], ROW_ROW, preferred_element_type=F32
            )
            yield 0.5
        back_norm(x_of, par, 0, acc1, W, emit, 64)
        small(sb, acc1, W)
        yield 4.5

    def turn(r):
        for c0, cn in lane_tiles(W):
            gyd[pl.ds(r, 128), c0 : c0 + cn] = jnp.transpose(tbuf[c0 : c0 + cn, pl.ds(r, 128)].astype(F32)).astype(BF)

    def network():
        for l in load_c:
            l.wait()

        row_loop(128, turn)
        for l in load_t:
            l.start()
        load_i.wait()
        h_ids = [halo(0, idp, 16, 16, True, -1), halo(1, idp, 16, 16, False, -1)]
        for l in load_t:
            l.wait()
        halo_wait(h_ids)

        def out_e(t, c0, cn):
            for d0, dn in lane_tiles(cn):
                own_t = jnp.transpose(tbuf[c0 + d0 : c0 + d0 + dn, :].astype(F32))
                mid[:, c0 + d0 : c0 + d0 + dn] = own_t + t[:, d0 : d0 + dn]

        yield from forward(
            tok_rows, ge_ref, a1e, a2e, a3e, weights[0:3], ue, ve, ape, 8, ENC_OFF,
            lambda: [halo(2, ape, 8, 8, True, 0), halo(3, ape, 8, 8, False, 0)], 0, out_e,
        )
        copies = []

        def out_d(t, c0, cn):
            v = mid[:, c0 : c0 + cn] + t
            for d0, dn in lane_tiles(cn):
                tbuf[c0 + d0 : c0 + d0 + dn, :] = jnp.transpose(v[:, d0 : d0 + dn]).astype(BF)

        yield from forward(
            mid_rows, gd_ref, a1d, a2d, a3d, weights[3:6], ud, vd, apd, 16, DEC_OFF,
            lambda: [halo(4, apd, 16, 16, True, 0)], 3, out_d,
        )

    interleave(network(), g_events)
    net.finish()
    out_copies = [
        pltpu.make_async_copy(tbuf.at[:, pl.ds(i * LEN_, LEN_)], out_h.at[i], o_sem.at[i]) for i in (0, 1)
    ]
    for l in out_copies:
        l.start()
    pl.when(net.has_up)(lambda: pl.semaphore_signal(hs_sem, inc=1, device_id=net.tU, device_id_type=MESH))
    small_ref[...] = jnp.zeros_like(small_ref)

    def emit_mid(r, n, val):
        t = gyd[pl.ds(r, n), :].astype(F32) + val
        mid[pl.ds(r, n), :] = t
        a1d[pl.ds(r, n), :] = t.astype(BF)

    for _ in backward(
        gyd, gd_ref, 8, mid_rows, a1d, a2d, a3d, weights[3:6], ud, vd, ape, 0, DEC_OFF,
        lambda: [halo(5, ape, 0, 16, False, 0)], grad_h[3:6], emit_mid,
    ):
        pass
    drain()
    for l in out_copies:
        l.wait()
    for l in load_t:
        l.start()

    def pool(ref, base, rows):
        return lambda k: ref.at[pl.ds(pl.multiple_of(base + k * rows, T16), rows)]

    def split(ref, at, rows):
        return ref.at[pl.ds(0, at)], ref.at[pl.ds(at, rows)]

    def buffers(mats, homes, zbuf, stages, res, tails, first):
        b = Buffers()
        b.rbc, b.rb1, b.rb2, b.rbz, b.last, b.res, b.tail = {}, {}, {}, {}, {}, {}, {}
        for i, m in enumerate(mats):
            rows = most(MATS[m][0], 4)
            b.rbc[m] = pool(homes[i], 0, rows)
            b.rb1[m] = [homes[i].at[pl.ds(6 * rows, 2 * most(MATS[m][0], 2))], homes[i].at[pl.ds(4 * rows, rows)]]
            b.rb2[m] = homes[i].at[pl.ds(5 * rows, rows)]
            b.rbz[m], b.last[m] = zbuf[i]
            b.res[m], b.tail[m] = res[i], tails[i]
        b.stage = lambda m: stages[1] if MATS[m][1] == W else stages[0]
        b.c_sem, b.s1_sem, b.s2_sem = c_sem.at[first], s1_sem.at[first], s2_sem.at[first]
        b.z_sem, b.t_sem, b.local_sem = z_sem, t_sem, r_sem
        asked = set()

        def once(i, cond=None):
            if i not in asked:
                asked.add(i)
                when(cond, lambda: pl.semaphore_wait(rdy.at[first, i], 1))

        b.once = once
        b.before = lambda is_x, i: once(1 if is_x else 2)
        b.before_z = (lambda d: once(3 + d, (net.has_up, net.has_down)[d])) if first else (lambda d: None)
        return b

    def ready(first):
        for i, t in enumerate((net.tC, net.tX, net.tY)):
            pl.semaphore_signal(rdy.at[first, i], inc=1, device_id=t, device_id_type=MESH)
        if first:
            pl.when(net.has_up)(lambda: pl.semaphore_signal(rdy.at[1, 4], inc=1, device_id=net.tU, device_id_type=MESH))
            pl.when(net.has_down)(lambda: pl.semaphore_signal(rdy.at[1, 3], inc=1, device_id=net.tD, device_id_type=MESH))

    bd = buffers(
        (3, 4, 5), (wid, wcd, wod), (split(zdi, 208, 64), split(zdc, 304, 80), split(zdo, 112, 32)), (sgd, sgo),
        (ud.at[pl.ds(0, 80)], ud.at[pl.ds(80, 96)], big.at[pl.ds(0, 48)]), (tl8.at[0], tl8.at[1], tl16.at[0]), 0,
    )
    d_events = sum_events(net, (4, 3, 5), grad_h, bd, SUM_TIME_D)
    late = [e for e in d_events if e[2].func.__name__ == "st_last" and e[2].args[0][0] == 5]
    d_events = [e for e in d_events if e not in late]

    def emit_tok(r, n, val):
        mid[pl.ds(r, n), :] = mid[pl.ds(r, n), :] + val

    def hal_e():
        pl.when(net.has_down)(lambda: pl.semaphore_wait(hs_sem, 1))
        return [halo(6, apd, 8, 8, True, 0), halo(7, apd, 8, 8, False, 0)]

    ready(0)
    bd.once(0)
    for l in load_t:
        l.wait()
    row_loop(128, turn)

    def token_rows(r, n):
        return gyd[pl.ds(r, n), :].astype(F32)

    interleave(
        backward(
            a1d, ge_ref, 0, token_rows, a1e, a2e, a3e, weights[0:3], ue, ve, apd, 8, ENC_OFF, hal_e, grad_h[0:3], emit_tok
        ),
        d_events,
    )
    drain()
    net.finish()
    ready(1)
    be = buffers(
        (0, 1, 2), (wie, wce, woe),
        (split(lk.at[0], 208, 64), (lk.at[1], lk.at[2, pl.ds(0, 128)]), split(a1d, 112, 32)),
        (lk.at[pl.ds(3, 2)], gyd2(gyd)),
        (vd.at[pl.ds(0, 80)], vd.at[pl.ds(80, 144)], big.at[pl.ds(48, 48)]), (tl8.at[2], tl8.at[3], tl16.at[1]), 1,
    )
    be.once(0)
    e_events = sum_events(net, (1, 2, 0), grad_h, be, SUM_TIME_E)

    def turn_out():
        log = []
        for c0, cn in lane_tiles(W):
            slot = len(log) % 2
            if len(log) >= 2:
                for l in log[-2]:
                    l.wait()
            tgb[slot, 0:cn, :] = jnp.transpose(mid[:, c0 : c0 + cn])
            ls = [
                pltpu.make_async_copy(
                    tgb.at[slot, pl.ds(0, cn), pl.ds(i * LEN_, LEN_)], tg_h.at[i, pl.ds(c0, cn)], o_sem.at[2 * slot + i]
                )
                for i in (0, 1)
            ]
            for l in ls:
                l.start()
            log.append(ls)
            yield 0.3
        for ls in log[-2:]:
            for l in ls:
                l.wait()

    z_pair = [(net.dp, z + 1 - 2 * (z % 2)), (net.dp, (z + 2) % 4)]

    def small_sums():
        at = small_ref
        for i, target in enumerate([net.tC, net.tX, net.tY] + z_pair):
            net.slot()
            net.send(at, sm_r.at[i], sm_sem.at[i], target)
            yield 3.0
            net.arrived(sm_r.at[i], sm_sem.at[i])
            to = big.at[pl.ds(96 + 16 * i, 16)] if i < 4 else small_out
            to[...] = at[...] + sm_r[i]
            at = to

    def tail_work():
        s = small_sums()
        next(s)
        for cost in turn_out():
            yield cost
        for cost in s:
            yield cost

    for e in late:
        e_events.append((SUM_TIME_E(0, 0.5), 0, e[2]))
    e_events.sort(key=lambda e: e[0])
    interleave(tail_work(), e_events)
    net.finish()
    fin = []
    for m in (3, 4, 5, 0, 1, 2):
        fin.append(finish_sum(net, m, bd if m > 2 else be, fin_h[m], f_sem.at[m]))
    for l in fin:
        l.wait()


class gyd2:
    def __init__(self, ref):
        self.ref = ref

    @property
    def at(self):
        return self

    def __getitem__(self, i):
        if isinstance(i, tuple):
            slot, rows = i
            return self.ref.at[pl.ds(slot * 64 + rows.start, rows.size)]
        return self.ref.at[pl.ds(i * 64, 64)]


def GATHER_TIME(m, t):
    return t * 9.0 if m < 3 else 25.0 + t * 9.0


def SUM_TIME_D(k, t):
    return 3.0 * k + 6.0 * t


def SUM_TIME_E(k, t):
    return 4.0 * k + 5.0 * t


def step(tok, cot, ids, ge, gd, shards):
    V, D_, R_ = pltpu.VMEM, pltpu.SemaphoreType.DMA, pltpu.SemaphoreType.REGULAR
    any_, vm = pl.BlockSpec(memory_space=pl.ANY), pl.BlockSpec(memory_space=pltpu.VMEM)
    sd = jax.ShapeDtypeStruct
    wshape = [(n * 32, L) for n, L, _ in MATS]
    narrow, wide = V((ROWS, N_), F32), V((ROWS, W), BF)
    scratch = [V(s, BF) for s in wshape] + [V((W, ROWS), BF), wide, V((ROWS, W), F32)] + [narrow] * 4 + [wide] * 2
    scratch += [V((ROWS, N_), BF)] * 4 + [V((2, 272, N_), F32)] * 2 + [V((2, 288, 128), jnp.int32)]
    scratch += [V((5, ROWS, N_), BF), V((ROWS, W), F32), V((2, 256, N_), BF), V((2, 128, W), BF), V((2, 128, ROWS), F32)]
    scratch += [V((2, 8, W), F32), V((2, 8, N_), F32), V((8, W), F32), V((16, W), F32)]
    scratch += [V((272, N_), BF), V((384, N_), BF), V((144, W), BF)]
    scratch += [V((2, most(75, 2), N_), BF), V((2, 64, W), BF)]
    scratch += [V((4, T16, N_), F32), V((2, T16, W), F32), V((5, T16, W), F32)]
    scratch += [D_((520,)), D_((32, 6)), D_((6,)), D_((6,)), D_((3,)), D_((8,)), D_((8,)), D_((2, 2)), D_((4,)), R_, R_((2, 5))]
    scratch += [D_((2, 4, 6)), D_((2, 2, 6)), D_((2, 6)), D_((2, 4, 6)), D_((6,)), D_((2,)), D_((5,)), D_((6,))]
    pad = lambda n: -(-n // 8) * 8
    return pl.pallas_call(
        step_kernel,
        out_shape=[sd((2, W, LEN_), BF), sd((2, W, LEN_), F32), sd((16, W), F32)]
        + [sd(s, BF) for s in wshape] + [sd((pad(n), L), F32) for n, L, _ in MATS],
        in_specs=[any_] * 3 + [vm] * 8,
        out_specs=[any_, any_, vm] + [any_] * 12,
        scratch_shapes=scratch,
        compiler_params=pltpu.CompilerParams(collective_id=0, has_side_effects=True, vmem_limit_bytes=int(63.9 * 2**20)),
    )(tok, cot, ids, ge, gd, *shards)


def per_device(
    tokens, doc_ids, cotangent, enc_in, enc_conv, enc_out, enc_gain, enc_shift, enc_bias,
    dec_in, dec_conv, dec_out, dec_gain, dec_shift, dec_bias,
):
    flat = [enc_in, enc_conv, enc_out, dec_in, dec_conv, dec_out]
    size = lax.axis_size("dp"), lax.axis_size("seq"), tokens.shape
    if size != (8, 4, (2, 1, LEN_, W)):
        return any_mesh(
            tokens, doc_ids, cotangent, flat, (enc_gain, enc_shift, enc_bias), (dec_gain, dec_shift, dec_bias)
        )
    shards = [w.reshape(n, L) for w, (n, L, _) in zip(flat, MATS)]
    ids = jnp.broadcast_to(doc_ids.reshape(2, LEN_, 1), (2, LEN_, 128))
    res = step(
        jnp.swapaxes(tokens.reshape(2, LEN_, W), 1, 2), jnp.swapaxes(cotangent.reshape(2, LEN_, W), 1, 2), ids,
        table(enc_gain, enc_shift, enc_bias), table(dec_gain, dec_shift, dec_bias), shards,
    )
    s, w = res[2], [g[:n].reshape(-1) for g, (n, _, _) in zip(res[9:], MATS)]
    e, d = untable(s[0:8]), untable(s[8:16])
    output, token_grad = (jnp.swapaxes(v, 1, 2).reshape(tokens.shape) for v in res[0:2])
    return (output, token_grad, w[0], w[1], w[2], *e, w[3], w[4], w[5], *d)


def table(gain, shift, bias):
    def wide(v): return jnp.pad(v, (0, W - v.shape[0]))
    one, two, three = slice(0, W), slice(W, W + N_), slice(W + N_, W + 2 * N_)
    rows = [gain[one], shift[one], bias, wide(gain[two]), wide(shift[two]), wide(gain[three]), wide(shift[three]), jnp.zeros((W,), F32)]
    return jnp.stack(rows)


def untable(s):
    gain = jnp.concatenate([s[0], s[3, :N_], s[5, :N_]])
    shift = jnp.concatenate([s[1], s[4, :N_], s[6, :N_]])
    return gain, shift, s[2]


def any_mesh(tokens, doc_ids, cotangent, flat, enc_small, dec_small):
    micro_count, seqs_here, length, wide_dim = tokens.shape
    count = micro_count * seqs_here
    lead = max(ENCODER_SPACING * ((ENCODER_TAPS - 1) // 2), DECODER_SPACING * (DECODER_TAPS - 1))
    seg_pad = extended(doc_ids.reshape(count, length), (("seq", 1),), lead)
    whole = [lax.all_gather(w, ("dp", "seq"), axis=0, tiled=True) for w in flat]
    enc, dec = [
        (whole[i].reshape(D2, D), whole[i + 1].reshape(-1, D), whole[i + 2].reshape(D, D2)) for i in (0, 3)
    ]
    rows = tokens.astype(jnp.float32).reshape(count, length, wide_dim)
    middle, enc_kept = block_forward(rows, seg_pad, lead, enc, *enc_small, False)
    final_rows, dec_kept = block_forward(middle, seg_pad, lead, dec, *dec_small, True)
    output = final_rows.astype(jnp.bfloat16).reshape(tokens.shape)
    grad_final = cotangent.astype(jnp.float32).reshape(-1, wide_dim)
    grad_middle, dec_w, dec_s = block_backward(
        grad_final, dec_kept, seg_pad, lead, dec, dec_small[0], True, count, length
    )
    grad_start, enc_w, enc_s = block_backward(
        grad_middle, enc_kept, seg_pad, lead, enc, enc_small[0], False, count, length
    )
    w = [lax.psum_scatter(g.reshape(-1), ("dp", "seq"), scatter_dimension=0, tiled=True) for g in enc_w + dec_w]
    s = lax.psum(enc_s + dec_s, ("dp", "seq"))
    return (
        output, grad_start.reshape(tokens.shape), w[0], w[1], w[2], s[0], s[1], s[2],
        w[3], w[4], w[5], s[3], s[4], s[5],
    )


def solution(mesh):
    placed = (
        P(None, "dp", "seq", None),
        P(None, "dp", "seq"),
        P(None, "dp", "seq", None),
        P(("dp", "seq")),
        P(("dp", "seq")),
        P(("dp", "seq")),
        P(),
        P(),
        P(),
        P(("dp", "seq")),
        P(("dp", "seq")),
        P(("dp", "seq")),
        P(),
        P(),
        P(),
    )
    return jax.shard_map(
        per_device,
        mesh=mesh,
        in_specs=placed,
        out_specs=(
            P(None, "dp", "seq", None),
            P(None, "dp", "seq", None),
            P(("dp", "seq")),
            P(("dp", "seq")),
            P(("dp", "seq")),
            P(),
            P(),
            P(),
            P(("dp", "seq")),
            P(("dp", "seq")),
            P(("dp", "seq")),
            P(),
            P(),
            P(),
        ),
        check_vma=False,
    )
```

```python
import functools

import jax
import jax.numpy as jnp
from jax import lax
from jax.experimental import pallas as pl
from jax.experimental.pallas import tpu as pltpu
from jax.sharding import PartitionSpec as P

MESH = pl.DeviceIdType.MESH
D2 = 1600
D = 800
ENCODER_TAPS = 5
ENCODER_SPACING = 4
DECODER_TAPS = 3
DECODER_SPACING = 8


epsilon = 1e-05


def from_behind(value, axis, by):
    length = lax.axis_size(axis)
    pairs = [(i, i + by) for i in range(length) if 0 <= i + by < length]
    return lax.ppermute(value, axis, pairs)


def extended(value, sides, width):
    for axis, dim in sides:
        size, length = (lax.axis_size(axis), value.shape[dim])
        up = [(i, (i + 1) % size) for i in range(size - 1)]
        down = [(j, i) for i, j in up]
        last = lax.slice_in_dim(value, length - width, length, axis=dim)
        initial = lax.slice_in_dim(value, 0, width, axis=dim)
        before = lax.ppermute(last, axis, up)
        after = lax.ppermute(initial, axis, down)
        value = jnp.concatenate([before, value, after], axis=dim)
    return value


def normalize(values):
    centred = values - jnp.mean(values, axis=-1, keepdims=True)
    factor = lax.rsqrt(jnp.mean(centred * centred, axis=-1, keepdims=True) + epsilon)
    return (centred * factor, factor)


def silu_slope(hidden):
    sigma = jax.nn.sigmoid(hidden)
    return sigma * (1.0 + hidden * (1.0 - sigma))


def norm_back(grad_h, scale_row, normed, factor):
    scaled = grad_h * scale_row
    mean_one = jnp.mean(scaled, axis=-1, keepdims=True)
    mean_two = jnp.mean(scaled * normed, axis=-1, keepdims=True)
    grad_in = factor * (scaled - mean_one - normed * mean_two)
    return (grad_in, jnp.sum(grad_h * normed, axis=0), jnp.sum(grad_h, axis=0))


def tap_offsets(causal):
    if causal:
        return [
            DECODER_SPACING * (tap_position - DECODER_TAPS + 1)
            for tap_position in range(DECODER_TAPS)
        ]
    return [
        ENCODER_SPACING * (tap_position - (ENCODER_TAPS - 1) // 2)
        for tap_position in range(ENCODER_TAPS)
    ]


def stacked_taps(padded, lead_rows, seg_pad, segment_leading, shift_offsets, length):
    own_ids = seg_pad[:, segment_leading : segment_leading + length]
    pieces = []
    for offset in shift_offsets:
        shifted = padded[:, lead_rows + offset : lead_rows + offset + length]
        same_doc = (
            seg_pad[:, segment_leading + offset : segment_leading + offset + length] == own_ids
        )
        pieces.append(jnp.where(same_doc[:, :, None], shifted, jnp.zeros_like(shifted)))
    return jnp.concatenate(pieces, axis=-1)


def block_forward(
    inputs, seg_pad, segment_leading, weights, norm_gain, norm_shift, output_bias, causal
):
    input_weight, convolution_weight, output_weight = weights
    seqs_here, length, wide_dim = inputs.shape
    narrow = input_weight.shape[1]
    flat_rows = inputs.reshape(-1, wide_dim)
    normed_one, factor_one = normalize(flat_rows)
    hidden_one = normed_one * norm_gain[:wide_dim] + norm_shift[:wide_dim]
    act_first = jax.nn.silu(hidden_one).astype(jnp.bfloat16)
    narrowed_rows = jnp.dot(act_first, input_weight, preferred_element_type=jnp.float32)
    normed_two, factor_two = normalize(narrowed_rows)
    hidden_two = (
        normed_two * norm_gain[wide_dim : wide_dim + narrow]
        + norm_shift[wide_dim : wide_dim + narrow]
    )
    act_second = jax.nn.silu(hidden_two).astype(jnp.bfloat16).reshape(seqs_here, length, narrow)
    shift_offsets = tap_offsets(causal)
    reach_rows = max([abs(offset) for offset in shift_offsets])
    if causal:
        tail_rows = from_behind(act_second[:, length - reach_rows :], "seq", 1)
        padded = jnp.concatenate([tail_rows, act_second], axis=1)
    else:
        padded = extended(act_second, (("seq", 1),), reach_rows)
    stacked = stacked_taps(
        padded, reach_rows, seg_pad, segment_leading, shift_offsets, length
    ).reshape(flat_rows.shape[0], -1)
    convolved_output = jnp.dot(stacked, convolution_weight, preferred_element_type=jnp.float32)
    normed_three, factor_three = normalize(convolved_output)
    hidden_three = normed_three * norm_gain[wide_dim + narrow :] + norm_shift[wide_dim + narrow :]
    act_third = jax.nn.silu(hidden_three).astype(jnp.bfloat16)
    residual_branch = (
        jnp.dot(act_third, output_weight, preferred_element_type=jnp.float32) + output_bias
    )
    result = (flat_rows + residual_branch).reshape(inputs.shape)
    kept_state = (
        normed_one,
        factor_one,
        hidden_one,
        act_first,
        normed_two,
        factor_two,
        hidden_two,
        stacked,
        normed_three,
        factor_three,
        hidden_three,
        act_third,
    )
    return (result, kept_state)


def block_backward(
    grad_out, kept_state, seg_pad, segment_leading, weights, norm_gain, causal, seqs_here, length
):
    input_weight, convolution_weight, output_weight = weights
    (
        normed_one,
        factor_one,
        hidden_one,
        act_first,
        normed_two,
        factor_two,
        hidden_two,
        stacked,
        normed_three,
        factor_three,
        hidden_three,
        act_third,
    ) = kept_state
    wide_dim = input_weight.shape[0]
    narrow = input_weight.shape[1]
    grad_low = grad_out.astype(jnp.bfloat16)
    grad_bias = jnp.sum(grad_low.astype(jnp.float32), axis=0)
    grad_w_out = jnp.einsum("nc,nd->cd", act_third, grad_low, preferred_element_type=jnp.float32)
    grad_act = jnp.einsum("nd,cd->nc", grad_low, output_weight, preferred_element_type=jnp.float32)
    grad_act = grad_act * silu_slope(hidden_three)
    grad_conv_out, gain_three, shift_three = norm_back(
        grad_act, norm_gain[wide_dim + narrow :], normed_three, factor_three
    )
    grad_conv_low = grad_conv_out.astype(jnp.bfloat16)
    grad_w_conv = jnp.einsum(
        "nc,nd->cd", stacked, grad_conv_low, preferred_element_type=jnp.float32
    )
    shift_offsets = tap_offsets(causal)
    reach_rows = max([abs(offset) for offset in shift_offsets])
    grad_grid = grad_conv_low.reshape(seqs_here, length, narrow)
    if causal:
        head_rows = from_behind(grad_grid[:, :reach_rows], "seq", -1)
        padded = jnp.concatenate([grad_grid, head_rows], axis=1)
        lead_rows = 0
    else:
        padded = extended(grad_grid, (("seq", 1),), reach_rows)
        lead_rows = reach_rows
    back_stack = stacked_taps(
        padded, lead_rows, seg_pad, segment_leading, [-offset for offset in shift_offsets], length
    ).reshape(seqs_here * length, -1)
    grad_act = sum(
        lax.dot_general(
            back_stack[:, k * narrow : (k + 1) * narrow],
            convolution_weight[k * narrow : (k + 1) * narrow],
            (((1,), (1,)), ((), ())),
            preferred_element_type=jnp.float32,
        )
        for k in range(len(shift_offsets))
    )
    grad_act = grad_act * silu_slope(hidden_two)
    grad_narrow, gain_two, shift_two = norm_back(
        grad_act, norm_gain[wide_dim : wide_dim + narrow], normed_two, factor_two
    )
    grad_narrow_low = grad_narrow.astype(jnp.bfloat16)
    grad_w_in = jnp.einsum(
        "nc,nd->cd", act_first, grad_narrow_low, preferred_element_type=jnp.float32
    )
    grad_act = jnp.einsum(
        "nd,cd->nc", grad_narrow_low, input_weight, preferred_element_type=jnp.float32
    )
    grad_act = grad_act * silu_slope(hidden_one)
    grad_flat, gain_one, shift_one = norm_back(
        grad_act, norm_gain[:wide_dim], normed_one, factor_one
    )
    grad_input = grad_out + grad_flat
    grad_gain = jnp.concatenate([gain_one, gain_two, gain_three])
    grad_shift = jnp.concatenate([shift_one, shift_two, shift_three])
    return (
        grad_input,
        (grad_w_in, grad_w_conv, grad_w_out),
        (grad_gain, grad_shift, grad_bias),
    )


EPS = 1e-5
F32, BF = jnp.float32, jnp.bfloat16
W, N_ = 1600, 800
ROWS, LEN_ = 512, 256
T16 = 16
MATS = ((50, 800, False), (125, 800, True), (25, 1600, False), (50, 800, False), (75, 800, True), (25, 1600, False))
ENC_OFF = [ENCODER_SPACING * (k - 2) for k in range(ENCODER_TAPS)]
DEC_OFF = [DECODER_SPACING * (k - 2) for k in range(DECODER_TAPS)]
ROW_ROW = (((1,), (1,)), ((), ()))
COL_COL = (((0,), (0,)), ((), ()))


def tile_at(n, s):
    return (n * s + T16 - 1) // T16


def dev(y, x, c, z):
    return ((y * 2 + x) * 2 + c, z)


def shard(y, x, c, z):
    return ((y * 2 + x) * 2 + c) * 4 + z


def when(cond, f):
    if cond is None:
        f()
    else:
        pl.when(cond)(f)


def both(a, b):
    if a is None:
        return b
    return a if b is None else jnp.logical_and(a, b)


def sizes(n, s, units):
    f = (n * units) // T16
    if (n * units) % T16 == 0:
        return [(f, None)]
    cnt = tile_at(n, s + units) - tile_at(n, s)
    return [(f, cnt == f), (f + 1, cnt == f + 1)]


def most(n, units):
    return ((n * units) // T16 + 1) * T16


def from_tile(t, tiles):
    return pl.ds(pl.multiple_of(t * T16, T16), tiles * T16)


def lane_tiles(n):
    return [(i, min(128, n - i)) for i in range(0, n, 128)]


def steps(n, step):
    return [(i, min(step, n - i)) for i in range(0, n, step)]


def norm_of(v):
    c = v - jnp.mean(v, axis=-1, keepdims=True)
    r = lax.rsqrt(jnp.mean(c * c, axis=-1, keepdims=True) + EPS)
    return c * r, r


def sigmoid(h):
    return 1.0 / (1.0 + jnp.exp(-h))


def slope(h):
    s = sigmoid(h)
    return s * (1.0 + h * (1.0 - s))


def row_loop(step, body):
    def it(i, _):
        body(pl.multiple_of(i * step, step))
        return 0

    lax.fori_loop(0, ROWS // step, it, 0)


def fold8(v):
    return jnp.sum(v.reshape(v.shape[0] // 8, 8, v.shape[1]), axis=0)


class Net:
    def __init__(self, send_sem):
        dp, z = lax.axis_index("dp"), lax.axis_index("seq")
        y, x, c = dp // 4, (dp // 2) % 2, dp % 2
        self.dp, self.y, self.x, self.c, self.z = dp, y, x, c, z
        self.X, self.Y, self.C = 1 - x, 1 - y, 1 - c
        self.me = shard(y, x, c, z)
        self.has_up, self.has_down = z < 3, z > 0
        self.tX, self.tY, self.tC = dev(y, 1 - x, c, z), dev(1 - y, x, c, z), dev(y, x, 1 - c, z)
        self.tU, self.tD = (dp, jnp.minimum(z + 1, 3)), (dp, jnp.maximum(z - 1, 0))
        nxt, prv = jnp.minimum(self.me + 1, 31), jnp.maximum(self.me - 1, 0)
        self.tN, self.tP = (nxt // 4, nxt % 4), (prv // 4, prv % 4)
        self.send_sem, self.k, self.sent = send_sem, -1, []

    def greet(self):
        barrier = pltpu.get_barrier_semaphore()
        far_next = jnp.logical_and(self.z == 3, self.dp < 7)
        far_prev = jnp.logical_and(self.z == 0, self.dp > 0)
        peers = [(self.tX, None), (self.tY, None), (self.tC, None)]
        peers += [((self.dp, (self.z + i) % 4), None) for i in (1, 2, 3)]
        peers += [(self.tN, far_next), (self.tP, far_prev)]
        for d, cond in peers:
            when(cond, lambda d=d: pl.semaphore_signal(barrier, inc=1, device_id=d, device_id_type=MESH))
        pl.semaphore_wait(barrier, 6 + jnp.where(far_next, 1, 0) + jnp.where(far_prev, 1, 0))

    def slot(self):
        self.k += 1

    def send(self, src, dst, rsem, target, cond=None):
        d = pltpu.make_async_remote_copy(
            src_ref=src, dst_ref=dst, send_sem=self.send_sem.at[self.k], recv_sem=rsem,
            device_id=target, device_id_type=MESH,
        )
        self.sent.append((d, cond))
        when(cond, d.start)

    def arrived(self, dst, rsem):
        pltpu.make_async_remote_copy(
            src_ref=dst, dst_ref=dst, send_sem=self.send_sem.at[0], recv_sem=rsem,
            device_id=self.tC, device_id_type=MESH,
        ).wait_recv()

    def finish(self):
        for d, cond in self.sent:
            when(cond, d.wait_send)
        self.sent = []


def zorder(z, j):
    if j == 0:
        return [(z, None)]
    return [(jnp.clip(z - j, 0, 3), z - j >= 0), (jnp.clip(z + j, 0, 3), z + j <= 3)]


def gather_events(net, inp, out, own, nxt, head, ext, recv_sem, n_sem, local_sem, time):
    y, x, c, z, X, Y, C, me = net.y, net.x, net.c, net.z, net.X, net.Y, net.C, net.me
    pending = []

    def ask(mats):
        for m in mats:
            n, L, _ = MATS[m]
            for i in range(n):
                ext[m][i, 0:L] = inp[m][i * L : (i + 1) * L].astype(F32)
            head[m][...] = ext[m][0:T16, 0:L].astype(BF)
            net.slot()
            net.send(head[m], nxt[m], n_sem.at[m], net.tP, me > 0)

    def build(m):
        n, L, _ = MATS[m]
        tiles = n // T16 + 1
        pl.when(me < 31)(lambda: net.arrived(nxt[m], n_sem.at[m]))
        ext[m][n : n + T16, 0:L] = nxt[m][...].astype(F32)
        o = tile_at(n, me) * T16 - n * me
        size = -(-max(n + T16, 15 + tiles * T16) // 8) * 8
        v = pltpu.roll(ext[m][0:size, 0:L], lax.rem(size - o, size), axis=0)
        own[m][...] = v[0 : tiles * T16].astype(BF)

    def send(m, s, target, cond=None, mine=False):
        n = MATS[m][0]
        net.slot()
        for tiles, c2 in sizes(n, s, 1):
            r = from_tile(tile_at(n, s), tiles)
            src = own[m].at[pl.ds(0, tiles * T16)] if mine else out[m].at[r]
            net.send(src, out[m].at[r], recv_sem.at[s, m], target, both(cond, c2))

    def wait(m, s, cond=None):
        n = MATS[m][0]
        for tiles, c2 in sizes(n, s, 1):
            when(both(cond, c2), lambda: net.arrived(out[m].at[from_tile(tile_at(n, s), tiles)], recv_sem.at[s, m]))

    def first(m):
        return net.tX if MATS[m][2] else net.tY

    def second(m):
        return net.tY if MATS[m][2] else net.tX

    def st_own(m):
        build(m)
        send(m, me, first(m), None, True)
        send(m, me, net.tU, net.has_up, True)
        send(m, me, net.tD, net.has_down, True)
        send(m, me, second(m), None, True)
        send(m, me, net.tC, None, True)
        for tiles, c2 in sizes(MATS[m][0], me, 1):
            l = pltpu.make_async_copy(
                own[m].at[pl.ds(0, tiles * T16)], out[m].at[from_tile(tile_at(MATS[m][0], me), tiles)], local_sem.at[m]
            )
            pending.append((m, l, c2))
            when(c2, l.start)

    def st_z(m, d):
        for o, has, t, has_t in (
            (z - d, z - d >= 0, net.tU, net.has_up), (z + d, z + d <= 3, net.tD, net.has_down)
        ):
            s = shard(y, x, c, jnp.clip(o, 0, 3))
            wait(m, s, has)
            send(m, s, first(m), has)
            if d < 3:
                send(m, s, t, jnp.logical_and(has, has_t))
            send(m, s, second(m), has)
            send(m, s, net.tC, has)

    def st_f(m, j):
        yy, xx = (y, X) if MATS[m][2] else (Y, x)
        for o, cond in zorder(z, j):
            s = shard(yy, xx, c, o)
            wait(m, s, cond)
            send(m, s, second(m), cond)
            send(m, s, net.tC, cond)

    def st_s(m, j):
        yy, xx = (Y, x) if MATS[m][2] else (y, X)
        for o, cond in zorder(z, j):
            s = shard(yy, xx, c, o)
            wait(m, s, cond)
            send(m, s, net.tC, cond)

    def st_d(m, j):
        for o, cond in zorder(z, j):
            s = shard(Y, X, c, o)
            wait(m, s, cond)
            send(m, s, net.tC, cond)

    def rest(m):
        for q in range(16):
            wait(m, shard(q // 8, (q // 4) % 2, C, q % 4))
        for k, l, c2 in pending:
            if k == m:
                when(c2, l.wait)

    ev = [(-1.0, 0, lambda: ask((0, 1, 2))), (5.0, 3, lambda: ask((3, 4, 5)))]
    for m in range(len(MATS)):

        def add(t, f, *a):
            ev.append((time(m, t), m, functools.partial(f, m, *a)))

        add(0, st_own)
        for d in (1, 2, 3):
            add(d, st_z, d)
        for j in range(4):
            add(1.1 + j, st_f, j)
            add(1.2 + j, st_s, j)
            add(2.3 + j, st_d, j)
    return sorted(ev, key=lambda e: (e[0], e[1])), rest


def sum_events(net, mats, grads, b, time):
    y, x, c, z, X, Y, C, me = net.y, net.x, net.c, net.z, net.X, net.Y, net.C, net.me
    pieces = [(m, h) for m in mats for h in (0, 1)]

    def groups(p):
        return [(Y, X), (y, X), (Y, x), (y, x)] if p[1] == 0 else [(Y, X), (Y, x), (y, X), (y, x)]

    def span(p, yy, xx, cc):
        m, h = p
        n = MATS[m][0]
        s0 = ((yy * 2 + xx) * 2 + cc) * 4
        s = s0 + 2 * h
        return s, tile_at(n, s), tile_at(n, s) - tile_at(n, s0)

    def add(srcs, put, tiles):
        def body(i, _):
            t = None
            for ref, t0 in srcs:
                v = ref[from_tile(t0 + i, 1), :].astype(F32)
                t = v if t is None else t + v
            put(i, t)
            return 0

        lax.fori_loop(0, tiles, body, 0)

    units = []
    started = {}

    def load(j):
        if j >= len(units) or j in started:
            return
        p, i = units[j]
        m = p[0]
        n = MATS[m][0]
        s, t0, _ = span(p, *groups(p)[i], c)
        st = b.stage(m)
        started[j] = []
        for tiles, c2 in sizes(n, s, 2):
            l = pltpu.make_async_copy(
                grads[m].at[from_tile(t0, tiles)], st.at[j % 2, pl.ds(0, tiles * T16)], b.local_sem.at[j % 2]
            )
            started[j].append((l, c2))
            when(c2, l.start)

    def st_start(p):
        m = p[0]
        k = pieces.index(p)
        for i, (yy, xx) in enumerate(groups(p)):
            s, t0, o = span(p, yy, xx, C)
            b.once(0)
            net.slot()
            for tiles, c2 in sizes(MATS[m][0], s, 2):
                net.send(
                    grads[m].at[from_tile(t0, tiles)], b.rbc[m](yy * 2 + xx).at[from_tile(o, tiles)],
                    b.c_sem.at[i, k], net.tC, c2,
                )

    def unit(p, i):
        m, h = p
        k = pieces.index(p)
        n = MATS[m][0]
        yy, xx = groups(p)[i]
        q = yy * 2 + xx
        s, _, o = span(p, yy, xx, c)
        j = units.index((p, i))
        load(j)
        cnt = tile_at(n, s + 2) - tile_at(n, s)
        buf = b.rbc[m](q)
        srcs = [(b.stage(m).at[j % 2], 0), (buf, o)]
        o0 = h * (most(n, 2) // T16)
        for tiles, c2 in sizes(n, s, 2):

            def ready():
                r = from_tile(o, tiles)
                net.arrived(buf.at[r], b.c_sem.at[i, k])
                if i == 2:
                    net.arrived(b.rb1[m][0].at[from_tile(o0, tiles)], b.s1_sem.at[0, k])
                if i == 3:
                    net.arrived(b.rb1[m][1].at[r], b.s1_sem.at[1, k])
                    net.arrived(b.rb2[m].at[r], b.s2_sem.at[k])

            when(c2, ready)
        for l, c2 in started[j]:
            when(c2, l.wait)
        load(j + 1)
        if i == 2:
            srcs += [(b.rb1[m][0], o0)]
        if i == 3:
            srcs += [(b.rb1[m][1], o), (b.rb2[m], o)]

        def put(i_, t):
            buf[from_tile(o + i_, 1), :] = t.astype(BF)

        add(srcs, put, cnt)
        if i < 3:
            dst = b.rb1[m][i] if i < 2 else b.rb2[m]
            sem = b.s1_sem.at[i, k] if i < 2 else b.s2_sem.at[k]
            target = net.tX if (i < 2) == (h == 0) else net.tY
            b.once(1 if target is net.tX else 2)
            net.slot()
            for tiles, c2 in sizes(n, s, 2):
                net.send(buf.at[from_tile(o, tiles)], dst.at[from_tile(o0 if i == 0 else o, tiles)], sem, target, c2)

    def block(m, zz):
        n = MATS[m][0]
        s0 = ((y * 2 + x) * 2 + c) * 4
        return s0 + zz, tile_at(n, s0 + zz) - tile_at(n, s0), tile_at(n, s0 + zz + 1) - tile_at(n, s0 + zz)

    def z_place(m, zz, d, to, o):
        return (b.last[m], 0) if d == 1 and zz == to else (b.rbz[m], o)

    def from_z(m, s, zz, d, to, o):
        ref, t0 = z_place(m, zz, d, to, o)
        for tiles, c2 in sizes(MATS[m][0], s, 1):
            when(c2, lambda: net.arrived(ref.at[from_tile(t0, tiles)], b.z_sem.at[d, zz, m]))
        return ref, t0

    def hop(p, zz, d, at, comes):
        m = p[0]
        s, o, cnt = block(m, zz)
        buf = b.rbc[m](y * 2 + x)
        cond = z == at
        if comes:

            @pl.when(cond)
            def _():
                got = from_z(m, s, zz, d, at, o)

                def put(i, t):
                    buf[from_tile(o + i, 1), :] = t.astype(BF)

                add([(buf, o), got], put, cnt)

        b.before_z(d)
        net.slot()
        for tiles, c2 in sizes(MATS[m][0], s, 1):
            ref, t0 = z_place(m, zz, d, (at + 1, at - 1)[d], o)
            net.send(
                buf.at[from_tile(o, tiles)], ref.at[from_tile(t0, tiles)], b.z_sem.at[d, zz, m],
                (net.tU, net.tD)[d], both(cond, c2),
            )

    def st_hop(p, h):
        for zz in (2 * p[1], 2 * p[1] + 1):
            if zz > h:
                hop(p, zz, 0, h, h > 0)
            if zz < 3 - h:
                hop(p, zz, 1, 3 - h, h > 0)

    def st_last(p):
        m, h = p
        n = MATS[m][0]

        for zz in (2 * h, 2 * h + 1):
            s, o, cnt = block(m, zz)

            @pl.when(z == zz)
            def _():
                srcs = [(b.rbc[m](y * 2 + x), o)]
                for d in (0, 1):
                    if (zz > 0, zz < 3)[d]:
                        srcs.append(from_z(m, s, zz, d, zz, o))

                def put(i, t):
                    b.res[m][from_tile(i + 1, 1), :] = t

                add(srcs, put, cnt)
        if h == 1:
            cnt = tile_at(n, me + 1) - tile_at(n, me)
            net.slot()
            net.send(b.res[m].at[from_tile(cnt, 1)], b.tail[m], b.t_sem.at[m], net.tN, me < 31)

    ev = []
    for k, p in enumerate(pieces):

        def a(t, f, *ar):
            ev.append((time(k, t), k, f, (p,) + ar))

        a(0, st_start)
        a(1, unit, 0)
        a(1.3, unit, 1)
        a(2, unit, 2)
        a(3, unit, 3)
        for h in (0, 1, 2):
            a(3.1 + h, st_hop, h)
        a(6, st_last)
    ev.sort(key=lambda e: (e[0], e[1]))
    units.extend((e[3][0], e[3][1]) for e in ev if e[2] is unit)
    return [(e[0], e[1], functools.partial(e[2], *e[3])) for e in ev]


def finish_sum(net, m, b, out_h, sem):
    n, L, _ = MATS[m]
    o = tile_at(n, net.me) * T16 - n * net.me
    res = b.res[m]
    pl.when(net.me > 0)(lambda: net.arrived(b.tail[m], b.t_sem.at[m]))
    res[0:T16, :] = b.tail[m][...]
    size = T16 + most(n, 1)
    v = pltpu.roll(res[0:size, :], lax.rem(size - (T16 - o), size), axis=0)
    keep = -(-n // 8) * 8
    res[0:keep, :] = v[0:keep]
    l = pltpu.make_async_copy(res.at[pl.ds(0, keep)], out_h, sem)
    l.start()
    return l


class Buffers:
    pass


class Schedule:
    def __init__(self):
        self.now, self.events = 0.0, []

    def add(self, events):
        self.events += [(self.now + e[0],) + tuple(e[1:]) for e in events]
        self.events.sort(key=lambda e: (e[0], e[1]))
        self.pop(self.now)

    def pop(self, until):
        while self.events and self.events[0][0] <= until:
            self.events.pop(0)[2]()

    def run(self, gen):
        for step in gen:
            if not isinstance(step, tuple):
                self.now += step
                self.pop(self.now)
            elif step[0] == "call":
                step[1]()
            else:
                m = step[1]
                while any(e[1] == m for e in self.events):
                    e = self.events.pop(0)
                    self.now = max(self.now, e[0])
                    e[2]()
                step[2](m)


class Slots:
    def __init__(self, ref, base, rows):
        self.ref, self.base, self.rows, self.at = ref, base, rows, self

    def __getitem__(self, i):
        slot, rows = i if isinstance(i, tuple) else (i, None)
        first = self.base + slot * self.rows
        return self.ref.at[pl.ds(first, self.rows) if rows is None else pl.ds(first + rows.start, rows.size)]


def step_kernel(*refs):
    r = refs
    (tok_h, cot_h, ids_ref), small_in, inp = r[0:3], r[3:9], r[9:15]
    out_h, tg_h, small_outs = r[15], r[16], r[17:23]
    grad_h, fin_out = r[23:29], r[29:35]
    (wie, wce, woe, wid, wcd, wod, tbuf, gyd, mid, ue, ve, ud, vd, a1e, a1d, a2e, a2d, a3e, a3d, ape, apd, idp, lk, big,
     st8, st16, tgb, acc1, acc2, accb, small_ref, zdi, zdc, zdo, sgd, sgo, tl8, tl16, sm_r,
     send_sem, recv_sem, n_sem, l_sem, in_sem, h_sem, h_recv, g_sem, o_sem, hs_sem, rdy,
     c_sem, s1_sem, s2_sem, z_sem, t_sem, r_sem, sm_sem, f_sem, ge_ref, gd_ref) = r[35:]
    net = Net(send_sem)
    z, y, x = net.z, net.y, net.x
    weights = (wie, wce, woe, wid, wcd, wod)
    load_c = [pltpu.make_async_copy(cot_h.at[i], tbuf.at[:, pl.ds(i * LEN_, LEN_)], in_sem.at[i]) for i in (0, 1)]
    load_t = [pltpu.make_async_copy(tok_h.at[i], tbuf.at[:, pl.ds(i * LEN_, LEN_)], in_sem.at[i]) for i in (0, 1)]
    for par, (gain, shift, bias) in ((ge_ref, small_in[0:3]), (gd_ref, small_in[3:6])):
        par[0, :], par[1, :], par[2, :] = gain[0:W], shift[0:W], bias[...]
        for row, ref in ((3, gain), (4, shift)):
            par[row, 0:N_] = ref[W : W + N_]
            par[row + 2, 0:N_] = ref[W + N_ : W + 2 * N_]
    load_i = pltpu.make_async_copy(ids_ref, idp.at[:, pl.ds(16, LEN_)], in_sem.at[2])
    load_i.start()
    for l in load_c:
        l.start()
    net.greet()

    own = [st8.at[0, pl.ds(0, 64)], st8.at[0, pl.ds(64, 128)], st16.at[0, pl.ds(0, 32)],
           st8.at[0, pl.ds(192, 64)], st8.at[1, pl.ds(0, 80)], st16.at[0, pl.ds(32, 32)]]
    nxt = [st8.at[1, pl.ds(80, 16)], st8.at[1, pl.ds(96, 16)], st16.at[1, pl.ds(0, 16)],
           st8.at[1, pl.ds(112, 16)], st8.at[1, pl.ds(128, 16)], st16.at[1, pl.ds(16, 16)]]
    head = [st8.at[1, pl.ds(144, 16)], st8.at[1, pl.ds(160, 16)], st16.at[1, pl.ds(32, 16)],
            st8.at[1, pl.ds(176, 16)], st8.at[1, pl.ds(192, 16)], st16.at[1, pl.ds(48, 16)]]
    ext = [big.at[pl.ds(a, n)] for a, n in ((0, 80), (80, 144), (400, 48), (224, 80), (304, 96), (448, 48))]
    g_events, g_rest = gather_events(
        net, inp, weights, own, nxt, head, ext, recv_sem, n_sem, l_sem, lambda m, t: GATHER_TIME(m, t)
    )

    def halo(k, buf, lead, reach, up, fill):
        if up:
            src, dst = buf.at[:, pl.ds(lead + LEN_ - reach, reach)], buf.at[:, pl.ds(lead - reach, reach)]
            target, can, arrives = net.tU, net.has_up, net.has_down
        else:
            src, dst = buf.at[:, pl.ds(lead, reach)], buf.at[:, pl.ds(lead + LEN_, reach)]
            target, can, arrives = net.tD, net.has_down, net.has_up
        d = pltpu.make_async_remote_copy(
            src_ref=src, dst_ref=dst, send_sem=h_sem.at[k], recv_sem=h_recv.at[k], device_id=target, device_id_type=MESH
        )
        pl.when(can)(d.start)

        @pl.when(jnp.logical_not(arrives))
        def _():
            dst[...] = jnp.full(dst.shape, fill, buf.dtype)

        return d, can, arrives

    def halo_wait(hs):
        for d, can, arrives in hs:
            pl.when(arrives)(d.wait_recv)
            pl.when(can)(d.wait_send)

    def first_norm(x_of, par, a):
        def body(r):
            n, _ = norm_of(x_of(r, 128))
            h = n * par[0:1, :] + par[1:2, :]
            a[pl.ds(r, 128), :] = (h * sigmoid(h)).astype(BF)

        row_loop(128, body)

    def mid_norm(u, par, row, put):
        def body(r):
            n, _ = norm_of(u[pl.ds(r, 128), :])
            h = n * par[row : row + 1, 0:N_] + par[row + 1 : row + 2, 0:N_]
            put(r, 128, (h * sigmoid(h)).astype(BF))

        row_loop(128, body)

    def into(buf, lead):
        def put(r, n, v):
            m = r // LEN_
            buf[m, pl.ds(pl.multiple_of(r - m * LEN_ + lead, 8), n), :] = v.astype(buf.dtype)

        return put

    def stack(buf, lead, offsets):
        def it(m, _):
            rows = pl.ds(pl.multiple_of(m * LEN_, LEN_), LEN_)
            mine = idp[m, 16 : 16 + LEN_, :]
            for k, o in enumerate(offsets):
                same = idp[m, 16 + o : 16 + o + LEN_, :] == mine
                for c0, cn in lane_tiles(N_):
                    v = buf[m, lead + o : lead + o + LEN_, c0 : c0 + cn]
                    lk[k, rows, c0 : c0 + cn] = jnp.where(same[:, :cn], v, 0.0).astype(BF)
            return 0

        lax.fori_loop(0, 2, it, 0)

    def tok_rows(r, n):
        return jnp.concatenate(
            [jnp.transpose(tbuf[c0 : c0 + cn, pl.ds(r, n)].astype(F32)) for c0, cn in lane_tiles(W)], axis=1
        )

    def mid_rows(r, n):
        return mid[pl.ds(r, n), :]

    def forward(x_of, par, a1, a2, a3, w, u, v, ap, lead, offsets, hal, base, put_out):
        wi, wc, wo = w
        first_norm(x_of, par, a1)
        yield 3.0
        yield ("need", base, g_rest)
        for c0, cn in steps(N_, 256):
            u[:, c0 : c0 + cn] = jnp.dot(a1[...], wi[:, c0 : c0 + cn], preferred_element_type=F32)
            yield 0.7

        def put2(r, n, val):
            a2[pl.ds(r, n), :] = val
            into(ap, lead)(r, n, val)

        mid_norm(u, par, 3, put2)
        hs = hal()
        yield 2.0
        halo_wait(hs)
        stack(ap, lead, offsets)
        yield 1.5
        yield ("need", base + 1, g_rest)
        for c0, cn in steps(N_, 256):
            t = None
            for k in range(len(offsets)):
                d = jnp.dot(lk[k], wc[k * N_ : (k + 1) * N_, c0 : c0 + cn], preferred_element_type=F32)
                t = d if t is None else t + d
            v[:, c0 : c0 + cn] = t
            yield 1.5

        def put3(r, n, val):
            a3[pl.ds(r, n), :] = val

        mid_norm(v, par, 5, put3)
        yield 1.5
        yield ("need", base + 2, g_rest)
        for c0, cn in steps(W, 256):
            put_out(jnp.dot(a3[...], wo[:, c0 : c0 + cn], preferred_element_type=F32) + par[2:3, c0 : c0 + cn], c0, cn)
            yield 0.5

    used = [[], []]

    def wgrad(a, rhs, dst, row0):
        which = 1 if rhs.shape[-1] == W else 0
        st = (st8, st16)[which]
        for c0, cn in steps(a.shape[1], st.shape[1]):
            log = used[which]
            slot = len(log) % 2
            if len(log) >= 2:
                log[-2].wait()
            c = pltpu.make_async_copy(
                st.at[slot, pl.ds(0, cn)], dst.at[pl.ds(row0 + c0, cn)], g_sem.at[which, slot]
            )
            st[slot, 0:cn, :] = lax.dot_general(
                a[:, c0 : c0 + cn], rhs, COL_COL, preferred_element_type=F32
            ).astype(BF)
            c.start()
            log.append(c)
            yield 0.4 if which == 0 else 0.3

    def drain():
        for log in used:
            for c in log[-2:]:
                c.wait()
            log.clear()

    def back_norm(src, par, row, accum, width, emit, step):
        accum[...] = jnp.zeros_like(accum)

        def body(r):
            n, f = norm_of(src(r, step))
            g = par[row : row + 1, 0:width]
            h = n * g + par[row + 1 : row + 2, 0:width]
            gh = big[pl.ds(r, step), 0:width] * slope(h)
            accum[0] += fold8(gh * n)
            accum[1] += fold8(gh)
            p = gh * g
            m1 = jnp.mean(p, axis=-1, keepdims=True)
            m2 = jnp.mean(p * n, axis=-1, keepdims=True)
            emit(r, step, f * (p - m1 - n * m2))

        row_loop(step, body)

    def small(row, acc, width):
        small_ref[row : row + 1, 0:width] = jnp.sum(acc[0], axis=0, keepdims=True)
        small_ref[row + 1 : row + 2, 0:width] = jnp.sum(acc[1], axis=0, keepdims=True)

    def backward(gy, par, sb, x_of, a1, a2, a3, w, u, v, gp, lead, offsets, hal, g, emit, after_taps, after_in):
        wi, wc, wo = w
        gi, gc, go = g
        accb[...] = jnp.zeros_like(accb)

        def bsum(r):
            accb[...] += fold8(gy[pl.ds(r, 64), :].astype(F32))

        row_loop(64, bsum)
        small_ref[sb + 2 : sb + 3, :] = jnp.sum(accb[...], axis=0, keepdims=True)
        yield 0.5
        for c0, cn in steps(N_, 256):
            big[:, c0 : c0 + cn] = lax.dot_general(gy[...], wo[c0 : c0 + cn, :], ROW_ROW, preferred_element_type=F32)
            yield 0.7
        yield from wgrad(a3, gy[...], go, 0)
        put = into(gp, lead)
        back_norm(
            lambda r, n: v[pl.ds(r, n), :], par, 5, acc2, N_, lambda r, n, val: put(r, n, val.astype(BF)), 128
        )
        hs = hal()
        small(sb + 5, acc2, N_)
        yield 2.5
        halo_wait(hs)
        stack(gp, lead, [-o for o in offsets])
        yield 1.5
        for k in range(len(offsets)):
            yield from wgrad(a2, lk[k], gc, k * N_)
        for c0, cn in steps(N_, 256):
            t = None
            for k in range(len(offsets)):
                d = lax.dot_general(
                    lk[k], wc[k * N_ + c0 : k * N_ + c0 + cn, :], ROW_ROW, preferred_element_type=F32
                )
                t = d if t is None else t + d
            big[:, c0 : c0 + cn] = t
            yield 1.5
        yield ("call", after_taps)
        gub = a3

        def put2(r, n, val):
            gub[pl.ds(r, n), :] = val.astype(BF)

        back_norm(lambda r, n: u[pl.ds(r, n), :], par, 3, acc2, N_, put2, 128)
        small(sb + 3, acc2, N_)
        yield 2.5
        yield from wgrad(a1, gub[...], gi, 0)
        for c0, cn in steps(W, 256):
            big[:, c0 : c0 + cn] = lax.dot_general(
                gub[...], wi[c0 : c0 + cn, :], ROW_ROW, preferred_element_type=F32
            )
            yield 0.5
        yield ("call", after_in)
        back_norm(x_of, par, 0, acc1, W, emit, 64)
        small(sb, acc1, W)
        yield 4.5

    def turn(r):
        for c0, cn in lane_tiles(W):
            gyd[pl.ds(r, 128), c0 : c0 + cn] = jnp.transpose(tbuf[c0 : c0 + cn, pl.ds(r, 128)].astype(F32)).astype(BF)

    def network():
        for l in load_c:
            l.wait()

        row_loop(128, turn)
        for l in load_t:
            l.start()
        load_i.wait()
        h_ids = [halo(0, idp, 16, 16, True, -1), halo(1, idp, 16, 16, False, -1)]
        for l in load_t:
            l.wait()
        halo_wait(h_ids)

        def out_e(t, c0, cn):
            for d0, dn in lane_tiles(cn):
                own_t = jnp.transpose(tbuf[c0 + d0 : c0 + d0 + dn, :].astype(F32))
                mid[:, c0 + d0 : c0 + d0 + dn] = own_t + t[:, d0 : d0 + dn]

        yield from forward(
            tok_rows, ge_ref, a1e, a2e, a3e, weights[0:3], ue, ve, ape, 8, ENC_OFF,
            lambda: [halo(2, ape, 8, 8, True, 0), halo(3, ape, 8, 8, False, 0)], 0, out_e,
        )
        copies = []

        def out_d(t, c0, cn):
            v = mid[:, c0 : c0 + cn] + t
            for d0, dn in lane_tiles(cn):
                tbuf[c0 + d0 : c0 + d0 + dn, :] = jnp.transpose(v[:, d0 : d0 + dn]).astype(BF)

        yield from forward(
            mid_rows, gd_ref, a1d, a2d, a3d, weights[3:6], ud, vd, apd, 16, DEC_OFF,
            lambda: [halo(4, apd, 16, 16, True, 0)], 3, out_d,
        )

    todo = Schedule()
    todo.add(g_events)
    todo.run(network())
    todo.pop(1e9)
    net.finish()
    out_copies = [
        pltpu.make_async_copy(tbuf.at[:, pl.ds(i * LEN_, LEN_)], out_h.at[i], o_sem.at[i]) for i in (0, 1)
    ]
    for l in out_copies:
        l.start()
    pl.when(net.has_up)(lambda: pl.semaphore_signal(hs_sem, inc=1, device_id=net.tU, device_id_type=MESH))
    small_ref[...] = jnp.zeros_like(small_ref)

    def split(ref, at, rows):
        return ref.at[pl.ds(0, at)], ref.at[pl.ds(at, rows)]

    z_asked = set()
    late, all_b = [], {}

    def phase(i, mats, homes, zbuf, stages, res, tails, time):
        drain()
        for k, t in enumerate((net.tC, net.tX, net.tY)):
            pl.semaphore_signal(rdy.at[i, k], inc=1, device_id=t, device_id_type=MESH)
        if i == 2:
            pl.when(net.has_up)(lambda: pl.semaphore_signal(rdy.at[i, 4], inc=1, device_id=net.tU, device_id_type=MESH))
            pl.when(net.has_down)(lambda: pl.semaphore_signal(rdy.at[i, 3], inc=1, device_id=net.tD, device_id_type=MESH))
        b = Buffers()
        b.rbc, b.rb1, b.rb2, b.rbz, b.last, b.res, b.tail = {}, {}, {}, {}, {}, {}, {}
        for k, m in enumerate(mats):
            rows = most(MATS[m][0], 4)
            home = homes[k]
            b.rbc[m] = lambda q, home=home, rows=rows: home.at[pl.ds(pl.multiple_of(q * rows, T16), rows)]
            b.rb1[m] = [home.at[pl.ds(6 * rows, 2 * most(MATS[m][0], 2))], home.at[pl.ds(4 * rows, rows)]]
            b.rb2[m] = home.at[pl.ds(5 * rows, rows)]
            b.rbz[m], b.last[m] = zbuf[k]
            b.res[m], b.tail[m] = res[k], tails[k]
            all_b[m] = b
        b.stage = lambda m: stages[mats.index(m)]
        b.c_sem, b.s1_sem, b.s2_sem = c_sem.at[i], s1_sem.at[i], s2_sem.at[i]
        b.z_sem, b.t_sem, b.local_sem = z_sem, t_sem, r_sem.at[i]
        asked = set()

        def once(k):
            if k not in asked:
                asked.add(k)
                pl.semaphore_wait(rdy.at[i, k], 1)

        def before_z(d):
            said = (None, None, 2, 2)[i]
            if said is not None and (said, d) not in z_asked:
                z_asked.add((said, d))
                when((net.has_up, net.has_down)[d], lambda: pl.semaphore_wait(rdy.at[said, 3 + d], 1))

        b.once, b.before_z = once, before_z
        ev = []
        for e in sum_events(net, mats, grad_h, b, time):
            f = e[2]
            if f.func.__name__ == "st_last" and MATS[f.args[0][0]][1] == W:
                late.append(f)
            else:
                ev.append(e)
        todo.add(ev)

    def emit_mid(r, n, val):
        t = gyd[pl.ds(r, n), :].astype(F32) + val
        mid[pl.ds(r, n), :] = t
        a1d[pl.ds(r, n), :] = t.astype(BF)

    def emit_tok(r, n, val):
        mid[pl.ds(r, n), :] = mid[pl.ds(r, n), :] + val

    def token_rows(r, n):
        return gyd[pl.ds(r, n), :].astype(F32)

    def hal_e():
        pl.when(net.has_down)(lambda: pl.semaphore_wait(hs_sem, 1))
        return [halo(6, apd, 8, 8, True, 0), halo(7, apd, 8, 8, False, 0)]

    def back():
        yield from backward(
            gyd, gd_ref, 8, mid_rows, a1d, a2d, a3d, weights[3:6], ud, vd, ape, 0, DEC_OFF,
            lambda: [halo(5, ape, 0, 16, False, 0)], grad_h[3:6], emit_mid,
            lambda: phase(
                0, (4, 5), (wcd, wod), (split(zdc, 304, 80), split(zdo, 112, 32)), (sgd, sgo),
                (vd.at[pl.ds(80, 96)], big.at[pl.ds(0, 48)]), (tl8.at[1], tl16.at[0]), SUM_TIME[0],
            ),
            lambda: phase(
                1, (3,), (wid,), (split(zdi, 208, 64),), (Slots(wcd, 2144, 112),),
                (vd.at[pl.ds(0, 80)],), (tl8.at[0],), SUM_TIME[1],
            ),
        )
        for l in out_copies:
            l.wait()
        for l in load_t:
            l.start()
        for l in load_t:
            l.wait()
        row_loop(128, turn)
        yield 2.0
        yield from backward(
            a1d, ge_ref, 0, token_rows, a1e, a2e, a3e, weights[0:3], ue, ve, apd, 8, ENC_OFF, hal_e, grad_h[0:3], emit_tok,
            lambda: phase(
                2, (1, 2), (wce, woe), ((lk.at[1], lk.at[2, pl.ds(0, 128)]), split(a1d, 112, 32)),
                (lk.at[pl.ds(3, 2)], Slots(a1d, 144, 64)),
                (ve.at[pl.ds(80, 144)], big.at[pl.ds(48, 48)]), (tl8.at[3], tl16.at[1]), SUM_TIME[2],
            ),
            lambda: phase(
                3, (0,), (wie,), (split(lk.at[0], 208, 64),), (Slots(wce, 3584, 112),),
                (ve.at[pl.ds(0, 80)],), (tl8.at[2],), SUM_TIME[3],
            ),
        )

    todo.run(back())

    def turn_out():
        log = []
        for c0, cn in lane_tiles(W):
            slot = len(log) % 2
            if len(log) >= 2:
                for l in log[-2]:
                    l.wait()
            tgb[slot, 0:cn, :] = jnp.transpose(mid[:, c0 : c0 + cn])
            ls = [
                pltpu.make_async_copy(
                    tgb.at[slot, pl.ds(0, cn), pl.ds(i * LEN_, LEN_)], tg_h.at[i, pl.ds(c0, cn)], o_sem.at[2 * slot + i]
                )
                for i in (0, 1)
            ]
            for l in ls:
                l.start()
            log.append(ls)
            yield 0.3
        for ls in log[-2:]:
            for l in ls:
                l.wait()

    z_pair = [(net.dp, z + 1 - 2 * (z % 2)), (net.dp, (z + 2) % 4)]

    def small_sums():
        at = small_ref
        for i, target in enumerate([net.tC, net.tX, net.tY] + z_pair):
            net.slot()
            net.send(at, sm_r.at[i], sm_sem.at[i], target)
            yield 3.0
            net.arrived(sm_r.at[i], sm_sem.at[i])
            to = big.at[pl.ds(96 + 16 * i, 16)]
            to[...] = at[...] + sm_r[i]
            at = to
        for first, (gain, shift, bias) in ((0, small_outs[0:3]), (8, small_outs[3:6])):
            for row, ref in ((0, gain), (1, shift)):
                ref[0:W] = at[first + row, :]
                ref[W : W + N_] = at[first + row + 3, 0:N_]
                ref[W + N_ : W + 2 * N_] = at[first + row + 5, 0:N_]
            bias[...] = at[first + 2, :]

    def tail_work():
        s = small_sums()
        next(s)
        for cost in turn_out():
            yield cost
        for cost in s:
            yield cost

    todo.add([(1e8, 0, f) for f in late])
    todo.run(tail_work())
    todo.pop(1e9)
    net.finish()
    fin = []
    for m in (3, 4, 5, 0, 1, 2):
        fin.append(finish_sum(net, m, all_b[m], fin_out[m], f_sem.at[m]))
    for l in fin:
        l.wait()


def GATHER_TIME(m, t):
    return t * 9.0 if m < 3 else 45.0 + t * 9.0


SUM_TIME = (
    lambda k, t: 8.0 * k + 8.0 * t,
    lambda k, t: 8.0 + 8.0 * k + 8.0 * t,
    lambda k, t: 6.0 * k + 10.0 * t,
    lambda k, t: 12.0 + 6.0 * k + 10.0 * t,
)


def step(tok, cot, ids, small, shards):
    V, D_, R_ = pltpu.VMEM, pltpu.SemaphoreType.DMA, pltpu.SemaphoreType.REGULAR
    any_, vm = pl.BlockSpec(memory_space=pl.ANY), pl.BlockSpec(memory_space=pltpu.VMEM)
    sd = jax.ShapeDtypeStruct
    wshape = [(n * 32, L) for n, L, _ in MATS]
    narrow, wide = V((ROWS, N_), F32), V((ROWS, W), BF)
    scratch = [V(s, BF) for s in wshape] + [V((W, ROWS), BF), wide, V((ROWS, W), F32)] + [narrow] * 4 + [wide] * 2
    scratch += [V((ROWS, N_), BF)] * 4 + [V((2, 272, N_), F32)] * 2 + [V((2, 288, 128), jnp.int32)]
    scratch += [V((5, ROWS, N_), BF), V((ROWS, W), F32), V((2, 256, N_), BF), V((2, 128, W), BF), V((2, 128, ROWS), F32)]
    scratch += [V((2, 8, W), F32), V((2, 8, N_), F32), V((8, W), F32), V((16, W), F32)]
    scratch += [V((272, N_), BF), V((384, N_), BF), V((144, W), BF)]
    scratch += [V((2, most(75, 2), N_), BF), V((2, 64, W), BF)]
    scratch += [V((4, T16, N_), F32), V((2, T16, W), F32), V((5, T16, W), F32)]
    scratch += [D_((520,)), D_((32, 6)), D_((6,)), D_((6,)), D_((3,)), D_((8,)), D_((8,)), D_((2, 2)), D_((4,)), R_, R_((4, 5))]
    scratch += [D_((4, 4, 4)), D_((4, 2, 4)), D_((4, 4)), D_((2, 4, 6)), D_((6,)), D_((4, 2)), D_((5,)), D_((6,))]
    small_shape = [sd(v.shape, F32) for v in small]
    scratch += [V((8, W), F32)] * 2
    return pl.pallas_call(
        step_kernel,
        out_shape=[sd((2, W, LEN_), BF), sd((2, W, LEN_), F32), *small_shape]
        + [sd(s, BF) for s in wshape] + [sd((-(-n // 8) * 8, L), F32) for n, L, _ in MATS],
        in_specs=[any_] * 3 + [vm] * 12,
        out_specs=[any_] * 2 + [vm] * 6 + [any_] * 12,
        scratch_shapes=scratch,
        compiler_params=pltpu.CompilerParams(collective_id=0, has_side_effects=True, vmem_limit_bytes=int(63.9 * 2**20)),
    )(tok, cot, ids, *small, *shards)


def per_device(
    tokens, doc_ids, cotangent, enc_in, enc_conv, enc_out, enc_gain, enc_shift, enc_bias,
    dec_in, dec_conv, dec_out, dec_gain, dec_shift, dec_bias,
):
    flat = [enc_in, enc_conv, enc_out, dec_in, dec_conv, dec_out]
    size = lax.axis_size("dp"), lax.axis_size("seq"), tokens.shape
    if size != (8, 4, (2, 1, LEN_, W)):
        return any_mesh(
            tokens, doc_ids, cotangent, flat, (enc_gain, enc_shift, enc_bias), (dec_gain, dec_shift, dec_bias)
        )
    ids = jnp.broadcast_to(doc_ids.reshape(2, LEN_, 1), (2, LEN_, 128))
    small = [enc_gain, enc_shift, enc_bias, dec_gain, dec_shift, dec_bias]
    res = step(
        jnp.swapaxes(tokens.reshape(2, LEN_, W), 1, 2), jnp.swapaxes(cotangent.reshape(2, LEN_, W), 1, 2), ids, small, flat
    )
    s, w = res[2:8], [g[:n].reshape(-1) for g, (n, _, _) in zip(res[14:], MATS)]
    output, token_grad = (jnp.swapaxes(v, 1, 2).reshape(tokens.shape) for v in res[0:2])
    return (output, token_grad, w[0], w[1], w[2], *s[0:3], w[3], w[4], w[5], *s[3:6])


def any_mesh(tokens, doc_ids, cotangent, flat, enc_small, dec_small):
    micro_count, seqs_here, length, wide_dim = tokens.shape
    count = micro_count * seqs_here
    lead = max(ENCODER_SPACING * ((ENCODER_TAPS - 1) // 2), DECODER_SPACING * (DECODER_TAPS - 1))
    seg_pad = extended(doc_ids.reshape(count, length), (("seq", 1),), lead)
    whole = [lax.all_gather(w, ("dp", "seq"), axis=0, tiled=True) for w in flat]
    enc, dec = [
        (whole[i].reshape(D2, D), whole[i + 1].reshape(-1, D), whole[i + 2].reshape(D, D2)) for i in (0, 3)
    ]
    rows = tokens.astype(jnp.float32).reshape(count, length, wide_dim)
    middle, enc_kept = block_forward(rows, seg_pad, lead, enc, *enc_small, False)
    final_rows, dec_kept = block_forward(middle, seg_pad, lead, dec, *dec_small, True)
    output = final_rows.astype(jnp.bfloat16).reshape(tokens.shape)
    grad_final = cotangent.astype(jnp.float32).reshape(-1, wide_dim)
    grad_middle, dec_w, dec_s = block_backward(
        grad_final, dec_kept, seg_pad, lead, dec, dec_small[0], True, count, length
    )
    grad_start, enc_w, enc_s = block_backward(
        grad_middle, enc_kept, seg_pad, lead, enc, enc_small[0], False, count, length
    )
    w = [lax.psum_scatter(g.reshape(-1), ("dp", "seq"), scatter_dimension=0, tiled=True) for g in enc_w + dec_w]
    s = lax.psum(enc_s + dec_s, ("dp", "seq"))
    return (
        output, grad_start.reshape(tokens.shape), w[0], w[1], w[2], s[0], s[1], s[2],
        w[3], w[4], w[5], s[3], s[4], s[5],
    )


def solution(mesh):
    placed = (
        P(None, "dp", "seq", None),
        P(None, "dp", "seq"),
        P(None, "dp", "seq", None),
        P(("dp", "seq")),
        P(("dp", "seq")),
        P(("dp", "seq")),
        P(),
        P(),
        P(),
        P(("dp", "seq")),
        P(("dp", "seq")),
        P(("dp", "seq")),
        P(),
        P(),
        P(),
    )
    return jax.shard_map(
        per_device,
        mesh=mesh,
        in_specs=placed,
        out_specs=(
            P(None, "dp", "seq", None),
            P(None, "dp", "seq", None),
            P(("dp", "seq")),
            P(("dp", "seq")),
            P(("dp", "seq")),
            P(),
            P(),
            P(),
            P(("dp", "seq")),
            P(("dp", "seq")),
            P(("dp", "seq")),
            P(),
            P(),
            P(),
        ),
        check_vma=False,
    )
```

```python
import functools

import jax
import jax.numpy as jnp
from jax import lax
from jax.experimental import pallas as pl
from jax.experimental.pallas import tpu as pltpu
from jax.sharding import PartitionSpec as P

MESH = pl.DeviceIdType.MESH
D2 = 1600
D = 800
ENCODER_TAPS = 5
ENCODER_SPACING = 4
DECODER_TAPS = 3
DECODER_SPACING = 8


epsilon = 1e-05


def from_behind(value, axis, by):
    length = lax.axis_size(axis)
    pairs = [(i, i + by) for i in range(length) if 0 <= i + by < length]
    return lax.ppermute(value, axis, pairs)


def extended(value, sides, width):
    for axis, dim in sides:
        size, length = (lax.axis_size(axis), value.shape[dim])
        up = [(i, (i + 1) % size) for i in range(size - 1)]
        down = [(j, i) for i, j in up]
        last = lax.slice_in_dim(value, length - width, length, axis=dim)
        initial = lax.slice_in_dim(value, 0, width, axis=dim)
        before = lax.ppermute(last, axis, up)
        after = lax.ppermute(initial, axis, down)
        value = jnp.concatenate([before, value, after], axis=dim)
    return value


def normalize(values):
    centred = values - jnp.mean(values, axis=-1, keepdims=True)
    factor = lax.rsqrt(jnp.mean(centred * centred, axis=-1, keepdims=True) + epsilon)
    return (centred * factor, factor)


def silu_slope(hidden):
    sigma = jax.nn.sigmoid(hidden)
    return sigma * (1.0 + hidden * (1.0 - sigma))


def norm_back(grad_h, scale_row, normed, factor):
    scaled = grad_h * scale_row
    mean_one = jnp.mean(scaled, axis=-1, keepdims=True)
    mean_two = jnp.mean(scaled * normed, axis=-1, keepdims=True)
    grad_in = factor * (scaled - mean_one - normed * mean_two)
    return (grad_in, jnp.sum(grad_h * normed, axis=0), jnp.sum(grad_h, axis=0))


def tap_offsets(causal):
    if causal:
        return [
            DECODER_SPACING * (tap_position - DECODER_TAPS + 1)
            for tap_position in range(DECODER_TAPS)
        ]
    return [
        ENCODER_SPACING * (tap_position - (ENCODER_TAPS - 1) // 2)
        for tap_position in range(ENCODER_TAPS)
    ]


def stacked_taps(padded, lead_rows, seg_pad, segment_leading, shift_offsets, length):
    own_ids = seg_pad[:, segment_leading : segment_leading + length]
    pieces = []
    for offset in shift_offsets:
        shifted = padded[:, lead_rows + offset : lead_rows + offset + length]
        same_doc = (
            seg_pad[:, segment_leading + offset : segment_leading + offset + length] == own_ids
        )
        pieces.append(jnp.where(same_doc[:, :, None], shifted, jnp.zeros_like(shifted)))
    return jnp.concatenate(pieces, axis=-1)


def block_forward(
    inputs, seg_pad, segment_leading, weights, norm_gain, norm_shift, output_bias, causal
):
    input_weight, convolution_weight, output_weight = weights
    seqs_here, length, wide_dim = inputs.shape
    narrow = input_weight.shape[1]
    flat_rows = inputs.reshape(-1, wide_dim)
    normed_one, factor_one = normalize(flat_rows)
    hidden_one = normed_one * norm_gain[:wide_dim] + norm_shift[:wide_dim]
    act_first = jax.nn.silu(hidden_one).astype(jnp.bfloat16)
    narrowed_rows = jnp.dot(act_first, input_weight, preferred_element_type=jnp.float32)
    normed_two, factor_two = normalize(narrowed_rows)
    hidden_two = (
        normed_two * norm_gain[wide_dim : wide_dim + narrow]
        + norm_shift[wide_dim : wide_dim + narrow]
    )
    act_second = jax.nn.silu(hidden_two).astype(jnp.bfloat16).reshape(seqs_here, length, narrow)
    shift_offsets = tap_offsets(causal)
    reach_rows = max([abs(offset) for offset in shift_offsets])
    if causal:
        tail_rows = from_behind(act_second[:, length - reach_rows :], "seq", 1)
        padded = jnp.concatenate([tail_rows, act_second], axis=1)
    else:
        padded = extended(act_second, (("seq", 1),), reach_rows)
    stacked = stacked_taps(
        padded, reach_rows, seg_pad, segment_leading, shift_offsets, length
    ).reshape(flat_rows.shape[0], -1)
    convolved_output = jnp.dot(stacked, convolution_weight, preferred_element_type=jnp.float32)
    normed_three, factor_three = normalize(convolved_output)
    hidden_three = normed_three * norm_gain[wide_dim + narrow :] + norm_shift[wide_dim + narrow :]
    act_third = jax.nn.silu(hidden_three).astype(jnp.bfloat16)
    residual_branch = (
        jnp.dot(act_third, output_weight, preferred_element_type=jnp.float32) + output_bias
    )
    result = (flat_rows + residual_branch).reshape(inputs.shape)
    kept_state = (
        normed_one,
        factor_one,
        hidden_one,
        act_first,
        normed_two,
        factor_two,
        hidden_two,
        stacked,
        normed_three,
        factor_three,
        hidden_three,
        act_third,
    )
    return (result, kept_state)


def block_backward(
    grad_out, kept_state, seg_pad, segment_leading, weights, norm_gain, causal, seqs_here, length
):
    input_weight, convolution_weight, output_weight = weights
    (
        normed_one,
        factor_one,
        hidden_one,
        act_first,
        normed_two,
        factor_two,
        hidden_two,
        stacked,
        normed_three,
        factor_three,
        hidden_three,
        act_third,
    ) = kept_state
    wide_dim = input_weight.shape[0]
    narrow = input_weight.shape[1]
    grad_low = grad_out.astype(jnp.bfloat16)
    grad_bias = jnp.sum(grad_low.astype(jnp.float32), axis=0)
    grad_w_out = jnp.einsum("nc,nd->cd", act_third, grad_low, preferred_element_type=jnp.float32)
    grad_act = jnp.einsum("nd,cd->nc", grad_low, output_weight, preferred_element_type=jnp.float32)
    grad_act = grad_act * silu_slope(hidden_three)
    grad_conv_out, gain_three, shift_three = norm_back(
        grad_act, norm_gain[wide_dim + narrow :], normed_three, factor_three
    )
    grad_conv_low = grad_conv_out.astype(jnp.bfloat16)
    grad_w_conv = jnp.einsum(
        "nc,nd->cd", stacked, grad_conv_low, preferred_element_type=jnp.float32
    )
    shift_offsets = tap_offsets(causal)
    reach_rows = max([abs(offset) for offset in shift_offsets])
    grad_grid = grad_conv_low.reshape(seqs_here, length, narrow)
    if causal:
        head_rows = from_behind(grad_grid[:, :reach_rows], "seq", -1)
        padded = jnp.concatenate([grad_grid, head_rows], axis=1)
        lead_rows = 0
    else:
        padded = extended(grad_grid, (("seq", 1),), reach_rows)
        lead_rows = reach_rows
    back_stack = stacked_taps(
        padded, lead_rows, seg_pad, segment_leading, [-offset for offset in shift_offsets], length
    ).reshape(seqs_here * length, -1)
    grad_act = sum(
        lax.dot_general(
            back_stack[:, k * narrow : (k + 1) * narrow],
            convolution_weight[k * narrow : (k + 1) * narrow],
            (((1,), (1,)), ((), ())),
            preferred_element_type=jnp.float32,
        )
        for k in range(len(shift_offsets))
    )
    grad_act = grad_act * silu_slope(hidden_two)
    grad_narrow, gain_two, shift_two = norm_back(
        grad_act, norm_gain[wide_dim : wide_dim + narrow], normed_two, factor_two
    )
    grad_narrow_low = grad_narrow.astype(jnp.bfloat16)
    grad_w_in = jnp.einsum(
        "nc,nd->cd", act_first, grad_narrow_low, preferred_element_type=jnp.float32
    )
    grad_act = jnp.einsum(
        "nd,cd->nc", grad_narrow_low, input_weight, preferred_element_type=jnp.float32
    )
    grad_act = grad_act * silu_slope(hidden_one)
    grad_flat, gain_one, shift_one = norm_back(
        grad_act, norm_gain[:wide_dim], normed_one, factor_one
    )
    grad_input = grad_out + grad_flat
    grad_gain = jnp.concatenate([gain_one, gain_two, gain_three])
    grad_shift = jnp.concatenate([shift_one, shift_two, shift_three])
    return (
        grad_input,
        (grad_w_in, grad_w_conv, grad_w_out),
        (grad_gain, grad_shift, grad_bias),
    )


EPS = 1e-5
F32, BF = jnp.float32, jnp.bfloat16
W, N_ = 1600, 800
ROWS, LEN_ = 512, 256
T16 = 16
MATS = ((50, 800, False), (125, 800, True), (25, 1600, False), (50, 800, False), (75, 800, True), (25, 1600, False))
ENC_OFF = [ENCODER_SPACING * (k - 2) for k in range(ENCODER_TAPS)]
DEC_OFF = [DECODER_SPACING * (k - 2) for k in range(DECODER_TAPS)]
ROW_ROW = (((1,), (1,)), ((), ()))
COL_COL = (((0,), (0,)), ((), ()))


def tile_at(n, s):
    return (n * s + T16 - 1) // T16


def dev(y, x, c, z):
    return ((y * 2 + x) * 2 + c, z)


def shard(y, x, c, z):
    return ((y * 2 + x) * 2 + c) * 4 + z


def when(cond, f):
    if cond is None:
        f()
    else:
        pl.when(cond)(f)


def both(a, b):
    if a is None:
        return b
    return a if b is None else jnp.logical_and(a, b)


def sizes(n, s, units):
    f = (n * units) // T16
    if (n * units) % T16 == 0:
        return [(f, None)]
    cnt = tile_at(n, s + units) - tile_at(n, s)
    return [(f, cnt == f), (f + 1, cnt == f + 1)]


def most(n, units):
    return ((n * units) // T16 + 1) * T16


def from_tile(t, tiles):
    return pl.ds(pl.multiple_of(t * T16, T16), tiles * T16)


def lane_tiles(n):
    return [(i, min(128, n - i)) for i in range(0, n, 128)]


def steps(n, step):
    return [(i, min(step, n - i)) for i in range(0, n, step)]


def norm_of(v):
    c = v - jnp.mean(v, axis=-1, keepdims=True)
    r = lax.rsqrt(jnp.mean(c * c, axis=-1, keepdims=True) + EPS)
    return c * r, r


def sigmoid(h):
    return 1.0 / (1.0 + jnp.exp(-h))


def slope(h):
    s = sigmoid(h)
    return s * (1.0 + h * (1.0 - s))


def row_loop(step, body):
    def it(i, _):
        body(pl.multiple_of(i * step, step))
        return 0

    lax.fori_loop(0, ROWS // step, it, 0)


def fold8(v):
    return jnp.sum(v.reshape(v.shape[0] // 8, 8, v.shape[1]), axis=0)


class Net:
    def __init__(self, send_sem):
        dp, z = lax.axis_index("dp"), lax.axis_index("seq")
        y, x, c = dp // 4, (dp // 2) % 2, dp % 2
        self.dp, self.y, self.x, self.c, self.z = dp, y, x, c, z
        self.X, self.Y, self.C = 1 - x, 1 - y, 1 - c
        self.me = shard(y, x, c, z)
        self.has_up, self.has_down = z < 3, z > 0
        self.tX, self.tY, self.tC = dev(y, 1 - x, c, z), dev(1 - y, x, c, z), dev(y, x, 1 - c, z)
        self.tU, self.tD = (dp, jnp.minimum(z + 1, 3)), (dp, jnp.maximum(z - 1, 0))
        nxt, prv = jnp.minimum(self.me + 1, 31), jnp.maximum(self.me - 1, 0)
        self.tN, self.tP = (nxt // 4, nxt % 4), (prv // 4, prv % 4)
        self.send_sem, self.k, self.sent = send_sem, -1, []

    def greet(self):
        barrier = pltpu.get_barrier_semaphore()
        far_next = jnp.logical_and(self.z == 3, self.dp < 7)
        far_prev = jnp.logical_and(self.z == 0, self.dp > 0)
        peers = [(self.tX, None), (self.tY, None), (self.tC, None)]
        peers += [((self.dp, (self.z + i) % 4), None) for i in (1, 2, 3)]
        peers += [(self.tN, far_next), (self.tP, far_prev)]
        for d, cond in peers:
            when(cond, lambda d=d: pl.semaphore_signal(barrier, inc=1, device_id=d, device_id_type=MESH))
        pl.semaphore_wait(barrier, 6 + jnp.where(far_next, 1, 0) + jnp.where(far_prev, 1, 0))

    def slot(self):
        self.k += 1

    def send(self, src, dst, rsem, target, cond=None):
        d = pltpu.make_async_remote_copy(
            src_ref=src, dst_ref=dst, send_sem=self.send_sem.at[self.k], recv_sem=rsem,
            device_id=target, device_id_type=MESH,
        )
        self.sent.append((d, cond))
        when(cond, d.start)

    def arrived(self, dst, rsem):
        pltpu.make_async_remote_copy(
            src_ref=dst, dst_ref=dst, send_sem=self.send_sem.at[0], recv_sem=rsem,
            device_id=self.tC, device_id_type=MESH,
        ).wait_recv()

    def finish(self):
        for d, cond in self.sent:
            when(cond, d.wait_send)
        self.sent = []


def zorder(z, j):
    if j == 0:
        return [(z, None)]
    return [(jnp.clip(z - j, 0, 3), z - j >= 0), (jnp.clip(z + j, 0, 3), z + j <= 3)]


def gather_events(net, inp, out, own, nxt, head, ext, recv_sem, n_sem, local_sem, time):
    y, x, c, z, X, Y, C, me = net.y, net.x, net.c, net.z, net.X, net.Y, net.C, net.me
    pending = []

    def ask(mats):
        for m in mats:
            n, L, _ = MATS[m]
            for i in range(n):
                ext[m][i, 0:L] = inp[m][i * L : (i + 1) * L].astype(F32)
            head[m][...] = ext[m][0:T16, 0:L].astype(BF)
            net.slot()
            net.send(head[m], nxt[m], n_sem.at[m], net.tP, me > 0)

    def build(m):
        n, L, _ = MATS[m]
        tiles = n // T16 + 1
        pl.when(me < 31)(lambda: net.arrived(nxt[m], n_sem.at[m]))
        ext[m][n : n + T16, 0:L] = nxt[m][...].astype(F32)
        o = tile_at(n, me) * T16 - n * me
        size = -(-max(n + T16, 15 + tiles * T16) // 8) * 8
        v = pltpu.roll(ext[m][0:size, 0:L], lax.rem(size - o, size), axis=0)
        own[m][...] = v[0 : tiles * T16].astype(BF)

    def send(m, s, target, cond=None, mine=False):
        n = MATS[m][0]
        net.slot()
        for tiles, c2 in sizes(n, s, 1):
            r = from_tile(tile_at(n, s), tiles)
            src = own[m].at[pl.ds(0, tiles * T16)] if mine else out[m].at[r]
            net.send(src, out[m].at[r], recv_sem.at[s, m], target, both(cond, c2))

    def wait(m, s, cond=None):
        n = MATS[m][0]
        for tiles, c2 in sizes(n, s, 1):
            when(both(cond, c2), lambda: net.arrived(out[m].at[from_tile(tile_at(n, s), tiles)], recv_sem.at[s, m]))

    def first(m):
        return net.tX if MATS[m][2] else net.tY

    def second(m):
        return net.tY if MATS[m][2] else net.tX

    def st_own(m):
        build(m)
        send(m, me, first(m), None, True)
        send(m, me, net.tU, net.has_up, True)
        send(m, me, net.tD, net.has_down, True)
        send(m, me, second(m), None, True)
        send(m, me, net.tC, None, True)
        for tiles, c2 in sizes(MATS[m][0], me, 1):
            l = pltpu.make_async_copy(
                own[m].at[pl.ds(0, tiles * T16)], out[m].at[from_tile(tile_at(MATS[m][0], me), tiles)], local_sem.at[m]
            )
            pending.append((m, l, c2))
            when(c2, l.start)

    def st_z(m, d):
        for o, has, t, has_t in (
            (z - d, z - d >= 0, net.tU, net.has_up), (z + d, z + d <= 3, net.tD, net.has_down)
        ):
            s = shard(y, x, c, jnp.clip(o, 0, 3))
            wait(m, s, has)
            send(m, s, first(m), has)
            if d < 3:
                send(m, s, t, jnp.logical_and(has, has_t))
            send(m, s, second(m), has)
            send(m, s, net.tC, has)

    def st_f(m, j):
        yy, xx = (y, X) if MATS[m][2] else (Y, x)
        for o, cond in zorder(z, j):
            s = shard(yy, xx, c, o)
            wait(m, s, cond)
            send(m, s, second(m), cond)
            send(m, s, net.tC, cond)

    def st_s(m, j):
        yy, xx = (Y, x) if MATS[m][2] else (y, X)
        for o, cond in zorder(z, j):
            s = shard(yy, xx, c, o)
            wait(m, s, cond)
            send(m, s, net.tC, cond)

    def st_d(m, j):
        for o, cond in zorder(z, j):
            s = shard(Y, X, c, o)
            wait(m, s, cond)
            send(m, s, net.tC, cond)

    def rest(m):
        for q in range(16):
            wait(m, shard(q // 8, (q // 4) % 2, C, q % 4))
        for k, l, c2 in pending:
            if k == m:
                when(c2, l.wait)

    ev = [(-1.0, 0, lambda: ask((0, 1, 2))), (5.0, 3, lambda: ask((3, 4, 5)))]
    for m in range(len(MATS)):

        def add(t, f, *a):
            ev.append((time(m, t), m, functools.partial(f, m, *a)))

        add(0, st_own)
        for d in (1, 2, 3):
            add(d, st_z, d)
        for j in range(4):
            add(1.1 + j, st_f, j)
            add(1.2 + j, st_s, j)
            add(2.3 + j, st_d, j)
    return sorted(ev, key=lambda e: (e[0], e[1])), rest


def sum_events(net, mats, grads, b, time):
    y, x, c, z, X, Y, C, me = net.y, net.x, net.c, net.z, net.X, net.Y, net.C, net.me
    pieces = [(m, h) for m in mats for h in (0, 1)]

    def groups(p):
        return [(Y, X), (y, X), (Y, x), (y, x)] if p[1] == 0 else [(Y, X), (Y, x), (y, X), (y, x)]

    def span(p, yy, xx, cc):
        m, h = p
        n = MATS[m][0]
        s0 = ((yy * 2 + xx) * 2 + cc) * 4
        s = s0 + 2 * h
        return s, tile_at(n, s), tile_at(n, s) - tile_at(n, s0)

    def add(srcs, put, tiles):
        def body(i, _):
            t = None
            for ref, t0 in srcs:
                v = ref[from_tile(t0 + i, 1), :].astype(F32)
                t = v if t is None else t + v
            put(i, t)
            return 0

        lax.fori_loop(0, tiles, body, 0)

    units = []
    started = {}

    def load(j):
        if j >= len(units) or j in started:
            return
        p, i = units[j]
        m = p[0]
        n = MATS[m][0]
        s, t0, _ = span(p, *groups(p)[i], c)
        st = b.stage(m)
        started[j] = []
        for tiles, c2 in sizes(n, s, 2):
            l = pltpu.make_async_copy(
                grads[m].at[from_tile(t0, tiles)], st.at[j % 2, pl.ds(0, tiles * T16)], b.local_sem.at[j % 2]
            )
            started[j].append((l, c2))
            when(c2, l.start)

    def st_start(p):
        m = p[0]
        k = pieces.index(p)
        for i, (yy, xx) in enumerate(groups(p)):
            s, t0, o = span(p, yy, xx, C)
            b.once(0)
            net.slot()
            for tiles, c2 in sizes(MATS[m][0], s, 2):
                net.send(
                    grads[m].at[from_tile(t0, tiles)], b.rbc[m](yy * 2 + xx).at[from_tile(o, tiles)],
                    b.c_sem.at[i, k], net.tC, c2,
                )

    def unit(p, i):
        m, h = p
        k = pieces.index(p)
        n = MATS[m][0]
        yy, xx = groups(p)[i]
        q = yy * 2 + xx
        s, _, o = span(p, yy, xx, c)
        j = units.index((p, i))
        load(j)
        cnt = tile_at(n, s + 2) - tile_at(n, s)
        buf = b.rbc[m](q)
        srcs = [(b.stage(m).at[j % 2], 0), (buf, o)]
        o0 = h * (most(n, 2) // T16)
        for tiles, c2 in sizes(n, s, 2):

            def ready():
                r = from_tile(o, tiles)
                net.arrived(buf.at[r], b.c_sem.at[i, k])
                if i == 2:
                    net.arrived(b.rb1[m][0].at[from_tile(o0, tiles)], b.s1_sem.at[0, k])
                if i == 3:
                    net.arrived(b.rb1[m][1].at[r], b.s1_sem.at[1, k])
                    net.arrived(b.rb2[m].at[r], b.s2_sem.at[k])

            when(c2, ready)
        for l, c2 in started[j]:
            when(c2, l.wait)
        load(j + 1)
        if i == 2:
            srcs += [(b.rb1[m][0], o0)]
        if i == 3:
            srcs += [(b.rb1[m][1], o), (b.rb2[m], o)]

        def put(i_, t):
            buf[from_tile(o + i_, 1), :] = t.astype(BF)

        add(srcs, put, cnt)
        if i < 3:
            dst = b.rb1[m][i] if i < 2 else b.rb2[m]
            sem = b.s1_sem.at[i, k] if i < 2 else b.s2_sem.at[k]
            target = net.tX if (i < 2) == (h == 0) else net.tY
            b.once(1 if target is net.tX else 2)
            net.slot()
            for tiles, c2 in sizes(n, s, 2):
                net.send(buf.at[from_tile(o, tiles)], dst.at[from_tile(o0 if i == 0 else o, tiles)], sem, target, c2)

    def block(m, zz):
        n = MATS[m][0]
        s0 = ((y * 2 + x) * 2 + c) * 4
        return s0 + zz, tile_at(n, s0 + zz) - tile_at(n, s0), tile_at(n, s0 + zz + 1) - tile_at(n, s0 + zz)

    def z_place(m, zz, d, to, o):
        return (b.last[m], 0) if d == 1 and zz == to else (b.rbz[m], o)

    def from_z(m, s, zz, d, to, o):
        ref, t0 = z_place(m, zz, d, to, o)
        for tiles, c2 in sizes(MATS[m][0], s, 1):
            when(c2, lambda: net.arrived(ref.at[from_tile(t0, tiles)], b.z_sem.at[d, zz, m]))
        return ref, t0

    def hop(p, zz, d, at, comes):
        m = p[0]
        s, o, cnt = block(m, zz)
        buf = b.rbc[m](y * 2 + x)
        cond = z == at
        if comes:

            @pl.when(cond)
            def _():
                got = from_z(m, s, zz, d, at, o)

                def put(i, t):
                    buf[from_tile(o + i, 1), :] = t.astype(BF)

                add([(buf, o), got], put, cnt)

        b.before_z(d)
        net.slot()
        for tiles, c2 in sizes(MATS[m][0], s, 1):
            ref, t0 = z_place(m, zz, d, (at + 1, at - 1)[d], o)
            net.send(
                buf.at[from_tile(o, tiles)], ref.at[from_tile(t0, tiles)], b.z_sem.at[d, zz, m],
                (net.tU, net.tD)[d], both(cond, c2),
            )

    def st_hop(p, h):
        for zz in (2 * p[1], 2 * p[1] + 1):
            if zz > h:
                hop(p, zz, 0, h, h > 0)
            if zz < 3 - h:
                hop(p, zz, 1, 3 - h, h > 0)

    def st_last(p):
        m, h = p
        n = MATS[m][0]

        for zz in (2 * h, 2 * h + 1):
            s, o, cnt = block(m, zz)

            @pl.when(z == zz)
            def _():
                srcs = [(b.rbc[m](y * 2 + x), o)]
                for d in (0, 1):
                    if (zz > 0, zz < 3)[d]:
                        srcs.append(from_z(m, s, zz, d, zz, o))

                def put(i, t):
                    b.res[m][from_tile(i + 1, 1), :] = t

                add(srcs, put, cnt)
        if h == 1:
            cnt = tile_at(n, me + 1) - tile_at(n, me)
            net.slot()
            net.send(b.res[m].at[from_tile(cnt, 1)], b.tail[m], b.t_sem.at[m], net.tN, me < 31)

    ev = []
    for k, p in enumerate(pieces):

        def a(t, f, *ar):
            ev.append((time(k, t), k, f, (p,) + ar))

        a(0, st_start)
        a(1, unit, 0)
        a(1.3, unit, 1)
        a(2, unit, 2)
        a(3, unit, 3)
        for h in (0, 1, 2):
            a(3.1 + h, st_hop, h)
        a(6, st_last)
    ev.sort(key=lambda e: (e[0], e[1]))
    units.extend((e[3][0], e[3][1]) for e in ev if e[2] is unit)
    return [(e[0], e[1], functools.partial(e[2], *e[3])) for e in ev]


def finish_sum(net, m, b, out_h, sem):
    n, L, _ = MATS[m]
    o = tile_at(n, net.me) * T16 - n * net.me
    res = b.res[m]
    pl.when(net.me > 0)(lambda: net.arrived(b.tail[m], b.t_sem.at[m]))
    res[0:T16, :] = b.tail[m][...]
    size = T16 + most(n, 1)
    v = pltpu.roll(res[0:size, :], lax.rem(size - (T16 - o), size), axis=0)
    keep = -(-n // 8) * 8
    res[0:keep, :] = v[0:keep]
    l = pltpu.make_async_copy(res.at[pl.ds(0, keep)], out_h, sem)
    l.start()
    return l


class Buffers:
    pass


class Schedule:
    def __init__(self):
        self.now, self.events = 0.0, []

    def add(self, events):
        self.events += [(self.now + e[0],) + tuple(e[1:]) for e in events]
        self.events.sort(key=lambda e: (e[0], e[1]))
        self.pop(self.now)

    def pop(self, until):
        while self.events and self.events[0][0] <= until:
            self.events.pop(0)[2]()

    def run(self, gen):
        for step in gen:
            if not isinstance(step, tuple):
                self.now += step
                self.pop(self.now)
            elif step[0] == "call":
                step[1]()
            else:
                m = step[1]
                while any(e[1] == m for e in self.events):
                    e = self.events.pop(0)
                    self.now = max(self.now, e[0])
                    e[2]()
                step[2](m)


class Slots:
    def __init__(self, ref, base, rows):
        self.ref, self.base, self.rows, self.at = ref, base, rows, self

    def __getitem__(self, i):
        slot, rows = i if isinstance(i, tuple) else (i, None)
        first = self.base + slot * self.rows
        return self.ref.at[pl.ds(first, self.rows) if rows is None else pl.ds(first + rows.start, rows.size)]


def step_kernel(*refs):
    r = refs
    (tok_h, cot_h, ids_ref), small_in, inp = r[0:3], r[3:9], r[9:15]
    out_h, tg_h, small_outs = r[15], r[16], r[17:23]
    grad_h, fin_out = r[23:29], r[29:35]
    (wie, wce, woe, wid, wcd, wod, tbuf, gyd, mid, ue, ve, ud, vd, a1e, a1d, a2e, a2d, a3e, a3d, ape, apd, idp, lk, big,
     st8, st16, tgb, acc1, acc2, accb, small_ref, zdi, zdc, zdo, sgd, sgo, tl8, tl16, sm_r,
     send_sem, recv_sem, n_sem, l_sem, in_sem, h_sem, h_recv, g_sem, o_sem, hs_sem, rdy,
     c_sem, s1_sem, s2_sem, z_sem, t_sem, r_sem, sm_sem, f_sem, ge_ref, gd_ref) = r[35:]
    net = Net(send_sem)
    z, y, x = net.z, net.y, net.x
    weights = (wie, wce, woe, wid, wcd, wod)
    load_c = [pltpu.make_async_copy(cot_h.at[i], tbuf.at[:, pl.ds(i * LEN_, LEN_)], in_sem.at[i]) for i in (0, 1)]
    load_t = [pltpu.make_async_copy(tok_h.at[i], tbuf.at[:, pl.ds(i * LEN_, LEN_)], in_sem.at[i]) for i in (0, 1)]
    for par, (gain, shift, bias) in ((ge_ref, small_in[0:3]), (gd_ref, small_in[3:6])):
        par[0, :], par[1, :], par[2, :] = gain[0:W], shift[0:W], bias[...]
        for row, ref in ((3, gain), (4, shift)):
            par[row, 0:N_] = ref[W : W + N_]
            par[row + 2, 0:N_] = ref[W + N_ : W + 2 * N_]
    load_i = pltpu.make_async_copy(ids_ref, idp.at[:, pl.ds(16, LEN_)], in_sem.at[2])
    load_i.start()
    for l in load_c:
        l.start()
    net.greet()

    own = [st8.at[0, pl.ds(0, 64)], st8.at[0, pl.ds(64, 128)], st16.at[0, pl.ds(0, 32)],
           st8.at[0, pl.ds(192, 64)], st8.at[1, pl.ds(0, 80)], st16.at[0, pl.ds(32, 32)]]
    nxt = [st8.at[1, pl.ds(80, 16)], st8.at[1, pl.ds(96, 16)], st16.at[1, pl.ds(0, 16)],
           st8.at[1, pl.ds(112, 16)], st8.at[1, pl.ds(128, 16)], st16.at[1, pl.ds(16, 16)]]
    head = [st8.at[1, pl.ds(144, 16)], st8.at[1, pl.ds(160, 16)], st16.at[1, pl.ds(32, 16)],
            st8.at[1, pl.ds(176, 16)], st8.at[1, pl.ds(192, 16)], st16.at[1, pl.ds(48, 16)]]
    ext = [big.at[pl.ds(a, n)] for a, n in ((0, 80), (80, 144), (400, 48), (224, 80), (304, 96), (448, 48))]
    g_events, g_rest = gather_events(
        net, inp, weights, own, nxt, head, ext, recv_sem, n_sem, l_sem, lambda m, t: GATHER_TIME(m, t)
    )

    def halo(k, buf, lead, reach, up, fill):
        if up:
            src, dst = buf.at[:, pl.ds(lead + LEN_ - reach, reach)], buf.at[:, pl.ds(lead - reach, reach)]
            target, can, arrives = net.tU, net.has_up, net.has_down
        else:
            src, dst = buf.at[:, pl.ds(lead, reach)], buf.at[:, pl.ds(lead + LEN_, reach)]
            target, can, arrives = net.tD, net.has_down, net.has_up
        d = pltpu.make_async_remote_copy(
            src_ref=src, dst_ref=dst, send_sem=h_sem.at[k], recv_sem=h_recv.at[k], device_id=target, device_id_type=MESH
        )
        pl.when(can)(d.start)

        @pl.when(jnp.logical_not(arrives))
        def _():
            dst[...] = jnp.full(dst.shape, fill, buf.dtype)

        return d, can, arrives

    def halo_wait(hs):
        for d, can, arrives in hs:
            pl.when(arrives)(d.wait_recv)
            pl.when(can)(d.wait_send)

    def first_norm(x_of, par, a):
        def body(r):
            n, _ = norm_of(x_of(r, 128))
            h = n * par[0:1, :] + par[1:2, :]
            a[pl.ds(r, 128), :] = (h * sigmoid(h)).astype(BF)

        row_loop(128, body)

    def mid_norm(u, par, row, put):
        def body(r):
            n, _ = norm_of(u[pl.ds(r, 128), :])
            h = n * par[row : row + 1, 0:N_] + par[row + 1 : row + 2, 0:N_]
            put(r, 128, (h * sigmoid(h)).astype(BF))

        row_loop(128, body)

    def into(buf, lead):
        def put(r, n, v):
            m = r // LEN_
            buf[m, pl.ds(pl.multiple_of(r - m * LEN_ + lead, 8), n), :] = v.astype(buf.dtype)

        return put

    def stack(buf, lead, offsets):
        def it(m, _):
            rows = pl.ds(pl.multiple_of(m * LEN_, LEN_), LEN_)
            mine = idp[m, 16 : 16 + LEN_, :]
            for k, o in enumerate(offsets):
                same = idp[m, 16 + o : 16 + o + LEN_, :] == mine
                for c0, cn in lane_tiles(N_):
                    v = buf[m, lead + o : lead + o + LEN_, c0 : c0 + cn]
                    lk[k, rows, c0 : c0 + cn] = jnp.where(same[:, :cn], v, 0.0).astype(BF)
            return 0

        lax.fori_loop(0, 2, it, 0)

    def tok_rows(r, n):
        return jnp.concatenate(
            [jnp.transpose(tbuf[c0 : c0 + cn, pl.ds(r, n)].astype(F32)) for c0, cn in lane_tiles(W)], axis=1
        )

    def mid_rows(r, n):
        return mid[pl.ds(r, n), :]

    def forward(x_of, par, a1, a2, a3, w, u, v, ap, lead, offsets, hal, base, put_out):
        wi, wc, wo = w
        first_norm(x_of, par, a1)
        yield 3.0
        yield ("need", base, g_rest)
        for c0, cn in steps(N_, 256):
            u[:, c0 : c0 + cn] = jnp.dot(a1[...], wi[:, c0 : c0 + cn], preferred_element_type=F32)
            yield 0.7

        def put2(r, n, val):
            a2[pl.ds(r, n), :] = val
            into(ap, lead)(r, n, val)

        mid_norm(u, par, 3, put2)
        hs = hal()
        yield 2.0
        halo_wait(hs)
        stack(ap, lead, offsets)
        yield 1.5
        yield ("need", base + 1, g_rest)
        for c0, cn in steps(N_, 256):
            t = None
            for k in range(len(offsets)):
                d = jnp.dot(lk[k], wc[k * N_ : (k + 1) * N_, c0 : c0 + cn], preferred_element_type=F32)
                t = d if t is None else t + d
            v[:, c0 : c0 + cn] = t
            yield 1.5

        def put3(r, n, val):
            a3[pl.ds(r, n), :] = val

        mid_norm(v, par, 5, put3)
        yield 1.5
        yield ("need", base + 2, g_rest)
        for c0, cn in steps(W, 256):
            put_out(jnp.dot(a3[...], wo[:, c0 : c0 + cn], preferred_element_type=F32) + par[2:3, c0 : c0 + cn], c0, cn)
            yield 0.5

    used = [[], []]

    def wgrad(a, rhs, dst, row0):
        which = 1 if rhs.shape[-1] == W else 0
        st = (st8, st16)[which]
        for c0, cn in steps(a.shape[1], st.shape[1]):
            log = used[which]
            slot = len(log) % 2
            if len(log) >= 2:
                log[-2].wait()
            c = pltpu.make_async_copy(
                st.at[slot, pl.ds(0, cn)], dst.at[pl.ds(row0 + c0, cn)], g_sem.at[which, slot]
            )
            st[slot, 0:cn, :] = lax.dot_general(
                a[:, c0 : c0 + cn], rhs, COL_COL, preferred_element_type=F32
            ).astype(BF)
            c.start()
            log.append(c)
            yield 0.4 if which == 0 else 0.3

    def drain():
        for log in used:
            for c in log[-2:]:
                c.wait()
            log.clear()

    def back_norm(src, par, row, accum, width, emit, step):
        accum[...] = jnp.zeros_like(accum)

        def body(r):
            n, f = norm_of(src(r, step))
            g = par[row : row + 1, 0:width]
            h = n * g + par[row + 1 : row + 2, 0:width]
            gh = big[pl.ds(r, step), 0:width] * slope(h)
            accum[0] += fold8(gh * n)
            accum[1] += fold8(gh)
            p = gh * g
            m1 = jnp.mean(p, axis=-1, keepdims=True)
            m2 = jnp.mean(p * n, axis=-1, keepdims=True)
            emit(r, step, f * (p - m1 - n * m2))

        row_loop(step, body)

    def small(row, acc, width):
        small_ref[row : row + 1, 0:width] = jnp.sum(acc[0], axis=0, keepdims=True)
        small_ref[row + 1 : row + 2, 0:width] = jnp.sum(acc[1], axis=0, keepdims=True)

    def backward(gy, par, sb, x_of, a1, a2, a3, w, u, v, gp, lead, offsets, hal, g, emit, after_taps, after_in):
        wi, wc, wo = w
        gi, gc, go = g
        accb[...] = jnp.zeros_like(accb)

        def bsum(r):
            accb[...] += fold8(gy[pl.ds(r, 64), :].astype(F32))

        row_loop(64, bsum)
        small_ref[sb + 2 : sb + 3, :] = jnp.sum(accb[...], axis=0, keepdims=True)
        yield 0.5
        for c0, cn in steps(N_, 256):
            big[:, c0 : c0 + cn] = lax.dot_general(gy[...], wo[c0 : c0 + cn, :], ROW_ROW, preferred_element_type=F32)
            yield 0.7
        yield from wgrad(a3, gy[...], go, 0)
        put = into(gp, lead)
        back_norm(
            lambda r, n: v[pl.ds(r, n), :], par, 5, acc2, N_, lambda r, n, val: put(r, n, val.astype(BF)), 128
        )
        hs = hal()
        small(sb + 5, acc2, N_)
        yield 2.5
        halo_wait(hs)
        stack(gp, lead, [-o for o in offsets])
        yield 1.5
        for k in range(len(offsets)):
            yield from wgrad(a2, lk[k], gc, k * N_)
        for c0, cn in steps(N_, 256):
            t = None
            for k in range(len(offsets)):
                d = lax.dot_general(
                    lk[k], wc[k * N_ + c0 : k * N_ + c0 + cn, :], ROW_ROW, preferred_element_type=F32
                )
                t = d if t is None else t + d
            big[:, c0 : c0 + cn] = t
            yield 1.5
        yield ("call", after_taps)
        gub = a3

        def put2(r, n, val):
            gub[pl.ds(r, n), :] = val.astype(BF)

        back_norm(lambda r, n: u[pl.ds(r, n), :], par, 3, acc2, N_, put2, 128)
        small(sb + 3, acc2, N_)
        yield 2.5
        yield from wgrad(a1, gub[...], gi, 0)
        for c0, cn in steps(W, 256):
            big[:, c0 : c0 + cn] = lax.dot_general(
                gub[...], wi[c0 : c0 + cn, :], ROW_ROW, preferred_element_type=F32
            )
            yield 0.5
        yield ("call", after_in)
        back_norm(x_of, par, 0, acc1, W, emit, 64)
        small(sb, acc1, W)
        yield 4.5

    def turn(r):
        for c0, cn in lane_tiles(W):
            gyd[pl.ds(r, 128), c0 : c0 + cn] = jnp.transpose(tbuf[c0 : c0 + cn, pl.ds(r, 128)].astype(F32)).astype(BF)

    def network():
        for l in load_c:
            l.wait()

        row_loop(128, turn)
        for l in load_t:
            l.start()
        load_i.wait()
        h_ids = [halo(0, idp, 16, 16, True, -1), halo(1, idp, 16, 16, False, -1)]
        for l in load_t:
            l.wait()
        halo_wait(h_ids)

        def out_e(t, c0, cn):
            for d0, dn in lane_tiles(cn):
                own_t = jnp.transpose(tbuf[c0 + d0 : c0 + d0 + dn, :].astype(F32))
                mid[:, c0 + d0 : c0 + d0 + dn] = own_t + t[:, d0 : d0 + dn]

        yield from forward(
            tok_rows, ge_ref, a1e, a2e, a3e, weights[0:3], ue, ve, ape, 8, ENC_OFF,
            lambda: [halo(2, ape, 8, 8, True, 0), halo(3, ape, 8, 8, False, 0)], 0, out_e,
        )
        copies = []

        def out_d(t, c0, cn):
            v = mid[:, c0 : c0 + cn] + t
            for d0, dn in lane_tiles(cn):
                tbuf[c0 + d0 : c0 + d0 + dn, :] = jnp.transpose(v[:, d0 : d0 + dn]).astype(BF)

        yield from forward(
            mid_rows, gd_ref, a1d, a2d, a3d, weights[3:6], ud, vd, apd, 16, DEC_OFF,
            lambda: [halo(4, apd, 16, 16, True, 0)], 3, out_d,
        )

    todo = Schedule()
    todo.add(g_events)
    todo.run(network())
    todo.pop(1e9)
    net.finish()
    out_copies = [
        pltpu.make_async_copy(tbuf.at[:, pl.ds(i * LEN_, LEN_)], out_h.at[i], o_sem.at[i]) for i in (0, 1)
    ]
    for l in out_copies:
        l.start()
    pl.when(net.has_up)(lambda: pl.semaphore_signal(hs_sem, inc=1, device_id=net.tU, device_id_type=MESH))
    small_ref[...] = jnp.zeros_like(small_ref)

    def split(ref, at, rows):
        return ref.at[pl.ds(0, at)], ref.at[pl.ds(at, rows)]

    z_asked = set()
    late, all_b = [], {}

    def phase(i, mats, homes, zbuf, stages, res, tails, time):
        drain()
        for k, t in enumerate((net.tC, net.tX, net.tY)):
            pl.semaphore_signal(rdy.at[i, k], inc=1, device_id=t, device_id_type=MESH)
        if i == 2:
            pl.when(net.has_up)(lambda: pl.semaphore_signal(rdy.at[i, 4], inc=1, device_id=net.tU, device_id_type=MESH))
            pl.when(net.has_down)(lambda: pl.semaphore_signal(rdy.at[i, 3], inc=1, device_id=net.tD, device_id_type=MESH))
        b = Buffers()
        b.rbc, b.rb1, b.rb2, b.rbz, b.last, b.res, b.tail = {}, {}, {}, {}, {}, {}, {}
        for k, m in enumerate(mats):
            rows = most(MATS[m][0], 4)
            home = homes[k]
            b.rbc[m] = lambda q, home=home, rows=rows: home.at[pl.ds(pl.multiple_of(q * rows, T16), rows)]
            b.rb1[m] = [home.at[pl.ds(6 * rows, 2 * most(MATS[m][0], 2))], home.at[pl.ds(4 * rows, rows)]]
            b.rb2[m] = home.at[pl.ds(5 * rows, rows)]
            b.rbz[m], b.last[m] = zbuf[k]
            b.res[m], b.tail[m] = res[k], tails[k]
            all_b[m] = b
        b.stage = lambda m: stages[mats.index(m)]
        b.c_sem, b.s1_sem, b.s2_sem = c_sem.at[i], s1_sem.at[i], s2_sem.at[i]
        b.z_sem, b.t_sem, b.local_sem = z_sem, t_sem, r_sem.at[i]
        asked = set()

        def once(k):
            if k not in asked:
                asked.add(k)
                pl.semaphore_wait(rdy.at[i, k], 1)

        def before_z(d):
            said = (None, None, 2, 2)[i]
            if said is not None and (said, d) not in z_asked:
                z_asked.add((said, d))
                when((net.has_up, net.has_down)[d], lambda: pl.semaphore_wait(rdy.at[said, 3 + d], 1))

        b.once, b.before_z = once, before_z
        ev = []
        for e in sum_events(net, mats, grad_h, b, time):
            f = e[2]
            if f.func.__name__ == "st_last" and MATS[f.args[0][0]][1] == W:
                late.append(f)
            else:
                ev.append(e)
        todo.add(ev)

    def emit_mid(r, n, val):
        t = gyd[pl.ds(r, n), :].astype(F32) + val
        mid[pl.ds(r, n), :] = t
        a1d[pl.ds(r, n), :] = t.astype(BF)

    def emit_tok(r, n, val):
        mid[pl.ds(r, n), :] = mid[pl.ds(r, n), :] + val

    def token_rows(r, n):
        return gyd[pl.ds(r, n), :].astype(F32)

    def hal_e():
        pl.when(net.has_down)(lambda: pl.semaphore_wait(hs_sem, 1))
        return [halo(6, apd, 8, 8, True, 0), halo(7, apd, 8, 8, False, 0)]

    def back():
        yield from backward(
            gyd, gd_ref, 8, mid_rows, a1d, a2d, a3d, weights[3:6], ud, vd, ape, 0, DEC_OFF,
            lambda: [halo(5, ape, 0, 16, False, 0)], grad_h[3:6], emit_mid,
            lambda: phase(
                0, (4, 5), (wcd, wod), (split(zdc, 304, 80), split(zdo, 112, 32)), (sgd, sgo),
                (vd.at[pl.ds(80, 96)], big.at[pl.ds(0, 48)]), (tl8.at[1], tl16.at[0]), SUM_TIME[0],
            ),
            lambda: phase(
                1, (3,), (wid,), (split(zdi, 208, 64),), (Slots(wcd, 2144, 112),),
                (vd.at[pl.ds(0, 80)],), (tl8.at[0],), SUM_TIME[1],
            ),
        )
        for l in out_copies:
            l.wait()
        for l in load_t:
            l.start()
        for l in load_t:
            l.wait()
        row_loop(128, turn)
        yield 2.0
        yield from backward(
            a1d, ge_ref, 0, token_rows, a1e, a2e, a3e, weights[0:3], ue, ve, apd, 8, ENC_OFF, hal_e, grad_h[0:3], emit_tok,
            lambda: phase(
                2, (1, 2), (wce, woe), ((lk.at[1], lk.at[2, pl.ds(0, 128)]), split(a1d, 112, 32)),
                (lk.at[pl.ds(3, 2)], Slots(a1d, 144, 64)),
                (ve.at[pl.ds(80, 144)], big.at[pl.ds(48, 48)]), (tl8.at[3], tl16.at[1]), SUM_TIME[2],
            ),
            lambda: phase(
                3, (0,), (wie,), (split(lk.at[0], 208, 64),), (Slots(wce, 3584, 112),),
                (ve.at[pl.ds(0, 80)],), (tl8.at[2],), SUM_TIME[3],
            ),
        )

    todo.run(back())

    def turn_out():
        log = []
        for c0, cn in lane_tiles(W):
            slot = len(log) % 2
            if len(log) >= 2:
                for l in log[-2]:
                    l.wait()
            tgb[slot, 0:cn, :] = jnp.transpose(mid[:, c0 : c0 + cn])
            ls = [
                pltpu.make_async_copy(
                    tgb.at[slot, pl.ds(0, cn), pl.ds(i * LEN_, LEN_)], tg_h.at[i, pl.ds(c0, cn)], o_sem.at[2 * slot + i]
                )
                for i in (0, 1)
            ]
            for l in ls:
                l.start()
            log.append(ls)
            yield 0.3
        for ls in log[-2:]:
            for l in ls:
                l.wait()

    z_pair = [(net.dp, z + 1 - 2 * (z % 2)), (net.dp, (z + 2) % 4)]

    def small_sums():
        at = small_ref
        for i, target in enumerate([net.tC, net.tX, net.tY] + z_pair):
            net.slot()
            net.send(at, sm_r.at[i], sm_sem.at[i], target)
            yield 3.0
            net.arrived(sm_r.at[i], sm_sem.at[i])
            to = big.at[pl.ds(96 + 16 * i, 16)]
            to[...] = at[...] + sm_r[i]
            at = to
        for first, (gain, shift, bias) in ((0, small_outs[0:3]), (8, small_outs[3:6])):
            for row, ref in ((0, gain), (1, shift)):
                ref[0:W] = at[first + row, :]
                ref[W : W + N_] = at[first + row + 3, 0:N_]
                ref[W + N_ : W + 2 * N_] = at[first + row + 5, 0:N_]
            bias[...] = at[first + 2, :]

    def tail_work():
        s = small_sums()
        next(s)
        for cost in turn_out():
            yield cost
        for cost in s:
            yield cost

    todo.add([(1e8, 0, f) for f in late])
    todo.run(tail_work())
    todo.pop(1e9)
    net.finish()
    fin = []
    for m in (3, 4, 5, 0, 1, 2):
        fin.append(finish_sum(net, m, all_b[m], fin_out[m], f_sem.at[m]))
    for l in fin:
        l.wait()


def GATHER_TIME(m, t):
    return t * 9.0 if m < 3 else 45.0 + t * 9.0


SUM_TIME = (
    lambda k, t: 12.0 * k + 8.0 * t,
    lambda k, t: 8.0 + 12.0 * k + 8.0 * t,
    lambda k, t: 8.0 * k + 6.0 * t,
    lambda k, t: 12.0 + 8.0 * k + 6.0 * t,
)


def step(tok, cot, ids, small, shards):
    V, D_, R_ = pltpu.VMEM, pltpu.SemaphoreType.DMA, pltpu.SemaphoreType.REGULAR
    any_, vm = pl.BlockSpec(memory_space=pl.ANY), pl.BlockSpec(memory_space=pltpu.VMEM)
    sd = jax.ShapeDtypeStruct
    wshape = [(n * 32, L) for n, L, _ in MATS]
    narrow, wide = V((ROWS, N_), F32), V((ROWS, W), BF)
    scratch = [V(s, BF) for s in wshape] + [V((W, ROWS), BF), wide, V((ROWS, W), F32)] + [narrow] * 4 + [wide] * 2
    scratch += [V((ROWS, N_), BF)] * 4 + [V((2, 272, N_), F32)] * 2 + [V((2, 288, 128), jnp.int32)]
    scratch += [V((5, ROWS, N_), BF), V((ROWS, W), F32), V((2, 256, N_), BF), V((2, 128, W), BF), V((2, 128, ROWS), F32)]
    scratch += [V((2, 8, W), F32), V((2, 8, N_), F32), V((8, W), F32), V((16, W), F32)]
    scratch += [V((272, N_), BF), V((384, N_), BF), V((144, W), BF)]
    scratch += [V((2, most(75, 2), N_), BF), V((2, 64, W), BF)]
    scratch += [V((4, T16, N_), F32), V((2, T16, W), F32), V((5, T16, W), F32)]
    scratch += [D_((520,)), D_((32, 6)), D_((6,)), D_((6,)), D_((3,)), D_((8,)), D_((8,)), D_((2, 2)), D_((4,)), R_, R_((4, 5))]
    scratch += [D_((4, 4, 4)), D_((4, 2, 4)), D_((4, 4)), D_((2, 4, 6)), D_((6,)), D_((4, 2)), D_((5,)), D_((6,))]
    small_shape = [sd(v.shape, F32) for v in small]
    scratch += [V((8, W), F32)] * 2
    return pl.pallas_call(
        step_kernel,
        out_shape=[sd((2, W, LEN_), BF), sd((2, W, LEN_), F32), *small_shape]
        + [sd(s, BF) for s in wshape] + [sd((-(-n // 8) * 8, L), F32) for n, L, _ in MATS],
        in_specs=[any_] * 3 + [vm] * 12,
        out_specs=[any_] * 2 + [vm] * 6 + [any_] * 12,
        scratch_shapes=scratch,
        compiler_params=pltpu.CompilerParams(collective_id=0, has_side_effects=True, vmem_limit_bytes=int(63.9 * 2**20)),
    )(tok, cot, ids, *small, *shards)


def per_device(
    tokens, doc_ids, cotangent, enc_in, enc_conv, enc_out, enc_gain, enc_shift, enc_bias,
    dec_in, dec_conv, dec_out, dec_gain, dec_shift, dec_bias,
):
    flat = [enc_in, enc_conv, enc_out, dec_in, dec_conv, dec_out]
    size = lax.axis_size("dp"), lax.axis_size("seq"), tokens.shape
    if size != (8, 4, (2, 1, LEN_, W)):
        return any_mesh(
            tokens, doc_ids, cotangent, flat, (enc_gain, enc_shift, enc_bias), (dec_gain, dec_shift, dec_bias)
        )
    ids = jnp.broadcast_to(doc_ids.reshape(2, LEN_, 1), (2, LEN_, 128))
    small = [enc_gain, enc_shift, enc_bias, dec_gain, dec_shift, dec_bias]
    res = step(
        jnp.swapaxes(tokens.reshape(2, LEN_, W), 1, 2), jnp.swapaxes(cotangent.reshape(2, LEN_, W), 1, 2), ids, small, flat
    )
    s, w = res[2:8], [g[:n].reshape(-1) for g, (n, _, _) in zip(res[14:], MATS)]
    output, token_grad = (jnp.swapaxes(v, 1, 2).reshape(tokens.shape) for v in res[0:2])
    return (output, token_grad, w[0], w[1], w[2], *s[0:3], w[3], w[4], w[5], *s[3:6])


def any_mesh(tokens, doc_ids, cotangent, flat, enc_small, dec_small):
    micro_count, seqs_here, length, wide_dim = tokens.shape
    count = micro_count * seqs_here
    lead = max(ENCODER_SPACING * ((ENCODER_TAPS - 1) // 2), DECODER_SPACING * (DECODER_TAPS - 1))
    seg_pad = extended(doc_ids.reshape(count, length), (("seq", 1),), lead)
    whole = [lax.all_gather(w, ("dp", "seq"), axis=0, tiled=True) for w in flat]
    enc, dec = [
        (whole[i].reshape(D2, D), whole[i + 1].reshape(-1, D), whole[i + 2].reshape(D, D2)) for i in (0, 3)
    ]
    rows = tokens.astype(jnp.float32).reshape(count, length, wide_dim)
    middle, enc_kept = block_forward(rows, seg_pad, lead, enc, *enc_small, False)
    final_rows, dec_kept = block_forward(middle, seg_pad, lead, dec, *dec_small, True)
    output = final_rows.astype(jnp.bfloat16).reshape(tokens.shape)
    grad_final = cotangent.astype(jnp.float32).reshape(-1, wide_dim)
    grad_middle, dec_w, dec_s = block_backward(
        grad_final, dec_kept, seg_pad, lead, dec, dec_small[0], True, count, length
    )
    grad_start, enc_w, enc_s = block_backward(
        grad_middle, enc_kept, seg_pad, lead, enc, enc_small[0], False, count, length
    )
    w = [lax.psum_scatter(g.reshape(-1), ("dp", "seq"), scatter_dimension=0, tiled=True) for g in enc_w + dec_w]
    s = lax.psum(enc_s + dec_s, ("dp", "seq"))
    return (
        output, grad_start.reshape(tokens.shape), w[0], w[1], w[2], s[0], s[1], s[2],
        w[3], w[4], w[5], s[3], s[4], s[5],
    )


def solution(mesh):
    placed = (
        P(None, "dp", "seq", None),
        P(None, "dp", "seq"),
        P(None, "dp", "seq", None),
        P(("dp", "seq")),
        P(("dp", "seq")),
        P(("dp", "seq")),
        P(),
        P(),
        P(),
        P(("dp", "seq")),
        P(("dp", "seq")),
        P(("dp", "seq")),
        P(),
        P(),
        P(),
    )
    return jax.shard_map(
        per_device,
        mesh=mesh,
        in_specs=placed,
        out_specs=(
            P(None, "dp", "seq", None),
            P(None, "dp", "seq", None),
            P(("dp", "seq")),
            P(("dp", "seq")),
            P(("dp", "seq")),
            P(),
            P(),
            P(),
            P(("dp", "seq")),
            P(("dp", "seq")),
            P(("dp", "seq")),
            P(),
            P(),
            P(),
        ),
        check_vma=False,
    )
```
